32 devices in a mesh: ctx: 8 (over z, y), tp: 4 (over x, core).
Axes of the slice: x: 2, y: 2, z: 4, core: 2. Of those that a mesh axis runs over, the one named last changes fastest.
Arguments:
- key_act: bfloat16 [2048, 2048], P('ctx', 'tp'), may hold values from -6 to 6
- value_act: bfloat16 [2048, 2048], P('ctx', 'tp'), may hold values from -6 to 6
- query_act: bfloat16 [2048, 2048], P('ctx', 'tp'), may hold values from -6 to 6
- grad_out: bfloat16 [2048, 2048], P('ctx', 'tp'), may hold values from -6 to 6
- long_filter: bfloat16 [2048, 2048], P('ctx', 'tp'), may hold values from -6 to 6
- w_key: bfloat16 [2048, 2048], P(None, 'tp'), may hold values from -0.125 to 0.125
- w_query: bfloat16 [2048, 2048], P(None, 'tp'), may hold values from -0.125 to 0.125
- w_value: bfloat16 [2048, 2048], P(None, 'tp'), may hold values from -0.125 to 0.125
Outputs:
- grad_input: bfloat16 [2048, 2048], P('ctx', 'tp')
- grad_filter: bfloat16 [2048, 2048], P('ctx', 'tp')
The draws below stay inside these ranges and needn't reach their ends.
All inputs are finite; a program needn't handle non-finite values.
Results may differ from the reference program's by a relative error of at most 0.025.
Values may be sent and summed in bfloat16 or wider, within the bound.
No kernel may reach another device: no remote copies, remote signals or barrier semaphores. Data moves between devices by JAX's collectives and lax.ppermute only.
A program may use at most 128 MiB of HBM per device.

```python
import math
import jax
import jax.numpy as jnp
from jax import lax

D = 2048
SEQ = 2048
N_TP = 4


def shard_levels(own_key, shape, cuts, low, top_value):
    level, own = 1.0, jax.random.fold_in(own_key, 6)
    for position, blocks in cuts:
        draws = jnp.exp(jax.random.uniform(jax.random.fold_in(own, position), (blocks,), jnp.float32, low / len(cuts), top_value / len(cuts)))
        level = level * jnp.repeat(draws, shape[position] // blocks).reshape([-1 if axis == position else 1 for axis in range(len(shape))])
    return level


def gaussian(own_key, dims, scale, bound, split=(), dtype=jnp.bfloat16):
    level = shard_levels(own_key, dims, split, -0.22, 0.18) if split else 1.0
    array = jax.random.normal(own_key, dims, jnp.float32) * scale * level
    return jnp.minimum(jnp.maximum(array, -bound), bound).astype(dtype)


def setup_inputs(seed: int = 0) -> dict:
    keys = jax.random.split(jax.random.key(seed), 9)
    key_act = gaussian(keys[0], (SEQ, D), 1.0, 6.0, ((0, 8), (1, 4)))
    value_act = gaussian(keys[1], (SEQ, D), 1.0, 6.0, ((0, 8), (1, 4)))
    query_act = gaussian(keys[2], (SEQ, D), 1.0, 6.0, ((0, 8), (1, 4)))
    grad_out = gaussian(keys[3], (SEQ, D), 1.0, 6.0, ((0, 8), (1, 4)))
    long_filter = gaussian(keys[4], (SEQ, D), 1.0, 6.0, ((0, 8), (1, 4)))
    w_key = gaussian(keys[5], (D, D), D ** -0.5, 0.125, ((1, 4),))
    w_query = gaussian(keys[6], (D, D), D ** -0.5, 0.125, ((1, 4),))
    w_value = gaussian(keys[7], (D, D), D ** -0.5, 0.125, ((1, 4),))
    return {"key_act": key_act, "value_act": value_act, "query_act": query_act, "grad_out": grad_out, "long_filter": long_filter, "w_key": w_key, "w_query": w_query, "w_value": w_value}


def convolve_block(stacked):
    product = stacked[0]
    kernel_raw = stacked[1]
    gated = stacked[2]
    padded_len = 2 * SEQ
    factor = 1.0 / math.sqrt(SEQ)
    spec_prod = jnp.fft.rfft(product, n=padded_len, axis=0)
    spec_kern = jnp.fft.rfft(kernel_raw, n=padded_len, axis=0) * factor
    spec_grad = jnp.fft.rfft(gated, n=padded_len, axis=0)
    conv_out = jnp.fft.irfft(spec_prod * spec_kern, n=padded_len, axis=0)[:SEQ]
    grad_product = jnp.fft.irfft(spec_grad * jnp.conj(spec_kern), n=padded_len, axis=0)[:SEQ]
    grad_filter = jnp.fft.irfft(spec_grad * jnp.conj(spec_prod), n=padded_len, axis=0)[:SEQ] * factor
    return jnp.stack([conv_out, grad_product, grad_filter]).astype(jnp.float32).astype(jnp.bfloat16)

def reference(key_act, value_act, query_act, grad_out, long_filter, w_key, w_query, w_value):
    product = (key_act.astype(jnp.float32) * value_act.astype(jnp.float32)).astype(jnp.bfloat16)
    gated = (grad_out.astype(jnp.float32) * query_act.astype(jnp.float32)).astype(jnp.bfloat16)
    width = 128 if D % 128 == 0 else D
    count = D // width
    stacked = jnp.stack([product.astype(jnp.float32), long_filter.astype(jnp.float32), gated.astype(jnp.float32)])
    blocked = stacked.reshape(3, SEQ, count, width).transpose(2, 0, 1, 3)
    outputs = lax.map(convolve_block, blocked)
    outputs = outputs.transpose(1, 2, 0, 3).reshape(3, SEQ, D)
    conv_out = outputs[0].astype(jnp.float32)
    grad_product = outputs[1].astype(jnp.float32)
    grad_filter = outputs[2]
    grad_key = (grad_product * value_act.astype(jnp.float32)).astype(jnp.bfloat16)
    grad_query = (conv_out * grad_out.astype(jnp.float32)).astype(jnp.bfloat16)
    grad_value = (grad_product * key_act.astype(jnp.float32)).astype(jnp.bfloat16)
    contract_dims = (((1,), (1,)), ((), ()))
    group_width = D // N_TP
    accumulated = jnp.zeros((SEQ, D), jnp.float32)
    for group_index in range(N_TP):
        start_col = group_index * group_width
        stop_col = start_col + group_width
        group_term = lax.dot_general(grad_key[:, start_col:stop_col], w_key[:, start_col:stop_col], contract_dims, preferred_element_type=jnp.float32)
        group_term = group_term + lax.dot_general(grad_query[:, start_col:stop_col], w_query[:, start_col:stop_col], contract_dims, preferred_element_type=jnp.float32)
        group_term = group_term + lax.dot_general(grad_value[:, start_col:stop_col], w_value[:, start_col:stop_col], contract_dims, preferred_element_type=jnp.float32)
        rounded = lax.optimization_barrier(group_term.astype(jnp.bfloat16))
        accumulated = accumulated + rounded.astype(jnp.float32)
    return (accumulated.astype(jnp.bfloat16), grad_filter)
```

```python
import math

import jax
import jax.numpy as jnp
import numpy as np
from jax import lax
from jax.experimental import pallas as pl
from jax.experimental.pallas import tpu as pltpu
from jax.sharding import PartitionSpec as P

VMEM_LIMIT = 48 * 1024 * 1024


def compiler_params():
    return pltpu.CompilerParams(vmem_limit_bytes=VMEM_LIMIT)


def dft_tables(blocks, block_len, scale):
    index = np.arange(block_len)
    angle = 2.0 * np.pi * (np.outer(index, index) % block_len) / block_len
    cos, sin = np.cos(angle), np.sin(angle)
    forward = np.block([[cos, -sin], [sin, cos]])
    inverse = forward.T
    rows = np.arange(blocks + 1)
    phase = 2.0 * np.pi * np.outer(rows, index) / (2 * blocks * block_len)
    weight = np.where((rows == 0) | (rows == blocks), 1.0, 2.0)[:, None] * scale
    twiddle = np.stack(
        [np.cos(phase), np.sin(phase), weight * np.cos(phase), weight * np.sin(phase)]
    )
    return (
        jnp.asarray(forward, jnp.bfloat16),
        jnp.asarray(inverse, jnp.bfloat16),
        jnp.asarray(twiddle, jnp.float32),
    )


def half_spectrum(values):
    size = len(values)
    if size == 1:
        return [(values[0], None), (values[0], None)]
    even, odd = half_spectrum(values[0::2]), half_spectrum(values[1::2])
    half = size // 2
    bins = [None] * (size + 1)
    bins[0] = (even[0][0] + odd[0][0], None)
    bins[size] = (even[0][0] - odd[0][0], None)
    bins[half] = (even[half][0], -odd[half][0])
    for k in range(1, half):
        angle = math.pi * k / size
        cos, sin = math.cos(angle), math.sin(angle)
        even_re, even_im = even[k]
        odd_re, odd_im = odd[k]
        if 2 * k == half:
            turn_re = cos * (odd_re + odd_im)
            turn_im = cos * (odd_im - odd_re)
        else:
            turn_re = cos * odd_re + sin * odd_im
            turn_im = cos * odd_im - sin * odd_re
        bins[k] = (even_re + turn_re, even_im + turn_im)
        bins[size - k] = (even_re - turn_re, turn_im - even_im)
    return bins


def half_spectrum_adjoint(bins):
    size = len(bins) - 1
    if size == 1:
        return [bins[0][0] + bins[1][0]]
    half = size // 2
    even, odd = [None] * (half + 1), [None] * (half + 1)
    even[0] = (bins[0][0] + bins[size][0], None)
    odd[0] = (bins[0][0] - bins[size][0], None)
    even[half] = (bins[half][0], None)
    odd[half] = (-bins[half][1], None)
    for k in range(1, half):
        angle = math.pi * k / size
        cos, sin = math.cos(angle), math.sin(angle)
        low_re, low_im = bins[k]
        high_re, high_im = bins[size - k]
        even[k] = (low_re + high_re, low_im - high_im)
        turn_re, turn_im = low_re - high_re, low_im + high_im
        if 2 * k == half:
            odd[k] = (cos * (turn_re - turn_im), cos * (turn_re + turn_im))
        else:
            odd[k] = (cos * turn_re - sin * turn_im, cos * turn_im + sin * turn_re)
    values = [None] * size
    values[0::2] = half_spectrum_adjoint(even)
    values[1::2] = half_spectrum_adjoint(odd)
    return values


def gate_kernel(key_ref, value_ref, query_ref, grad_ref, filter_ref, out_ref):
    blocks, _, channels, block_len = out_ref.shape

    def put(slot, wide):
        turned = wide.T.astype(jnp.bfloat16)
        out_ref[:, slot] = turned.reshape(blocks, channels, block_len)

    put(0, key_ref[...].astype(jnp.float32) * value_ref[...].astype(jnp.float32))
    put(1, filter_ref[...].astype(jnp.float32))
    put(2, query_ref[...].astype(jnp.float32) * grad_ref[...].astype(jnp.float32))


def conv_kernel(in_ref, fwd_ref, inv_ref, twid_ref, out_ref, rows_ref, spec_ref):
    blocks, signals, channels, block_len = in_ref.shape
    chunk = min(channels, 16)
    steps = channels // chunk

    def analyse(step, carry):
        signal = step // steps
        start = pl.multiple_of((step % steps) * chunk, chunk)
        values = [
            in_ref[p, signal, pl.ds(start, chunk), :].astype(jnp.float32) for p in range(blocks)
        ]
        bins = half_spectrum(values)
        for k in range(blocks + 1):
            re, im = bins[k]
            if k == 0:
                im = jnp.zeros_like(re)
            else:
                cos, sin = twid_ref[0, k : k + 1, :], twid_ref[1, k : k + 1, :]
                if im is None:
                    re, im = re * cos, -(re * sin)
                else:
                    re, im = re * cos + im * sin, im * cos - re * sin
            rows_ref[k, signal, pl.ds(start, chunk), :block_len] = re.astype(jnp.bfloat16)
            rows_ref[k, signal, pl.ds(start, chunk), block_len:] = im.astype(jnp.bfloat16)
        return carry

    lax.fori_loop(0, signals * steps, analyse, 0)

    total = (blocks + 1) * signals * channels
    spec_ref[...] = jnp.dot(
        rows_ref[...].reshape(total, 2 * block_len),
        fwd_ref[...],
        preferred_element_type=jnp.float32,
    ).reshape(spec_ref.shape)

    def combine(step, carry):
        k = step // steps
        start = pl.multiple_of((step % steps) * chunk, chunk)
        rows = pl.ds(start, chunk)
        prod_re, prod_im = spec_ref[k, 0, rows, :block_len], spec_ref[k, 0, rows, block_len:]
        kern_re, kern_im = spec_ref[k, 1, rows, :block_len], spec_ref[k, 1, rows, block_len:]
        grad_re, grad_im = spec_ref[k, 2, rows, :block_len], spec_ref[k, 2, rows, block_len:]

        def put(slot, re, im):
            rows_ref[k, slot, rows, :block_len] = re.astype(jnp.bfloat16)
            rows_ref[k, slot, rows, block_len:] = im.astype(jnp.bfloat16)

        put(0, prod_re * kern_re - prod_im * kern_im, prod_re * kern_im + prod_im * kern_re)
        put(1, grad_re * kern_re + grad_im * kern_im, grad_im * kern_re - grad_re * kern_im)
        put(2, grad_re * prod_re + grad_im * prod_im, grad_im * prod_re - grad_re * prod_im)
        return carry

    lax.fori_loop(0, (blocks + 1) * steps, combine, 0)

    spec_ref[...] = jnp.dot(
        rows_ref[...].reshape(total, 2 * block_len),
        inv_ref[...],
        preferred_element_type=jnp.float32,
    ).reshape(spec_ref.shape)

    def synthesise(step, carry):
        signal = step // steps
        start = pl.multiple_of((step % steps) * chunk, chunk)
        rows = pl.ds(start, chunk)
        bins = []
        for k in range(blocks + 1):
            re, im = spec_ref[k, signal, rows, :block_len], spec_ref[k, signal, rows, block_len:]
            cos, sin = twid_ref[2, k : k + 1, :], twid_ref[3, k : k + 1, :]
            if k == 0:
                bins.append((re * cos, None))
            elif k == blocks:
                bins.append((re * cos - im * sin, None))
            else:
                bins.append((re * cos - im * sin, im * cos + re * sin))
        values = half_spectrum_adjoint(bins)
        for p in range(blocks):
            out_ref[p, signal, rows, :] = values[p].astype(jnp.bfloat16)
        return carry

    lax.fori_loop(0, signals * steps, synthesise, 0)


def project_kernel(
    back_ref, key_ref, value_ref, grad_ref, wk_ref, wq_ref, wv_ref, out_ref, filt_ref, lhs_ref
):
    blocks, _, channels, block_len = back_ref.shape
    width = blocks * channels

    @pl.when(pl.program_id(0) == 0)
    def _():
        def natural(slot):
            return back_ref[:, slot].reshape(width, block_len).astype(jnp.float32).T

        conv_out, grad_product = natural(0), natural(1)
        lhs_ref[0] = (grad_product * value_ref[...].astype(jnp.float32)).astype(jnp.bfloat16)
        lhs_ref[1] = (conv_out * grad_ref[...].astype(jnp.float32)).astype(jnp.bfloat16)
        lhs_ref[2] = (grad_product * key_ref[...].astype(jnp.float32)).astype(jnp.bfloat16)
        filt_ref[...] = natural(2).astype(jnp.bfloat16)

    dims = (((1,), (1,)), ((), ()))
    total = lax.dot_general(lhs_ref[0], wk_ref[...], dims, preferred_element_type=jnp.float32)
    total += lax.dot_general(lhs_ref[1], wq_ref[...], dims, preferred_element_type=jnp.float32)
    total += lax.dot_general(lhs_ref[2], wv_ref[...], dims, preferred_element_type=jnp.float32)
    out_ref[...] = total.astype(jnp.bfloat16)


def per_device(key_act, value_act, query_act, grad_out, long_filter, w_key, w_query, w_value):
    blocks = lax.axis_size("ctx")
    groups = lax.axis_size("tp")
    block_len, width = key_act.shape
    channels = width // blocks
    seq_len = blocks * block_len
    out_width = w_key.shape[0]
    part = out_width // groups

    sent = pl.pallas_call(
        gate_kernel,
        out_shape=jax.ShapeDtypeStruct((blocks, 3, channels, block_len), jnp.bfloat16),
        compiler_params=compiler_params(),
        name="gate",
    )(key_act, value_act, query_act, grad_out, long_filter)
    moved = lax.all_to_all(sent, "ctx", split_axis=0, concat_axis=0, tiled=True)

    forward, inverse, twiddle = dft_tables(
        blocks, block_len, 1.0 / (math.sqrt(seq_len) * 2 * seq_len)
    )
    results = pl.pallas_call(
        conv_kernel,
        out_shape=jax.ShapeDtypeStruct((blocks, 3, channels, block_len), jnp.bfloat16),
        scratch_shapes=[
            pltpu.VMEM((blocks + 1, 3, channels, 2 * block_len), jnp.bfloat16),
            pltpu.VMEM((blocks + 1, 3, channels, 2 * block_len), jnp.float32),
        ],
        compiler_params=compiler_params(),
        name="conv",
    )(moved, forward, inverse, twiddle)
    back = lax.all_to_all(results, "ctx", split_axis=0, concat_axis=0, tiled=True)

    whole = lambda shape: pl.BlockSpec(shape, lambda i: (0,) * len(shape))
    weight = pl.BlockSpec((part, width), lambda i: (i, 0))
    partial_sum, grad_filter = pl.pallas_call(
        project_kernel,
        grid=(groups,),
        in_specs=[
            whole((blocks, 3, channels, block_len)),
            whole((block_len, width)),
            whole((block_len, width)),
            whole((block_len, width)),
            weight,
            weight,
            weight,
        ],
        out_specs=[
            pl.BlockSpec((block_len, part), lambda i: (0, i)),
            whole((block_len, width)),
        ],
        out_shape=[
            jax.ShapeDtypeStruct((block_len, out_width), jnp.bfloat16),
            jax.ShapeDtypeStruct((block_len, width), jnp.bfloat16),
        ],
        scratch_shapes=[pltpu.VMEM((3, block_len, width), jnp.bfloat16)],
        compiler_params=compiler_params(),
        name="project",
    )(back, key_act, value_act, grad_out, w_key, w_query, w_value)
    grad_input = lax.psum_scatter(partial_sum, "tp", scatter_dimension=1, tiled=True)
    return (grad_input, grad_filter)


def solution(mesh):
    placed = (P("ctx", "tp"),) * 5 + (P(None, "tp"),) * 3
    return jax.shard_map(
        per_device,
        mesh=mesh,
        in_specs=placed,
        out_specs=(P("ctx", "tp"), P("ctx", "tp")),
        check_vma=False,
    )
```

```python
import math

import jax
import jax.numpy as jnp
import numpy as np
from jax import lax
from jax.experimental import pallas as pl
from jax.experimental.pallas import tpu as pltpu
from jax.sharding import PartitionSpec as P


def compiler_params(mib):
    return pltpu.CompilerParams(vmem_limit_bytes=mib * 1024 * 1024)


def dft_tables(blocks, block_len, scale):
    index = np.arange(block_len)
    angle = 2.0 * np.pi * (np.outer(index, index) % block_len) / block_len
    cos, sin = np.cos(angle), np.sin(angle)
    forward = np.block([[cos, -sin], [sin, cos]])
    inverse = forward.T
    rows = np.arange(blocks + 1)
    phase = 2.0 * np.pi * np.outer(rows, index) / (2 * blocks * block_len)
    weight = np.where((rows == 0) | (rows == blocks), 1.0, 2.0)[:, None] * scale
    twiddle = np.stack(
        [np.cos(phase), np.sin(phase), weight * np.cos(phase), weight * np.sin(phase)]
    )
    return (
        jnp.asarray(forward, jnp.bfloat16),
        jnp.asarray(inverse, jnp.bfloat16),
        jnp.asarray(twiddle, jnp.float32),
    )


def half_spectrum(values):
    size = len(values)
    if size == 1:
        return [(values[0], None), (values[0], None)]
    even, odd = half_spectrum(values[0::2]), half_spectrum(values[1::2])
    half = size // 2
    bins = [None] * (size + 1)
    bins[0] = (even[0][0] + odd[0][0], None)
    bins[size] = (even[0][0] - odd[0][0], None)
    bins[half] = (even[half][0], -odd[half][0])
    for k in range(1, half):
        angle = math.pi * k / size
        cos, sin = math.cos(angle), math.sin(angle)
        even_re, even_im = even[k]
        odd_re, odd_im = odd[k]
        if 2 * k == half:
            turn_re = cos * (odd_re + odd_im)
            turn_im = cos * (odd_im - odd_re)
        else:
            turn_re = cos * odd_re + sin * odd_im
            turn_im = cos * odd_im - sin * odd_re
        bins[k] = (even_re + turn_re, even_im + turn_im)
        bins[size - k] = (even_re - turn_re, turn_im - even_im)
    return bins


def half_spectrum_adjoint(bins):
    size = len(bins) - 1
    if size == 1:
        return [bins[0][0] + bins[1][0]]
    half = size // 2
    even, odd = [None] * (half + 1), [None] * (half + 1)
    even[0] = (bins[0][0] + bins[size][0], None)
    odd[0] = (bins[0][0] - bins[size][0], None)
    even[half] = (bins[half][0], None)
    odd[half] = (-bins[half][1], None)
    for k in range(1, half):
        angle = math.pi * k / size
        cos, sin = math.cos(angle), math.sin(angle)
        low_re, low_im = bins[k]
        high_re, high_im = bins[size - k]
        even[k] = (low_re + high_re, low_im - high_im)
        turn_re, turn_im = low_re - high_re, low_im + high_im
        if 2 * k == half:
            odd[k] = (cos * (turn_re - turn_im), cos * (turn_re + turn_im))
        else:
            odd[k] = (cos * turn_re - sin * turn_im, cos * turn_im + sin * turn_re)
    values = [None] * size
    values[0::2] = half_spectrum_adjoint(even)
    values[1::2] = half_spectrum_adjoint(odd)
    return values


def gate_kernel(key_ref, value_ref, query_ref, grad_ref, filter_ref, out_ref):
    blocks, _, channels, block_len = out_ref.shape

    def put(slot, wide):
        turned = wide.T.astype(jnp.bfloat16)
        out_ref[:, slot] = turned.reshape(blocks, channels, block_len)

    put(0, key_ref[...].astype(jnp.float32) * value_ref[...].astype(jnp.float32))
    put(1, filter_ref[...].astype(jnp.float32))
    put(2, query_ref[...].astype(jnp.float32) * grad_ref[...].astype(jnp.float32))


def conv_kernel(in_ref, fwd_ref, inv_ref, twid_ref, gates_ref, filt_ref, rows_ref, spec_ref):
    blocks, signals, channels, block_len = in_ref.shape
    chunk = min(channels, 16)
    steps = channels // chunk

    def analyse(step, carry):
        signal = step // steps
        start = pl.multiple_of((step % steps) * chunk, chunk)
        values = [
            in_ref[p, signal, pl.ds(start, chunk), :].astype(jnp.float32) for p in range(blocks)
        ]
        bins = half_spectrum(values)
        for k in range(blocks + 1):
            re, im = bins[k]
            if k == 0:
                im = jnp.zeros_like(re)
            else:
                cos, sin = twid_ref[0, k : k + 1, :], twid_ref[1, k : k + 1, :]
                if im is None:
                    re, im = re * cos, -(re * sin)
                else:
                    re, im = re * cos + im * sin, im * cos - re * sin
            rows_ref[k, signal, pl.ds(start, chunk), :block_len] = re.astype(jnp.bfloat16)
            rows_ref[k, signal, pl.ds(start, chunk), block_len:] = im.astype(jnp.bfloat16)
        return carry

    lax.fori_loop(0, signals * steps, analyse, 0)

    total = (blocks + 1) * signals * channels
    spec_ref[...] = jnp.dot(
        rows_ref[...].reshape(total, 2 * block_len),
        fwd_ref[...],
        preferred_element_type=jnp.float32,
    ).reshape(spec_ref.shape)

    def combine(step, carry):
        k = step // steps
        start = pl.multiple_of((step % steps) * chunk, chunk)
        rows = pl.ds(start, chunk)
        prod_re, prod_im = spec_ref[k, 0, rows, :block_len], spec_ref[k, 0, rows, block_len:]
        kern_re, kern_im = spec_ref[k, 1, rows, :block_len], spec_ref[k, 1, rows, block_len:]
        grad_re, grad_im = spec_ref[k, 2, rows, :block_len], spec_ref[k, 2, rows, block_len:]

        def put(slot, re, im):
            rows_ref[k, slot, rows, :block_len] = re.astype(jnp.bfloat16)
            rows_ref[k, slot, rows, block_len:] = im.astype(jnp.bfloat16)

        put(0, prod_re * kern_re - prod_im * kern_im, prod_re * kern_im + prod_im * kern_re)
        put(1, grad_re * kern_re + grad_im * kern_im, grad_im * kern_re - grad_re * kern_im)
        put(2, grad_re * prod_re + grad_im * prod_im, grad_im * prod_re - grad_re * prod_im)
        return carry

    lax.fori_loop(0, (blocks + 1) * steps, combine, 0)

    spec_ref[...] = jnp.dot(
        rows_ref[...].reshape(total, 2 * block_len),
        inv_ref[...],
        preferred_element_type=jnp.float32,
    ).reshape(spec_ref.shape)

    def synthesise(step, out_ref, signal, slot):
        start = pl.multiple_of(step * chunk, chunk)
        rows = pl.ds(start, chunk)
        bins = []
        for k in range(blocks + 1):
            re, im = spec_ref[k, signal, rows, :block_len], spec_ref[k, signal, rows, block_len:]
            cos, sin = twid_ref[2, k : k + 1, :], twid_ref[3, k : k + 1, :]
            if k == 0:
                bins.append((re * cos, None))
            elif k == blocks:
                bins.append((re * cos - im * sin, None))
            else:
                bins.append((re * cos - im * sin, im * cos + re * sin))
        values = half_spectrum_adjoint(bins)
        for p in range(blocks):
            out_ref[p, slot, rows, :] = values[p].astype(jnp.bfloat16)

    @pl.loop(0, 2 * steps)
    def _(step):
        synthesise(step % steps, gates_ref, step // steps, step // steps)

    @pl.loop(0, steps)
    def _(step):
        synthesise(step, filt_ref, 2, 0)


def natural(back_ref, slot):
    blocks, _, channels, block_len = back_ref.shape
    return back_ref[:, slot].reshape(blocks * channels, block_len).astype(jnp.float32).T


def term(lhs_ref, weight_refs, group):
    part = weight_refs[0].shape[0] // lax.axis_size("tp")
    rows = pl.ds(pl.multiple_of(group * part, part), part)
    dims = (((1,), (1,)), ((), ()))
    total = None
    for slot, weight_ref in enumerate(weight_refs):
        piece = lax.dot_general(
            lhs_ref[slot], weight_ref[rows, :], dims, preferred_element_type=jnp.float32
        )
        total = piece if total is None else total + piece
    return total


def mate_kernel(back_ref, key_ref, value_ref, grad_ref, wk_ref, wq_ref, wv_ref, lhs_ref, out_ref):
    conv_out, grad_product = natural(back_ref, 0), natural(back_ref, 1)
    lhs_ref[0] = (grad_product * value_ref[...].astype(jnp.float32)).astype(jnp.bfloat16)
    lhs_ref[1] = (conv_out * grad_ref[...].astype(jnp.float32)).astype(jnp.bfloat16)
    lhs_ref[2] = (grad_product * key_ref[...].astype(jnp.float32)).astype(jnp.bfloat16)
    me = lax.axis_index("tp")
    for slot, distance in enumerate((3, 1)):
        out_ref[slot] = term(lhs_ref, (wk_ref, wq_ref, wv_ref), me ^ distance).astype(jnp.bfloat16)


def own_kernel(lhs_ref, wk_ref, wq_ref, wv_ref, far_ref, own_ref):
    me = lax.axis_index("tp")
    far_ref[...] = term(lhs_ref, (wk_ref, wq_ref, wv_ref), me ^ 2)
    own_ref[...] = term(lhs_ref, (wk_ref, wq_ref, wv_ref), me)


def turn_kernel(back_ref, out_ref):
    out_ref[...] = natural(back_ref, 0).astype(jnp.bfloat16)


def exchange(block, distance):
    pairs = [(i, i ^ distance) for i in range(lax.axis_size("tp"))]
    return lax.ppermute(block, "tp", pairs)


def per_device(key_act, value_act, query_act, grad_out, long_filter, w_key, w_query, w_value):
    blocks = lax.axis_size("ctx")
    groups = lax.axis_size("tp")
    block_len, width = key_act.shape
    channels = width // blocks
    seq_len = blocks * block_len
    part = w_key.shape[0] // groups
    flops = 2 * block_len * part * 3 * width

    sent = pl.pallas_call(
        gate_kernel,
        out_shape=jax.ShapeDtypeStruct((blocks, 3, channels, block_len), jnp.bfloat16),
        compiler_params=compiler_params(60),
        name="gate",
    )(key_act, value_act, query_act, grad_out, long_filter)
    moved = lax.all_to_all(sent, "ctx", split_axis=0, concat_axis=0, tiled=True)

    forward, inverse, twiddle = dft_tables(
        blocks, block_len, 1.0 / (math.sqrt(seq_len) * 2 * seq_len)
    )
    gates, filt = pl.pallas_call(
        conv_kernel,
        out_shape=[
            jax.ShapeDtypeStruct((blocks, 2, channels, block_len), jnp.bfloat16),
            jax.ShapeDtypeStruct((blocks, 1, channels, block_len), jnp.bfloat16),
        ],
        scratch_shapes=[
            pltpu.VMEM((blocks + 1, 3, channels, 2 * block_len), jnp.bfloat16),
            pltpu.VMEM((blocks + 1, 3, channels, 2 * block_len), jnp.float32),
        ],
        compiler_params=compiler_params(24),
        name="conv",
    )(moved, forward, inverse, twiddle)
    back = lax.all_to_all(gates, "ctx", split_axis=0, concat_axis=0, tiled=True)
    filt, back = lax.optimization_barrier((filt, back))
    back_filt = lax.all_to_all(filt, "ctx", split_axis=0, concat_axis=0, tiled=True)

    weights = (w_key, w_query, w_value)
    lhs, to_mate = pl.pallas_call(
        mate_kernel,
        out_shape=[
            jax.ShapeDtypeStruct((3, block_len, width), jnp.bfloat16),
            jax.ShapeDtypeStruct((2, block_len, part), jnp.bfloat16),
        ],
        compiler_params=compiler_params(24),
        cost_estimate=pl.CostEstimate(flops=2 * flops, bytes_accessed=1 << 23, transcendentals=0),
        name="mate",
    )(back, key_act, value_act, grad_out, *weights)
    from_mate = exchange(to_mate, 1)
    far, own = pl.pallas_call(
        own_kernel,
        out_shape=[jax.ShapeDtypeStruct((block_len, part), jnp.float32)] * 2,
        compiler_params=compiler_params(24),
        cost_estimate=pl.CostEstimate(flops=2 * flops, bytes_accessed=1 << 23, transcendentals=0),
        name="own",
    )(lhs, *weights)
    from_far = exchange((far + from_mate[0].astype(jnp.float32)).astype(jnp.bfloat16), 2)
    near = own + from_mate[1].astype(jnp.float32)
    grad_input = (near + from_far.astype(jnp.float32)).astype(jnp.bfloat16)
    grad_filter = pl.pallas_call(
        turn_kernel,
        out_shape=jax.ShapeDtypeStruct((block_len, width), jnp.bfloat16),
        compiler_params=compiler_params(24),
        name="turn",
    )(back_filt)
    return (grad_input, grad_filter)


def solution(mesh):
    placed = (P("ctx", "tp"),) * 5 + (P(None, "tp"),) * 3
    return jax.shard_map(
        per_device,
        mesh=mesh,
        in_specs=placed,
        out_specs=(P("ctx", "tp"), P("ctx", "tp")),
        check_vma=False,
    )
```

```python
import math

import jax
import jax.numpy as jnp
import numpy as np
from jax import lax
from jax.experimental import pallas as pl
from jax.experimental.pallas import tpu as pltpu
from jax.sharding import PartitionSpec as P


def compiler_params(mib):
    return pltpu.CompilerParams(vmem_limit_bytes=mib * 1024 * 1024)


def dft_tables(blocks, block_len, scale):
    index = np.arange(block_len)
    angle = 2.0 * np.pi * (np.outer(index, index) % block_len) / block_len
    cos, sin = np.cos(angle), np.sin(angle)
    forward = np.block([[cos, -sin], [sin, cos]])
    inverse = forward.T
    rows = np.arange(blocks + 1)
    phase = 2.0 * np.pi * np.outer(rows, index) / (2 * blocks * block_len)
    weight = np.where((rows == 0) | (rows == blocks), 1.0, 2.0)[:, None] * scale
    twiddle = np.stack(
        [np.cos(phase), np.sin(phase), weight * np.cos(phase), weight * np.sin(phase)]
    )
    return (
        jnp.asarray(forward, jnp.bfloat16),
        jnp.asarray(inverse, jnp.bfloat16),
        jnp.asarray(twiddle, jnp.float32),
    )


def half_spectrum(values):
    size = len(values)
    if size == 1:
        return [(values[0], None), (values[0], None)]
    even, odd = half_spectrum(values[0::2]), half_spectrum(values[1::2])
    half = size // 2
    bins = [None] * (size + 1)
    bins[0] = (even[0][0] + odd[0][0], None)
    bins[size] = (even[0][0] - odd[0][0], None)
    bins[half] = (even[half][0], -odd[half][0])
    for k in range(1, half):
        angle = math.pi * k / size
        cos, sin = math.cos(angle), math.sin(angle)
        even_re, even_im = even[k]
        odd_re, odd_im = odd[k]
        if 2 * k == half:
            turn_re = cos * (odd_re + odd_im)
            turn_im = cos * (odd_im - odd_re)
        else:
            turn_re = cos * odd_re + sin * odd_im
            turn_im = cos * odd_im - sin * odd_re
        bins[k] = (even_re + turn_re, even_im + turn_im)
        bins[size - k] = (even_re - turn_re, turn_im - even_im)
    return bins


def half_spectrum_adjoint(bins):
    size = len(bins) - 1
    if size == 1:
        return [bins[0][0] + bins[1][0]]
    half = size // 2
    even, odd = [None] * (half + 1), [None] * (half + 1)
    even[0] = (bins[0][0] + bins[size][0], None)
    odd[0] = (bins[0][0] - bins[size][0], None)
    even[half] = (bins[half][0], None)
    odd[half] = (-bins[half][1], None)
    for k in range(1, half):
        angle = math.pi * k / size
        cos, sin = math.cos(angle), math.sin(angle)
        low_re, low_im = bins[k]
        high_re, high_im = bins[size - k]
        even[k] = (low_re + high_re, low_im - high_im)
        turn_re, turn_im = low_re - high_re, low_im + high_im
        if 2 * k == half:
            odd[k] = (cos * (turn_re - turn_im), cos * (turn_re + turn_im))
        else:
            odd[k] = (cos * turn_re - sin * turn_im, cos * turn_im + sin * turn_re)
    values = [None] * size
    values[0::2] = half_spectrum_adjoint(even)
    values[1::2] = half_spectrum_adjoint(odd)
    return values


def gate_kernel(key_ref, value_ref, query_ref, grad_ref, filter_ref, *refs):
    out_refs, turn_ref = refs[:-1], refs[-1]
    blocks, _, channels, block_len = turn_ref.shape

    def put(slot, wide):
        turned = wide.T.astype(jnp.bfloat16)
        turn_ref[:, slot] = turned.reshape(blocks, channels, block_len)

    put(0, key_ref[...].astype(jnp.float32) * value_ref[...].astype(jnp.float32))
    put(1, filter_ref[...].astype(jnp.float32))
    put(2, query_ref[...].astype(jnp.float32) * grad_ref[...].astype(jnp.float32))
    me = lax.axis_index("ctx")
    for distance, out_ref in enumerate(out_refs):
        out_ref[...] = turn_ref[me ^ distance]


def conv_kernel(*refs):
    blocks = lax.axis_size("ctx")
    in_refs, (fwd_ref, inv_ref, twid_ref) = refs[:blocks], refs[blocks : blocks + 3]
    gates_refs, filt_refs = refs[blocks + 3 : 2 * blocks + 3], refs[2 * blocks + 3 : 3 * blocks + 3]
    in_ref, rows_ref, spec_ref = refs[3 * blocks + 3 :]
    _, signals, channels, block_len = in_ref.shape
    me = lax.axis_index("ctx")
    for distance, ref in enumerate(in_refs):
        in_ref[me ^ distance] = ref[...]
    chunk = min(channels, 16)
    steps = channels // chunk

    def analyse(step, carry):
        signal = step // steps
        start = pl.multiple_of((step % steps) * chunk, chunk)
        values = [
            in_ref[p, signal, pl.ds(start, chunk), :].astype(jnp.float32) for p in range(blocks)
        ]
        bins = half_spectrum(values)
        for k in range(blocks + 1):
            re, im = bins[k]
            if k == 0:
                im = jnp.zeros_like(re)
            else:
                cos, sin = twid_ref[0, k : k + 1, :], twid_ref[1, k : k + 1, :]
                if im is None:
                    re, im = re * cos, -(re * sin)
                else:
                    re, im = re * cos + im * sin, im * cos - re * sin
            rows_ref[k, signal, pl.ds(start, chunk), :block_len] = re.astype(jnp.bfloat16)
            rows_ref[k, signal, pl.ds(start, chunk), block_len:] = im.astype(jnp.bfloat16)
        return carry

    lax.fori_loop(0, signals * steps, analyse, 0)

    total = (blocks + 1) * signals * channels
    spec_ref[...] = jnp.dot(
        rows_ref[...].reshape(total, 2 * block_len),
        fwd_ref[...],
        preferred_element_type=jnp.float32,
    ).reshape(spec_ref.shape)

    def combine(step, carry):
        k = step // steps
        start = pl.multiple_of((step % steps) * chunk, chunk)
        rows = pl.ds(start, chunk)
        prod_re, prod_im = spec_ref[k, 0, rows, :block_len], spec_ref[k, 0, rows, block_len:]
        kern_re, kern_im = spec_ref[k, 1, rows, :block_len], spec_ref[k, 1, rows, block_len:]
        grad_re, grad_im = spec_ref[k, 2, rows, :block_len], spec_ref[k, 2, rows, block_len:]

        def put(slot, re, im):
            rows_ref[k, slot, rows, :block_len] = re.astype(jnp.bfloat16)
            rows_ref[k, slot, rows, block_len:] = im.astype(jnp.bfloat16)

        put(0, prod_re * kern_re - prod_im * kern_im, prod_re * kern_im + prod_im * kern_re)
        put(1, grad_re * kern_re + grad_im * kern_im, grad_im * kern_re - grad_re * kern_im)
        put(2, grad_re * prod_re + grad_im * prod_im, grad_im * prod_re - grad_re * prod_im)
        return carry

    lax.fori_loop(0, (blocks + 1) * steps, combine, 0)

    spec_ref[...] = jnp.dot(
        rows_ref[...].reshape(total, 2 * block_len),
        inv_ref[...],
        preferred_element_type=jnp.float32,
    ).reshape(spec_ref.shape)

    def synthesise(step, carry):
        signal = step // steps
        start = pl.multiple_of((step % steps) * chunk, chunk)
        rows = pl.ds(start, chunk)
        bins = []
        for k in range(blocks + 1):
            re, im = spec_ref[k, signal, rows, :block_len], spec_ref[k, signal, rows, block_len:]
            cos, sin = twid_ref[2, k : k + 1, :], twid_ref[3, k : k + 1, :]
            if k == 0:
                bins.append((re * cos, None))
            elif k == blocks:
                bins.append((re * cos - im * sin, None))
            else:
                bins.append((re * cos - im * sin, im * cos + re * sin))
        values = half_spectrum_adjoint(bins)
        for p in range(blocks):
            in_ref[p, signal, rows, :] = values[p].astype(jnp.bfloat16)
        return carry

    lax.fori_loop(0, signals * steps, synthesise, 0)
    for distance in range(blocks):
        gates_refs[distance][...] = in_ref[me ^ distance, 0:2]
        filt_refs[distance][...] = in_ref[me ^ distance, 2:3]


def term(lhs_ref, weight_refs, group):
    part = weight_refs[0].shape[0] // lax.axis_size("tp")
    rows = pl.ds(pl.multiple_of(group * part, part), part)
    dims = (((1,), (1,)), ((), ()))
    total = None
    for slot, weight_ref in enumerate(weight_refs):
        piece = lax.dot_general(
            lhs_ref[slot], weight_ref[rows, :], dims, preferred_element_type=jnp.float32
        )
        total = piece if total is None else total + piece
    return total


def natural(back_refs, turn_ref):
    blocks, signals, channels, block_len = turn_ref.shape
    me = lax.axis_index("ctx")
    for distance, ref in enumerate(back_refs):
        turn_ref[me ^ distance] = ref[...]
    return [
        turn_ref[:, slot].reshape(blocks * channels, block_len).astype(jnp.float32).T
        for slot in range(signals)
    ]


def project_kernel(*refs):
    blocks = lax.axis_size("ctx")
    back_refs, (key_ref, value_ref, grad_ref) = refs[:blocks], refs[blocks : blocks + 3]
    weight_refs = refs[blocks + 3 : blocks + 6]
    mate_ref, far_ref, own_ref, turn_ref, lhs_ref = refs[blocks + 6 :]
    conv_out, grad_product = natural(back_refs, turn_ref)
    lhs_ref[0] = (grad_product * value_ref[...].astype(jnp.float32)).astype(jnp.bfloat16)
    lhs_ref[1] = (conv_out * grad_ref[...].astype(jnp.float32)).astype(jnp.bfloat16)
    lhs_ref[2] = (grad_product * key_ref[...].astype(jnp.float32)).astype(jnp.bfloat16)
    group = lax.axis_index("tp")
    mate_ref[0] = term(lhs_ref, weight_refs, group ^ 3).astype(jnp.bfloat16)
    mate_ref[1] = term(lhs_ref, weight_refs, group ^ 1).astype(jnp.bfloat16)
    far_ref[...] = term(lhs_ref, weight_refs, group ^ 2)
    own_ref[...] = term(lhs_ref, weight_refs, group)


def turn_kernel(*refs):
    back_refs, (out_ref, turn_ref) = refs[:-2], refs[-2:]
    out_ref[...] = natural(back_refs, turn_ref)[0].astype(jnp.bfloat16)


def exchange(block, axis, distance):
    pairs = [(i, i ^ distance) for i in range(lax.axis_size(axis))]
    return lax.ppermute(block, axis, pairs)


def swap(pieces):
    moved = list(pieces)
    for distance in reversed(range(1, len(pieces))):
        moved[distance] = exchange(pieces[distance], "ctx", distance)
    return moved


def per_device(key_act, value_act, query_act, grad_out, long_filter, w_key, w_query, w_value):
    blocks = lax.axis_size("ctx")
    groups = lax.axis_size("tp")
    block_len, width = key_act.shape
    channels = width // blocks
    seq_len = blocks * block_len
    part = w_key.shape[0] // groups

    def arrays(count, *shape, dtype=jnp.bfloat16):
        return [jax.ShapeDtypeStruct(shape, dtype)] * count

    sent = pl.pallas_call(
        gate_kernel,
        out_shape=arrays(blocks, 3, channels, block_len),
        scratch_shapes=[pltpu.VMEM((blocks, 3, channels, block_len), jnp.bfloat16)],
        compiler_params=compiler_params(60),
        name="gate",
    )(key_act, value_act, query_act, grad_out, long_filter)
    moved = swap(sent)

    forward, inverse, twiddle = dft_tables(
        blocks, block_len, 1.0 / (math.sqrt(seq_len) * 2 * seq_len)
    )
    results = pl.pallas_call(
        conv_kernel,
        out_shape=arrays(blocks, 2, channels, block_len) + arrays(blocks, 1, channels, block_len),
        scratch_shapes=[
            pltpu.VMEM((blocks, 3, channels, block_len), jnp.bfloat16),
            pltpu.VMEM((blocks + 1, 3, channels, 2 * block_len), jnp.bfloat16),
            pltpu.VMEM((blocks + 1, 3, channels, 2 * block_len), jnp.float32),
        ],
        compiler_params=compiler_params(20),
        name="conv",
    )(*moved, forward, inverse, twiddle)
    back = swap(results[:blocks])
    filt, back = lax.optimization_barrier((results[blocks:], back))
    back_filt = swap(filt)

    to_mate, far, own = pl.pallas_call(
        project_kernel,
        out_shape=arrays(1, 2, block_len, part) + arrays(2, block_len, part, dtype=jnp.float32),
        scratch_shapes=[
            pltpu.VMEM((blocks, 2, channels, block_len), jnp.bfloat16),
            pltpu.VMEM((3, block_len, width), jnp.bfloat16),
        ],
        compiler_params=compiler_params(16),
        cost_estimate=pl.CostEstimate(
            flops=2 * block_len * 3 * width * w_key.shape[0],
            bytes_accessed=1 << 23,
            transcendentals=0,
        ),
        name="project",
    )(*back, key_act, value_act, grad_out, w_key, w_query, w_value)
    from_mate = exchange(to_mate, "tp", 1)
    far = (far + from_mate[0].astype(jnp.float32)).astype(jnp.bfloat16)
    from_far = exchange(far, "tp", 2)
    near = own + from_mate[1].astype(jnp.float32)
    grad_input = (near + from_far.astype(jnp.float32)).astype(jnp.bfloat16)
    grad_filter = pl.pallas_call(
        turn_kernel,
        out_shape=arrays(1, block_len, width)[0],
        scratch_shapes=[pltpu.VMEM((blocks, 1, channels, block_len), jnp.bfloat16)],
        compiler_params=compiler_params(16),
        name="turn",
    )(*back_filt)
    return (grad_input, grad_filter)


def solution(mesh):
    placed = (P("ctx", "tp"),) * 5 + (P(None, "tp"),) * 3
    return jax.shard_map(
        per_device,
        mesh=mesh,
        in_specs=placed,
        out_specs=(P("ctx", "tp"), P("ctx", "tp")),
        check_vma=False,
    )
```

```python
import math

import jax
import jax.numpy as jnp
import numpy as np
from jax import lax
from jax.experimental import pallas as pl
from jax.experimental.pallas import tpu as pltpu
from jax.sharding import PartitionSpec as P


def compiler_params(mib):
    return pltpu.CompilerParams(vmem_limit_bytes=int(mib * 1024 * 1024))


def dft_tables(blocks, block_len, scale):
    index = np.arange(block_len)
    angle = 2.0 * np.pi * (np.outer(index, index) % block_len) / block_len
    cos, sin = np.cos(angle), np.sin(angle)
    forward = np.block([[cos, -sin], [sin, cos]])
    inverse = forward.T
    rows = np.arange(blocks + 1)
    phase = 2.0 * np.pi * np.outer(rows, index) / (2 * blocks * block_len)
    weight = np.where((rows == 0) | (rows == blocks), 1.0, 2.0)[:, None] * scale
    twiddle = np.stack(
        [np.cos(phase), np.sin(phase), weight * np.cos(phase), weight * np.sin(phase)]
    )
    return (
        jnp.asarray(forward, jnp.bfloat16),
        jnp.asarray(inverse, jnp.bfloat16),
        jnp.asarray(twiddle, jnp.float32),
    )


def half_spectrum(values):
    size = len(values)
    if size == 1:
        return [(values[0], None), (values[0], None)]
    even, odd = half_spectrum(values[0::2]), half_spectrum(values[1::2])
    half = size // 2
    bins = [None] * (size + 1)
    bins[0] = (even[0][0] + odd[0][0], None)
    bins[size] = (even[0][0] - odd[0][0], None)
    bins[half] = (even[half][0], -odd[half][0])
    for k in range(1, half):
        angle = math.pi * k / size
        cos, sin = math.cos(angle), math.sin(angle)
        even_re, even_im = even[k]
        odd_re, odd_im = odd[k]
        if 2 * k == half:
            turn_re = cos * (odd_re + odd_im)
            turn_im = cos * (odd_im - odd_re)
        else:
            turn_re = cos * odd_re + sin * odd_im
            turn_im = cos * odd_im - sin * odd_re
        bins[k] = (even_re + turn_re, even_im + turn_im)
        bins[size - k] = (even_re - turn_re, turn_im - even_im)
    return bins


def half_spectrum_adjoint(bins):
    size = len(bins) - 1
    if size == 1:
        return [bins[0][0] + bins[1][0]]
    half = size // 2
    even, odd = [None] * (half + 1), [None] * (half + 1)
    even[0] = (bins[0][0] + bins[size][0], None)
    odd[0] = (bins[0][0] - bins[size][0], None)
    even[half] = (bins[half][0], None)
    odd[half] = (-bins[half][1], None)
    for k in range(1, half):
        angle = math.pi * k / size
        cos, sin = math.cos(angle), math.sin(angle)
        low_re, low_im = bins[k]
        high_re, high_im = bins[size - k]
        even[k] = (low_re + high_re, low_im - high_im)
        turn_re, turn_im = low_re - high_re, low_im + high_im
        if 2 * k == half:
            odd[k] = (cos * (turn_re - turn_im), cos * (turn_re + turn_im))
        else:
            odd[k] = (cos * turn_re - sin * turn_im, cos * turn_im + sin * turn_re)
    values = [None] * size
    values[0::2] = half_spectrum_adjoint(even)
    values[1::2] = half_spectrum_adjoint(odd)
    return values


HBM = pl.BlockSpec(memory_space=pltpu.HBM)
VMEM = pl.BlockSpec(memory_space=pltpu.VMEM)


def far_first(pieces):
    return zip(reversed(range(len(pieces))), pieces)


def fetch(sources, targets, sems):
    copies = [
        pltpu.make_async_copy(source, target, sems.at[i])
        for i, (source, target) in enumerate(zip(sources, targets))
    ]
    for copy in copies:
        copy.start()
    return copies


def gate_kernel(*refs):
    sources, refs = refs[:5], refs[5:]
    out_refs, (turn_ref, held_ref, sems) = refs[:-3], refs[-3:]
    blocks, _, channels, block_len = turn_ref.shape
    filter_copy, *copies = fetch(sources, [held_ref.at[i] for i in range(5)], sems)

    def put(slot, wide):
        turned = wide.T.astype(jnp.bfloat16)
        turn_ref[:, slot] = turned.reshape(blocks, channels, block_len)

    filter_copy.wait()
    put(1, held_ref[0].astype(jnp.float32))
    for copy in copies[:2]:
        copy.wait()
    put(0, held_ref[1].astype(jnp.float32) * held_ref[2].astype(jnp.float32))
    for copy in copies[2:]:
        copy.wait()
    put(2, held_ref[3].astype(jnp.float32) * held_ref[4].astype(jnp.float32))
    me = lax.axis_index("ctx")
    for distance, out_ref in far_first(out_refs):
        out_ref[...] = turn_ref[me ^ distance]


def conv_kernel(*refs):
    blocks = lax.axis_size("ctx")
    in_refs, (twid_ref, fwd_ref, inv_ref) = refs[:blocks], refs[blocks : blocks + 3]
    out_refs, (in_ref, rows_ref, spec_ref) = refs[blocks + 3 : -3], refs[-3:]
    _, signals, channels, block_len = in_ref.shape
    me = lax.axis_index("ctx")
    for distance, ref in far_first(in_refs):
        in_ref[me ^ distance] = ref[...]
    chunk = min(channels, 16)
    steps = channels // chunk

    def analyse(step, carry):
        signal = step // steps
        start = pl.multiple_of((step % steps) * chunk, chunk)
        values = [
            in_ref[p, signal, pl.ds(start, chunk), :].astype(jnp.float32) for p in range(blocks)
        ]
        bins = half_spectrum(values)
        for k in range(blocks + 1):
            re, im = bins[k]
            if k == 0:
                im = jnp.zeros_like(re)
            else:
                cos, sin = twid_ref[0, k : k + 1, :], twid_ref[1, k : k + 1, :]
                if im is None:
                    re, im = re * cos, -(re * sin)
                else:
                    re, im = re * cos + im * sin, im * cos - re * sin
            rows_ref[k, signal, pl.ds(start, chunk), :block_len] = re.astype(jnp.bfloat16)
            rows_ref[k, signal, pl.ds(start, chunk), block_len:] = im.astype(jnp.bfloat16)
        return carry

    lax.fori_loop(0, signals * steps, analyse, 0)

    total = (blocks + 1) * signals * channels
    spec_ref[...] = jnp.dot(
        rows_ref[...].reshape(total, 2 * block_len),
        fwd_ref[...],
        preferred_element_type=jnp.float32,
    ).reshape(spec_ref.shape)

    def combine(step, carry):
        k = step // steps
        start = pl.multiple_of((step % steps) * chunk, chunk)
        rows = pl.ds(start, chunk)
        prod_re, prod_im = spec_ref[k, 0, rows, :block_len], spec_ref[k, 0, rows, block_len:]
        kern_re, kern_im = spec_ref[k, 1, rows, :block_len], spec_ref[k, 1, rows, block_len:]
        grad_re, grad_im = spec_ref[k, 2, rows, :block_len], spec_ref[k, 2, rows, block_len:]

        def put(slot, re, im):
            rows_ref[k, slot, rows, :block_len] = re.astype(jnp.bfloat16)
            rows_ref[k, slot, rows, block_len:] = im.astype(jnp.bfloat16)

        put(0, prod_re * kern_re - prod_im * kern_im, prod_re * kern_im + prod_im * kern_re)
        put(1, grad_re * kern_re + grad_im * kern_im, grad_im * kern_re - grad_re * kern_im)
        put(2, grad_re * prod_re + grad_im * prod_im, grad_im * prod_re - grad_re * prod_im)
        return carry

    lax.fori_loop(0, (blocks + 1) * steps, combine, 0)

    spec_ref[...] = jnp.dot(
        rows_ref[...].reshape(total, 2 * block_len),
        inv_ref[...],
        preferred_element_type=jnp.float32,
    ).reshape(spec_ref.shape)

    def synthesise(step, carry):
        signal = step // steps
        start = pl.multiple_of((step % steps) * chunk, chunk)
        rows = pl.ds(start, chunk)
        bins = []
        for k in range(blocks + 1):
            re, im = spec_ref[k, signal, rows, :block_len], spec_ref[k, signal, rows, block_len:]
            cos, sin = twid_ref[2, k : k + 1, :], twid_ref[3, k : k + 1, :]
            if k == 0:
                bins.append((re * cos, None))
            elif k == blocks:
                bins.append((re * cos - im * sin, None))
            else:
                bins.append((re * cos - im * sin, im * cos + re * sin))
        values = half_spectrum_adjoint(bins)
        for p in range(blocks):
            in_ref[p, signal, rows, :] = values[p].astype(jnp.bfloat16)
        return carry

    lax.fori_loop(0, signals * steps, synthesise, 0)
    for distance, out_ref in far_first(out_refs):
        out_ref[...] = in_ref[me ^ distance]


def term(lhs_ref, weight_refs, group):
    part = weight_refs[0].shape[0] // lax.axis_size("tp")
    rows = pl.ds(pl.multiple_of(group * part, part), part)
    dims = (((1,), (1,)), ((), ()))
    total = None
    for slot, weight_ref in enumerate(weight_refs):
        piece = lax.dot_general(
            lhs_ref[slot], weight_ref[rows, :], dims, preferred_element_type=jnp.float32
        )
        total = piece if total is None else total + piece
    return total


def natural(back_refs, turn_ref):
    blocks, signals, channels, block_len = turn_ref.shape
    me = lax.axis_index("ctx")
    for distance, ref in far_first(back_refs):
        turn_ref[me ^ distance] = ref[...]
    return [
        turn_ref[:, slot].reshape(blocks * channels, block_len).astype(jnp.float32).T
        for slot in range(signals)
    ]


def mate_kernel(*refs):
    blocks = lax.axis_size("ctx")
    back_refs, (key_ref, value_ref, grad_ref) = refs[:blocks], refs[blocks : blocks + 3]
    weight_refs = refs[blocks + 3 : blocks + 6]
    lhs_ref, out_ref, filt_ref, turn_ref = refs[blocks + 6 :]
    conv_out, grad_product, grad_filter = natural(back_refs, turn_ref)
    lhs_ref[0] = (grad_product * value_ref[...].astype(jnp.float32)).astype(jnp.bfloat16)
    lhs_ref[1] = (conv_out * grad_ref[...].astype(jnp.float32)).astype(jnp.bfloat16)
    lhs_ref[2] = (grad_product * key_ref[...].astype(jnp.float32)).astype(jnp.bfloat16)
    group = lax.axis_index("tp")
    out_ref[0] = term(lhs_ref, weight_refs, group ^ 3).astype(jnp.bfloat16)
    out_ref[1] = term(lhs_ref, weight_refs, group ^ 1).astype(jnp.bfloat16)
    filt_ref[...] = grad_filter.astype(jnp.bfloat16)


def own_kernel(lhs_ref, wk_ref, wq_ref, wv_ref, far_ref, own_ref):
    group = lax.axis_index("tp")
    far_ref[...] = term(lhs_ref, (wk_ref, wq_ref, wv_ref), group ^ 2)
    own_ref[...] = term(lhs_ref, (wk_ref, wq_ref, wv_ref), group)


def exchange(block, axis, distance):
    pairs = [(i, i ^ distance) for i in range(lax.axis_size(axis))]
    return lax.ppermute(block, axis, pairs)


def swap(pieces):
    return [
        exchange(piece, "ctx", distance) if distance else piece
        for distance, piece in far_first(pieces)
    ]


def per_device(key_act, value_act, query_act, grad_out, long_filter, w_key, w_query, w_value):
    blocks = lax.axis_size("ctx")
    groups = lax.axis_size("tp")
    block_len, width = key_act.shape
    channels = width // blocks
    seq_len = blocks * block_len
    part = w_key.shape[0] // groups
    block_cost = pl.CostEstimate(
        flops=4 * block_len * 3 * width * part, bytes_accessed=1 << 22, transcendentals=0
    )

    def arrays(count, *shape, dtype=jnp.bfloat16):
        return [jax.ShapeDtypeStruct(shape, dtype)] * count

    sent = pl.pallas_call(
        gate_kernel,
        in_specs=[HBM] * 5,
        out_specs=[VMEM] * blocks,
        out_shape=arrays(blocks, 3, channels, block_len),
        scratch_shapes=[
            pltpu.VMEM((blocks, 3, channels, block_len), jnp.bfloat16),
            pltpu.VMEM((5, block_len, width), jnp.bfloat16),
            pltpu.SemaphoreType.DMA((5,)),
        ],
        compiler_params=compiler_params(62),
        name="gate",
    )(long_filter, key_act, value_act, query_act, grad_out)
    moved = swap(sent)

    forward, inverse, twiddle = dft_tables(
        blocks, block_len, 1.0 / (math.sqrt(seq_len) * 2 * seq_len)
    )
    results = pl.pallas_call(
        conv_kernel,
        in_specs=[VMEM] * (blocks + 3),
        out_shape=arrays(blocks, 3, channels, block_len),
        scratch_shapes=[
            pltpu.VMEM((blocks, 3, channels, block_len), jnp.bfloat16),
            pltpu.VMEM((blocks + 1, 3, channels, 2 * block_len), jnp.bfloat16),
            pltpu.VMEM((blocks + 1, 3, channels, 2 * block_len), jnp.float32),
        ],
        compiler_params=compiler_params(20),
        name="conv",
    )(*moved, twiddle, forward, inverse)
    back = swap(results)

    weights = (w_key, w_query, w_value)
    lhs, to_mate, grad_filter = pl.pallas_call(
        mate_kernel,
        in_specs=[VMEM] * (blocks + 6),
        out_shape=[
            *arrays(1, 3, block_len, width),
            *arrays(1, 2, block_len, part),
            *arrays(1, block_len, width),
        ],
        scratch_shapes=[pltpu.VMEM((blocks, 3, channels, block_len), jnp.bfloat16)],
        compiler_params=compiler_params(16),
        cost_estimate=block_cost,
        name="mate",
    )(*back, key_act, value_act, grad_out, *weights)
    from_mate = exchange(to_mate, "tp", 1)
    far, own = pl.pallas_call(
        own_kernel,
        in_specs=[VMEM] * 4,
        out_shape=arrays(2, block_len, part, dtype=jnp.float32),
        compiler_params=compiler_params(16),
        cost_estimate=block_cost,
        name="own",
    )(lhs, *weights)
    far = (far + from_mate[0].astype(jnp.float32)).astype(jnp.bfloat16)
    from_far = exchange(far, "tp", 2)
    near = own + from_mate[1].astype(jnp.float32)
    grad_input = (near + from_far.astype(jnp.float32)).astype(jnp.bfloat16)
    return (grad_input, grad_filter)


def solution(mesh):
    placed = (P("ctx", "tp"),) * 5 + (P(None, "tp"),) * 3
    return jax.shard_map(
        per_device,
        mesh=mesh,
        in_specs=placed,
        out_specs=(P("ctx", "tp"), P("ctx", "tp")),
        check_vma=False,
    )
```

```python
import math

import jax
import jax.numpy as jnp
import numpy as np
from jax import lax
from jax.experimental import pallas as pl
from jax.experimental.pallas import tpu as pltpu
from jax.sharding import PartitionSpec as P


def compiler_params(mib):
    return pltpu.CompilerParams(vmem_limit_bytes=int(mib * 1024 * 1024))


def dft_tables(blocks, block_len, scale):
    index = np.arange(block_len)
    angle = 2.0 * np.pi * (np.outer(index, index) % block_len) / block_len
    cos, sin = np.cos(angle), np.sin(angle)
    forward = np.block([[cos, -sin], [sin, cos]])
    inverse = forward.T
    rows = np.arange(blocks + 1)
    phase = 2.0 * np.pi * np.outer(rows, index) / (2 * blocks * block_len)
    weight = np.where((rows == 0) | (rows == blocks), 1.0, 2.0)[:, None] * scale
    twiddle = np.stack(
        [np.cos(phase), np.sin(phase), weight * np.cos(phase), weight * np.sin(phase)]
    )
    return (
        jnp.asarray(forward, jnp.bfloat16),
        jnp.asarray(inverse, jnp.bfloat16),
        jnp.asarray(twiddle, jnp.float32),
    )


def half_spectrum(values):
    size = len(values)
    if size == 1:
        return [(values[0], None), (values[0], None)]
    even, odd = half_spectrum(values[0::2]), half_spectrum(values[1::2])
    half = size // 2
    bins = [None] * (size + 1)
    bins[0] = (even[0][0] + odd[0][0], None)
    bins[size] = (even[0][0] - odd[0][0], None)
    bins[half] = (even[half][0], -odd[half][0])
    for k in range(1, half):
        angle = math.pi * k / size
        cos, sin = math.cos(angle), math.sin(angle)
        even_re, even_im = even[k]
        odd_re, odd_im = odd[k]
        if 2 * k == half:
            turn_re = cos * (odd_re + odd_im)
            turn_im = cos * (odd_im - odd_re)
        else:
            turn_re = cos * odd_re + sin * odd_im
            turn_im = cos * odd_im - sin * odd_re
        bins[k] = (even_re + turn_re, even_im + turn_im)
        bins[size - k] = (even_re - turn_re, turn_im - even_im)
    return bins


def half_spectrum_adjoint(bins):
    size = len(bins) - 1
    if size == 1:
        return [bins[0][0] + bins[1][0]]
    half = size // 2
    even, odd = [None] * (half + 1), [None] * (half + 1)
    even[0] = (bins[0][0] + bins[size][0], None)
    odd[0] = (bins[0][0] - bins[size][0], None)
    even[half] = (bins[half][0], None)
    odd[half] = (-bins[half][1], None)
    for k in range(1, half):
        angle = math.pi * k / size
        cos, sin = math.cos(angle), math.sin(angle)
        low_re, low_im = bins[k]
        high_re, high_im = bins[size - k]
        even[k] = (low_re + high_re, low_im - high_im)
        turn_re, turn_im = low_re - high_re, low_im + high_im
        if 2 * k == half:
            odd[k] = (cos * (turn_re - turn_im), cos * (turn_re + turn_im))
        else:
            odd[k] = (cos * turn_re - sin * turn_im, cos * turn_im + sin * turn_re)
    values = [None] * size
    values[0::2] = half_spectrum_adjoint(even)
    values[1::2] = half_spectrum_adjoint(odd)
    return values


HBM = pl.BlockSpec(memory_space=pltpu.HBM)
VMEM = pl.BlockSpec(memory_space=pltpu.VMEM)


def in_hbm(*arrays):
    return [pltpu.with_memory_space_constraint(array, pltpu.HBM) for array in arrays]


def far_first(pieces):
    return zip(reversed(range(len(pieces))), pieces)


def fetch(sources, targets, sems):
    copies = [
        pltpu.make_async_copy(source, target, sems.at[i])
        for i, (source, target) in enumerate(zip(sources, targets))
    ]
    for copy in copies:
        copy.start()
    return copies


def gate_kernel(*refs):
    sources, refs = refs[:5], refs[5:]
    out_refs, (turn_ref, held_ref, sems) = refs[:-3], refs[-3:]
    blocks, _, channels, block_len = turn_ref.shape
    filter_copy, *copies = fetch(sources, [held_ref.at[i] for i in range(5)], sems)

    def put(slot, wide):
        turned = wide.T.astype(jnp.bfloat16)
        turn_ref[:, slot] = turned.reshape(blocks, channels, block_len)

    filter_copy.wait()
    put(1, held_ref[0].astype(jnp.float32))
    for copy in copies[:2]:
        copy.wait()
    put(0, held_ref[1].astype(jnp.float32) * held_ref[2].astype(jnp.float32))
    for copy in copies[2:]:
        copy.wait()
    put(2, held_ref[3].astype(jnp.float32) * held_ref[4].astype(jnp.float32))
    me = lax.axis_index("ctx")
    for distance, out_ref in far_first(out_refs):
        out_ref[...] = turn_ref[me ^ distance]


def conv_kernel(*refs):
    blocks = lax.axis_size("ctx")
    in_refs, tables, out_refs = refs[:blocks], refs[blocks : blocks + 3], refs[blocks + 3 : -7]
    in_ref, rows_ref, spec_ref, twid_ref, fwd_ref, inv_ref, sems = refs[-7:]
    twid_copy, fwd_copy, inv_copy = fetch(tables, (twid_ref, fwd_ref, inv_ref), sems)
    _, signals, channels, block_len = in_ref.shape
    me = lax.axis_index("ctx")
    for distance, ref in far_first(in_refs):
        in_ref[me ^ distance] = ref[...]
    twid_copy.wait()
    chunk = min(channels, 16)
    steps = channels // chunk

    def analyse(step, carry):
        signal = step // steps
        start = pl.multiple_of((step % steps) * chunk, chunk)
        values = [
            in_ref[p, signal, pl.ds(start, chunk), :].astype(jnp.float32) for p in range(blocks)
        ]
        bins = half_spectrum(values)
        for k in range(blocks + 1):
            re, im = bins[k]
            if k == 0:
                im = jnp.zeros_like(re)
            else:
                cos, sin = twid_ref[0, k : k + 1, :], twid_ref[1, k : k + 1, :]
                if im is None:
                    re, im = re * cos, -(re * sin)
                else:
                    re, im = re * cos + im * sin, im * cos - re * sin
            rows_ref[k, signal, pl.ds(start, chunk), :block_len] = re.astype(jnp.bfloat16)
            rows_ref[k, signal, pl.ds(start, chunk), block_len:] = im.astype(jnp.bfloat16)
        return carry

    lax.fori_loop(0, signals * steps, analyse, 0)
    fwd_copy.wait()
    inv_copy.wait()

    total = (blocks + 1) * signals * channels
    spec_ref[...] = jnp.dot(
        rows_ref[...].reshape(total, 2 * block_len),
        fwd_ref[...],
        preferred_element_type=jnp.float32,
    ).reshape(spec_ref.shape)

    def combine(step, carry):
        k = step // steps
        start = pl.multiple_of((step % steps) * chunk, chunk)
        rows = pl.ds(start, chunk)
        prod_re, prod_im = spec_ref[k, 0, rows, :block_len], spec_ref[k, 0, rows, block_len:]
        kern_re, kern_im = spec_ref[k, 1, rows, :block_len], spec_ref[k, 1, rows, block_len:]
        grad_re, grad_im = spec_ref[k, 2, rows, :block_len], spec_ref[k, 2, rows, block_len:]

        def put(slot, re, im):
            rows_ref[k, slot, rows, :block_len] = re.astype(jnp.bfloat16)
            rows_ref[k, slot, rows, block_len:] = im.astype(jnp.bfloat16)

        put(0, prod_re * kern_re - prod_im * kern_im, prod_re * kern_im + prod_im * kern_re)
        put(1, grad_re * kern_re + grad_im * kern_im, grad_im * kern_re - grad_re * kern_im)
        put(2, grad_re * prod_re + grad_im * prod_im, grad_im * prod_re - grad_re * prod_im)
        return carry

    lax.fori_loop(0, (blocks + 1) * steps, combine, 0)

    spec_ref[...] = jnp.dot(
        rows_ref[...].reshape(total, 2 * block_len),
        inv_ref[...],
        preferred_element_type=jnp.float32,
    ).reshape(spec_ref.shape)

    def synthesise(step, carry):
        signal = step // steps
        start = pl.multiple_of((step % steps) * chunk, chunk)
        rows = pl.ds(start, chunk)
        bins = []
        for k in range(blocks + 1):
            re, im = spec_ref[k, signal, rows, :block_len], spec_ref[k, signal, rows, block_len:]
            cos, sin = twid_ref[2, k : k + 1, :], twid_ref[3, k : k + 1, :]
            if k == 0:
                bins.append((re * cos, None))
            elif k == blocks:
                bins.append((re * cos - im * sin, None))
            else:
                bins.append((re * cos - im * sin, im * cos + re * sin))
        values = half_spectrum_adjoint(bins)
        for p in range(blocks):
            in_ref[p, signal, rows, :] = values[p].astype(jnp.bfloat16)
        return carry

    lax.fori_loop(0, signals * steps, synthesise, 0)
    for distance, out_ref in far_first(out_refs):
        out_ref[...] = in_ref[me ^ distance]


def term(lhs_ref, weight_refs, group):
    part = weight_refs[0].shape[0] // lax.axis_size("tp")
    rows = pl.ds(pl.multiple_of(group * part, part), part)
    dims = (((1,), (1,)), ((), ()))
    total = None
    for slot, weight_ref in enumerate(weight_refs):
        piece = lax.dot_general(
            lhs_ref[slot], weight_ref[rows, :], dims, preferred_element_type=jnp.float32
        )
        total = piece if total is None else total + piece
    return total


def natural(back_refs, turn_ref):
    blocks, signals, channels, block_len = turn_ref.shape
    me = lax.axis_index("ctx")
    for distance, ref in far_first(back_refs):
        turn_ref[me ^ distance] = ref[...]
    return [
        turn_ref[:, slot].reshape(blocks * channels, block_len).astype(jnp.float32).T
        for slot in range(signals)
    ]


def hold_kernel(*refs):
    count = len(refs) // 2
    for copy in fetch(refs[:count], refs[count : 2 * count], refs[-1]):
        copy.wait()


def mate_kernel(*refs):
    blocks = lax.axis_size("ctx")
    back_refs, (key_ref, value_ref, grad_ref) = refs[:blocks], refs[blocks : blocks + 3]
    weight_refs = refs[blocks + 3 : blocks + 6]
    lhs_ref, out_ref, filt_ref, turn_ref = refs[blocks + 6 :]
    conv_out, grad_product, grad_filter = natural(back_refs, turn_ref)
    lhs_ref[0] = (grad_product * value_ref[...].astype(jnp.float32)).astype(jnp.bfloat16)
    lhs_ref[1] = (conv_out * grad_ref[...].astype(jnp.float32)).astype(jnp.bfloat16)
    lhs_ref[2] = (grad_product * key_ref[...].astype(jnp.float32)).astype(jnp.bfloat16)
    group = lax.axis_index("tp")
    out_ref[0] = term(lhs_ref, weight_refs, group ^ 3).astype(jnp.bfloat16)
    out_ref[1] = term(lhs_ref, weight_refs, group ^ 1).astype(jnp.bfloat16)
    filt_ref[...] = grad_filter.astype(jnp.bfloat16)


def own_kernel(lhs_ref, wk_ref, wq_ref, wv_ref, far_ref, own_ref):
    group = lax.axis_index("tp")
    far_ref[...] = term(lhs_ref, (wk_ref, wq_ref, wv_ref), group ^ 2)
    own_ref[...] = term(lhs_ref, (wk_ref, wq_ref, wv_ref), group)


def exchange(block, axis, distance):
    pairs = [(i, i ^ distance) for i in range(lax.axis_size(axis))]
    return lax.ppermute(block, axis, pairs)


def swap(pieces):
    return [
        exchange(piece, "ctx", distance) if distance else piece
        for distance, piece in far_first(pieces)
    ]


def per_device(key_act, value_act, query_act, grad_out, long_filter, w_key, w_query, w_value):
    blocks = lax.axis_size("ctx")
    groups = lax.axis_size("tp")
    block_len, width = key_act.shape
    channels = width // blocks
    seq_len = blocks * block_len
    part = w_key.shape[0] // groups
    block_cost = pl.CostEstimate(
        flops=4 * block_len * 3 * width * part, bytes_accessed=1 << 22, transcendentals=0
    )

    def arrays(count, *shape, dtype=jnp.bfloat16):
        return [pltpu.VMEM(shape, dtype)] * count

    sent = pl.pallas_call(
        gate_kernel,
        in_specs=[HBM] * 5,
        out_shape=arrays(blocks, 3, channels, block_len),
        scratch_shapes=[
            pltpu.VMEM((blocks, 3, channels, block_len), jnp.bfloat16),
            pltpu.VMEM((5, block_len, width), jnp.bfloat16),
            pltpu.SemaphoreType.DMA((5,)),
        ],
        compiler_params=compiler_params(12),
        name="gate",
    )(*in_hbm(long_filter, key_act, value_act, query_act, grad_out))
    moved = swap(sent)

    forward, inverse, twiddle = dft_tables(
        blocks, block_len, 1.0 / (math.sqrt(seq_len) * 2 * seq_len)
    )
    results = pl.pallas_call(
        conv_kernel,
        in_specs=[VMEM] * blocks + [HBM] * 3,
        out_shape=arrays(blocks, 3, channels, block_len),
        scratch_shapes=[
            pltpu.VMEM((blocks, 3, channels, block_len), jnp.bfloat16),
            pltpu.VMEM((blocks + 1, 3, channels, 2 * block_len), jnp.bfloat16),
            pltpu.VMEM((blocks + 1, 3, channels, 2 * block_len), jnp.float32),
            pltpu.VMEM(twiddle.shape, jnp.float32),
            pltpu.VMEM(forward.shape, jnp.bfloat16),
            pltpu.VMEM(inverse.shape, jnp.bfloat16),
            pltpu.SemaphoreType.DMA((3,)),
        ],
        compiler_params=compiler_params(20),
        name="conv",
    )(*moved, *in_hbm(twiddle, forward, inverse))
    back = swap(results)

    held = (key_act, value_act, grad_out, w_key, w_query, w_value)
    held, _ = lax.optimization_barrier((held, results[0]))
    held = pl.pallas_call(
        hold_kernel,
        in_specs=[HBM] * len(held),
        out_shape=[pltpu.VMEM(array.shape, array.dtype) for array in held],
        scratch_shapes=[pltpu.SemaphoreType.DMA((len(held),))],
        compiler_params=compiler_params(12),
        cost_estimate=pl.CostEstimate(flops=0, bytes_accessed=1 << 23, transcendentals=0),
        name="hold",
    )(*in_hbm(*held))
    weights = held[3:]
    lhs, to_mate, grad_filter = pl.pallas_call(
        mate_kernel,
        in_specs=[VMEM] * (blocks + 6),
        out_shape=[
            *arrays(1, 3, block_len, width),
            *arrays(1, 2, block_len, part),
            jax.ShapeDtypeStruct((block_len, width), jnp.bfloat16),
        ],
        scratch_shapes=[pltpu.VMEM((blocks, 3, channels, block_len), jnp.bfloat16)],
        compiler_params=compiler_params(16),
        cost_estimate=block_cost,
        name="mate",
    )(*back, *held)
    from_mate = exchange(to_mate, "tp", 1)
    far, own = pl.pallas_call(
        own_kernel,
        in_specs=[VMEM] * 4,
        out_shape=arrays(2, block_len, part, dtype=jnp.float32),
        compiler_params=compiler_params(16),
        cost_estimate=block_cost,
        name="own",
    )(lhs, *weights)
    far = (far + from_mate[0].astype(jnp.float32)).astype(jnp.bfloat16)
    from_far = exchange(far, "tp", 2)
    near = own + from_mate[1].astype(jnp.float32)
    grad_input = (near + from_far.astype(jnp.float32)).astype(jnp.bfloat16)
    return (grad_input, grad_filter)


def solution(mesh):
    placed = (P("ctx", "tp"),) * 5 + (P(None, "tp"),) * 3
    return jax.shard_map(
        per_device,
        mesh=mesh,
        in_specs=placed,
        out_specs=(P("ctx", "tp"), P("ctx", "tp")),
        check_vma=False,
    )
```

```python
import math

import jax
import jax.numpy as jnp
import numpy as np
from jax import lax
from jax.experimental import pallas as pl
from jax.experimental.pallas import tpu as pltpu
from jax.sharding import PartitionSpec as P


def compiler_params(mib):
    return pltpu.CompilerParams(vmem_limit_bytes=int(mib * 1024 * 1024))


def dft_tables(blocks, block_len, scale):
    index = np.arange(block_len)
    angle = 2.0 * np.pi * (np.outer(index, index) % block_len) / block_len
    cos, sin = np.cos(angle), np.sin(angle)
    forward = np.block([[cos, -sin], [sin, cos]])
    inverse = forward.T
    rows = np.arange(blocks + 1)
    phase = 2.0 * np.pi * np.outer(rows, index) / (2 * blocks * block_len)
    weight = np.where((rows == 0) | (rows == blocks), 1.0, 2.0)[:, None] * scale
    twiddle = np.stack(
        [np.cos(phase), np.sin(phase), weight * np.cos(phase), weight * np.sin(phase)]
    )
    return (
        jnp.asarray(forward, jnp.bfloat16),
        jnp.asarray(inverse, jnp.bfloat16),
        jnp.asarray(twiddle, jnp.float32),
    )


def half_spectrum(values):
    size = len(values)
    if size == 1:
        return [(values[0], None), (values[0], None)]
    even, odd = half_spectrum(values[0::2]), half_spectrum(values[1::2])
    half = size // 2
    bins = [None] * (size + 1)
    bins[0] = (even[0][0] + odd[0][0], None)
    bins[size] = (even[0][0] - odd[0][0], None)
    bins[half] = (even[half][0], -odd[half][0])
    for k in range(1, half):
        angle = math.pi * k / size
        cos, sin = math.cos(angle), math.sin(angle)
        even_re, even_im = even[k]
        odd_re, odd_im = odd[k]
        if 2 * k == half:
            turn_re = cos * (odd_re + odd_im)
            turn_im = cos * (odd_im - odd_re)
        else:
            turn_re = cos * odd_re + sin * odd_im
            turn_im = cos * odd_im - sin * odd_re
        bins[k] = (even_re + turn_re, even_im + turn_im)
        bins[size - k] = (even_re - turn_re, turn_im - even_im)
    return bins


def half_spectrum_adjoint(bins):
    size = len(bins) - 1
    if size == 1:
        return [bins[0][0] + bins[1][0]]
    half = size // 2
    even, odd = [None] * (half + 1), [None] * (half + 1)
    even[0] = (bins[0][0] + bins[size][0], None)
    odd[0] = (bins[0][0] - bins[size][0], None)
    even[half] = (bins[half][0], None)
    odd[half] = (-bins[half][1], None)
    for k in range(1, half):
        angle = math.pi * k / size
        cos, sin = math.cos(angle), math.sin(angle)
        low_re, low_im = bins[k]
        high_re, high_im = bins[size - k]
        even[k] = (low_re + high_re, low_im - high_im)
        turn_re, turn_im = low_re - high_re, low_im + high_im
        if 2 * k == half:
            odd[k] = (cos * (turn_re - turn_im), cos * (turn_re + turn_im))
        else:
            odd[k] = (cos * turn_re - sin * turn_im, cos * turn_im + sin * turn_re)
    values = [None] * size
    values[0::2] = half_spectrum_adjoint(even)
    values[1::2] = half_spectrum_adjoint(odd)
    return values


HBM = pl.BlockSpec(memory_space=pltpu.HBM)
VMEM = pl.BlockSpec(memory_space=pltpu.VMEM)


def in_hbm(*arrays):
    return [pltpu.with_memory_space_constraint(array, pltpu.HBM) for array in arrays]


def far_first(pieces):
    return zip(reversed(range(len(pieces))), pieces)


def fetch(sources, targets, sems):
    copies = [
        pltpu.make_async_copy(source, target, sems.at[i])
        for i, (source, target) in enumerate(zip(sources, targets))
    ]
    for copy in copies:
        copy.start()
    return copies


def gate_kernel(*refs):
    sources, refs = refs[:5], refs[5:]
    out_refs, (turn_ref, held_ref, sems) = refs[:-3], refs[-3:]
    blocks, _, channels, block_len = turn_ref.shape
    filter_copy, *copies = fetch(sources, [held_ref.at[i] for i in range(5)], sems)

    def put(slot, wide):
        turned = wide.T.astype(jnp.bfloat16)
        turn_ref[:, slot] = turned.reshape(blocks, channels, block_len)

    filter_copy.wait()
    put(1, held_ref[0].astype(jnp.float32))
    for copy in copies[:2]:
        copy.wait()
    put(0, held_ref[1].astype(jnp.float32) * held_ref[2].astype(jnp.float32))
    for copy in copies[2:]:
        copy.wait()
    put(2, held_ref[3].astype(jnp.float32) * held_ref[4].astype(jnp.float32))
    me = lax.axis_index("ctx")
    for distance, out_ref in far_first(out_refs):
        out_ref[...] = turn_ref[me ^ distance]


def conv_kernel(*refs):
    blocks = lax.axis_size("ctx")
    in_refs, tables, out_refs = refs[:blocks], refs[blocks : blocks + 3], refs[blocks + 3 : -7]
    in_ref, rows_ref, spec_ref, twid_ref, fwd_ref, inv_ref, sems = refs[-7:]
    twid_copy, fwd_copy, inv_copy = fetch(tables, (twid_ref, fwd_ref, inv_ref), sems)
    groups, bins_count, signals, chunk, _ = rows_ref.shape
    block_len = in_ref.shape[-1]
    me = lax.axis_index("ctx")
    for distance, ref in far_first(in_refs):
        in_ref[me ^ distance] = ref[...]
    twid_copy.wait()

    def each(count, body):
        if blocks <= 8:
            for i in range(count):
                body(i)
        else:
            pl.loop(0, count)(body)

    def put(group, k, slot, re, im):
        rows_ref[group, k, slot, :, :block_len] = re.astype(jnp.bfloat16)
        rows_ref[group, k, slot, :, block_len:] = im.astype(jnp.bfloat16)

    def get(group, k, slot):
        return spec_ref[group, k, slot, :, :block_len], spec_ref[group, k, slot, :, block_len:]

    def analyse(group):
        rows = pl.ds(group * chunk, chunk)

        def one(signal):
            bins = half_spectrum(
                [in_ref[p, signal, rows, :].astype(jnp.float32) for p in range(blocks)]
            )
            for k, (re, im) in enumerate(bins):
                cos, sin = twid_ref[0, k : k + 1, :], twid_ref[1, k : k + 1, :]
                if k == 0:
                    put(group, k, signal, re, jnp.zeros_like(re))
                elif im is None:
                    put(group, k, signal, re * cos, -(re * sin))
                else:
                    put(group, k, signal, re * cos + im * sin, im * cos - re * sin)

        each(signals, one)

    def transform(group, table_ref):
        spec_ref[group] = jnp.dot(
            rows_ref[group].reshape(bins_count * signals * chunk, 2 * block_len),
            table_ref[...],
            preferred_element_type=jnp.float32,
        ).reshape(spec_ref.shape[1:])

    def forward(group):
        if group == 0:
            fwd_copy.wait()
        transform(group, fwd_ref)

    def combine(group):
        def one(k):
            prod_re, prod_im = get(group, k, 0)
            kern_re, kern_im = get(group, k, 1)
            grad_re, grad_im = get(group, k, 2)
            conv_re = prod_re * kern_re - prod_im * kern_im
            conv_im = prod_re * kern_im + prod_im * kern_re
            back_re = grad_re * kern_re + grad_im * kern_im
            back_im = grad_im * kern_re - grad_re * kern_im
            filt_re = grad_re * prod_re + grad_im * prod_im
            filt_im = grad_im * prod_re - grad_re * prod_im
            put(group, k, 0, conv_re, conv_im)
            put(group, k, 1, back_re, back_im)
            put(group, k, 2, filt_re, filt_im)

        each(bins_count, one)

    def inverse(group):
        if group == 0:
            inv_copy.wait()
        transform(group, inv_ref)

    def synthesise(group):
        rows = pl.ds(group * chunk, chunk)

        def one(signal):
            bins = []
            for k in range(bins_count):
                re, im = get(group, k, signal)
                cos, sin = twid_ref[2, k : k + 1, :], twid_ref[3, k : k + 1, :]
                if k == 0:
                    bins.append((re * cos, None))
                elif k == blocks:
                    bins.append((re * cos - im * sin, None))
                else:
                    bins.append((re * cos - im * sin, im * cos + re * sin))
            for p, value in enumerate(half_spectrum_adjoint(bins)):
                in_ref[p, signal, rows, :] = value.astype(jnp.bfloat16)

        each(signals, one)

    stages = (analyse, forward, combine, inverse, synthesise)
    for step in range(groups + len(stages) - 1):
        for depth, stage in reversed(list(enumerate(stages))):
            if 0 <= step - depth < groups:
                stage(step - depth)
    for distance, out_ref in far_first(out_refs):
        out_ref[...] = in_ref[me ^ distance]


def term(lhs_ref, weight_refs, group):
    part = weight_refs[0].shape[0] // lax.axis_size("tp")
    rows = pl.ds(pl.multiple_of(group * part, part), part)
    dims = (((1,), (1,)), ((), ()))
    total = None
    for slot, weight_ref in enumerate(weight_refs):
        piece = lax.dot_general(
            lhs_ref[slot], weight_ref[rows, :], dims, preferred_element_type=jnp.float32
        )
        total = piece if total is None else total + piece
    return total


def natural(back_refs, turn_ref, slots):
    blocks, _, channels, block_len = turn_ref.shape
    me = lax.axis_index("ctx")
    for distance, ref in far_first(back_refs):
        for i, slot in enumerate(slots):
            turn_ref[me ^ distance, i] = ref[slot]
    return [
        turn_ref[:, i].reshape(blocks * channels, block_len).astype(jnp.float32).T
        for i in range(len(slots))
    ]


def hold_kernel(*refs):
    count = len(refs) // 2
    for copy in fetch(refs[:count], refs[count : 2 * count], refs[-1]):
        copy.wait()


def mate_kernel(*refs):
    blocks = lax.axis_size("ctx")
    back_refs, (key_ref, value_ref, grad_ref) = refs[:blocks], refs[blocks : blocks + 3]
    weight_refs = refs[blocks + 3 : blocks + 6]
    lhs_ref, out_ref, turn_ref = refs[blocks + 6 :]
    conv_out, grad_product = natural(back_refs, turn_ref, (0, 1))
    lhs_ref[0] = (grad_product * value_ref[...].astype(jnp.float32)).astype(jnp.bfloat16)
    lhs_ref[1] = (conv_out * grad_ref[...].astype(jnp.float32)).astype(jnp.bfloat16)
    lhs_ref[2] = (grad_product * key_ref[...].astype(jnp.float32)).astype(jnp.bfloat16)
    out_ref[...] = term(lhs_ref, weight_refs, lax.axis_index("tp") ^ 3).astype(jnp.bfloat16)


def own_kernel(lhs_ref, wk_ref, wq_ref, wv_ref, far_ref, near_ref, own_ref):
    group = lax.axis_index("tp")
    weight_refs = (wk_ref, wq_ref, wv_ref)
    far_ref[...] = term(lhs_ref, weight_refs, group ^ 2)
    near_ref[...] = term(lhs_ref, weight_refs, group ^ 1).astype(jnp.bfloat16)
    own_ref[...] = term(lhs_ref, weight_refs, group)


def turn_kernel(*refs):
    back_refs, (out_ref, turn_ref) = refs[:-2], refs[-2:]
    out_ref[...] = natural(back_refs, turn_ref, (2,))[0].astype(jnp.bfloat16)


def exchange(block, axis, distance):
    pairs = [(i, i ^ distance) for i in range(lax.axis_size(axis))]
    return lax.ppermute(block, axis, pairs)


def swap(pieces):
    return [
        exchange(piece, "ctx", distance) if distance else piece
        for distance, piece in far_first(pieces)
    ]


def per_device(key_act, value_act, query_act, grad_out, long_filter, w_key, w_query, w_value):
    blocks = lax.axis_size("ctx")
    groups = lax.axis_size("tp")
    block_len, width = key_act.shape
    channels = width // blocks
    chunk = min(channels, 16)
    seq_len = blocks * block_len
    part = w_key.shape[0] // groups
    block_cost = pl.CostEstimate(
        flops=4 * block_len * 3 * width * part, bytes_accessed=1 << 22, transcendentals=0
    )

    def arrays(count, *shape, dtype=jnp.bfloat16):
        return [pltpu.VMEM(shape, dtype)] * count

    sent = pl.pallas_call(
        gate_kernel,
        in_specs=[HBM] * 5,
        out_shape=arrays(blocks, 3, channels, block_len),
        scratch_shapes=[
            pltpu.VMEM((blocks, 3, channels, block_len), jnp.bfloat16),
            pltpu.VMEM((5, block_len, width), jnp.bfloat16),
            pltpu.SemaphoreType.DMA((5,)),
        ],
        compiler_params=compiler_params(12),
        name="gate",
    )(*in_hbm(long_filter, key_act, value_act, query_act, grad_out))
    moved = swap(sent)

    forward, inverse, twiddle = dft_tables(
        blocks, block_len, 1.0 / (math.sqrt(seq_len) * 2 * seq_len)
    )
    results = pl.pallas_call(
        conv_kernel,
        in_specs=[VMEM] * blocks + [HBM] * 3,
        out_shape=arrays(blocks, 3, channels, block_len),
        scratch_shapes=[
            pltpu.VMEM((blocks, 3, channels, block_len), jnp.bfloat16),
            pltpu.VMEM((channels // chunk, blocks + 1, 3, chunk, 2 * block_len), jnp.bfloat16),
            pltpu.VMEM((channels // chunk, blocks + 1, 3, chunk, 2 * block_len), jnp.float32),
            pltpu.VMEM(twiddle.shape, jnp.float32),
            pltpu.VMEM(forward.shape, jnp.bfloat16),
            pltpu.VMEM(inverse.shape, jnp.bfloat16),
            pltpu.SemaphoreType.DMA((3,)),
        ],
        compiler_params=compiler_params(20),
        name="conv",
    )(*moved, *in_hbm(twiddle, forward, inverse))
    back = swap(results)

    held = (key_act, value_act, grad_out, w_key, w_query, w_value)
    held, _ = lax.optimization_barrier((held, results[-1]))
    held = pl.pallas_call(
        hold_kernel,
        in_specs=[HBM] * len(held),
        out_shape=[pltpu.VMEM(array.shape, array.dtype) for array in held],
        scratch_shapes=[pltpu.SemaphoreType.DMA((len(held),))],
        compiler_params=compiler_params(12),
        cost_estimate=pl.CostEstimate(flops=0, bytes_accessed=1 << 23, transcendentals=0),
        name="hold",
    )(*in_hbm(*held))
    weights = held[3:]
    lhs, to_mate = pl.pallas_call(
        mate_kernel,
        in_specs=[VMEM] * (blocks + 6),
        out_shape=arrays(1, 3, block_len, width) + arrays(1, block_len, part),
        scratch_shapes=[pltpu.VMEM((blocks, 2, channels, block_len), jnp.bfloat16)],
        compiler_params=compiler_params(16),
        cost_estimate=block_cost,
        name="mate",
    )(*back, *held)
    from_mate = exchange(to_mate, "tp", 1)
    far, near, own = pl.pallas_call(
        own_kernel,
        in_specs=[VMEM] * 4,
        out_shape=[
            *arrays(1, block_len, part, dtype=jnp.float32),
            *arrays(1, block_len, part),
            *arrays(1, block_len, part, dtype=jnp.float32),
        ],
        compiler_params=compiler_params(16),
        cost_estimate=block_cost,
        name="own",
    )(lhs, *weights)
    far = (far + from_mate.astype(jnp.float32)).astype(jnp.bfloat16)
    far, near, back = lax.optimization_barrier((far, near, back))
    from_far = exchange(far, "tp", 2)
    from_near = exchange(near, "tp", 1)
    grad_filter = pl.pallas_call(
        turn_kernel,
        in_specs=[VMEM] * blocks,
        out_shape=jax.ShapeDtypeStruct((block_len, width), jnp.bfloat16),
        scratch_shapes=[pltpu.VMEM((blocks, 1, channels, block_len), jnp.bfloat16)],
        compiler_params=compiler_params(16),
        cost_estimate=block_cost,
        name="turn",
    )(*back)
    total = from_far.astype(jnp.float32) + from_near.astype(jnp.float32) + own
    grad_input = total.astype(jnp.bfloat16)
    return (grad_input, grad_filter)


def solution(mesh):
    placed = (P("ctx", "tp"),) * 5 + (P(None, "tp"),) * 3
    return jax.shard_map(
        per_device,
        mesh=mesh,
        in_specs=placed,
        out_specs=(P("ctx", "tp"), P("ctx", "tp")),
        check_vma=False,
    )
```

```python
import math

import jax
import jax.numpy as jnp
import numpy as np
from jax import lax
from jax.experimental import pallas as pl
from jax.experimental.pallas import tpu as pltpu
from jax.sharding import PartitionSpec as P


def compiler_params(mib):
    return pltpu.CompilerParams(vmem_limit_bytes=int(mib * 1024 * 1024))


def dft_tables(blocks, block_len, scale):
    index = np.arange(block_len)
    angle = 2.0 * np.pi * (np.outer(index, index) % block_len) / block_len
    cos, sin = np.cos(angle), np.sin(angle)
    forward = np.block([[cos, -sin], [sin, cos]])
    inverse = forward.T
    rows = np.arange(blocks + 1)
    phase = 2.0 * np.pi * np.outer(rows, index) / (2 * blocks * block_len)
    weight = np.where((rows == 0) | (rows == blocks), 1.0, 2.0)[:, None] * scale
    twiddle = np.stack(
        [np.cos(phase), np.sin(phase), weight * np.cos(phase), weight * np.sin(phase)]
    )
    return (
        jnp.asarray(forward, jnp.bfloat16),
        jnp.asarray(inverse, jnp.bfloat16),
        jnp.asarray(twiddle, jnp.float32),
    )


def half_spectrum(values):
    size = len(values)
    if size == 1:
        return [(values[0], None), (values[0], None)]
    even, odd = half_spectrum(values[0::2]), half_spectrum(values[1::2])
    half = size // 2
    bins = [None] * (size + 1)
    bins[0] = (even[0][0] + odd[0][0], None)
    bins[size] = (even[0][0] - odd[0][0], None)
    bins[half] = (even[half][0], -odd[half][0])
    for k in range(1, half):
        angle = math.pi * k / size
        cos, sin = math.cos(angle), math.sin(angle)
        even_re, even_im = even[k]
        odd_re, odd_im = odd[k]
        if 2 * k == half:
            turn_re = cos * (odd_re + odd_im)
            turn_im = cos * (odd_im - odd_re)
        else:
            turn_re = cos * odd_re + sin * odd_im
            turn_im = cos * odd_im - sin * odd_re
        bins[k] = (even_re + turn_re, even_im + turn_im)
        bins[size - k] = (even_re - turn_re, turn_im - even_im)
    return bins


def half_spectrum_adjoint(bins):
    size = len(bins) - 1
    if size == 1:
        return [bins[0][0] + bins[1][0]]
    half = size // 2
    even, odd = [None] * (half + 1), [None] * (half + 1)
    even[0] = (bins[0][0] + bins[size][0], None)
    odd[0] = (bins[0][0] - bins[size][0], None)
    even[half] = (bins[half][0], None)
    odd[half] = (-bins[half][1], None)
    for k in range(1, half):
        angle = math.pi * k / size
        cos, sin = math.cos(angle), math.sin(angle)
        low_re, low_im = bins[k]
        high_re, high_im = bins[size - k]
        even[k] = (low_re + high_re, low_im - high_im)
        turn_re, turn_im = low_re - high_re, low_im + high_im
        if 2 * k == half:
            odd[k] = (cos * (turn_re - turn_im), cos * (turn_re + turn_im))
        else:
            odd[k] = (cos * turn_re - sin * turn_im, cos * turn_im + sin * turn_re)
    values = [None] * size
    values[0::2] = half_spectrum_adjoint(even)
    values[1::2] = half_spectrum_adjoint(odd)
    return values


HBM = pl.BlockSpec(memory_space=pltpu.HBM)
VMEM = pl.BlockSpec(memory_space=pltpu.VMEM)


def in_hbm(*arrays):
    return [pltpu.with_memory_space_constraint(array, pltpu.HBM) for array in arrays]


def by_distance(pieces):
    last = len(pieces) - 1
    order = [last - i // 2 if i % 2 == 0 else 1 + i // 2 for i in range(last)]
    return zip([*order, 0], pieces)


def fetch(sources, targets, sems):
    copies = [
        pltpu.make_async_copy(source, target, sems.at[i])
        for i, (source, target) in enumerate(zip(sources, targets))
    ]
    for copy in copies:
        copy.start()
    return copies


def gate_kernel(*refs):
    sources, refs = refs[:5], refs[5:]
    out_refs, (turn_ref, held_ref, sems) = refs[:-3], refs[-3:]
    blocks, _, channels, block_len = turn_ref.shape
    filter_copy, *copies = fetch(sources, [held_ref.at[i] for i in range(5)], sems)

    def put(slot, wide):
        turned = wide.T.astype(jnp.bfloat16)
        turn_ref[:, slot] = turned.reshape(blocks, channels, block_len)

    filter_copy.wait()
    put(1, held_ref[0].astype(jnp.float32))
    for copy in copies[:2]:
        copy.wait()
    put(0, held_ref[1].astype(jnp.float32) * held_ref[2].astype(jnp.float32))
    for copy in copies[2:]:
        copy.wait()
    put(2, held_ref[3].astype(jnp.float32) * held_ref[4].astype(jnp.float32))
    me = lax.axis_index("ctx")
    for distance, out_ref in by_distance(out_refs):
        out_ref[...] = turn_ref[me ^ distance]


def conv_kernel(*refs):
    blocks = lax.axis_size("ctx")
    in_refs, sources, refs = refs[:blocks], refs[blocks : blocks + 9], refs[blocks + 9 :]
    out_refs, held_refs = refs[:blocks], refs[blocks : blocks + 6]
    in_ref, rows_ref, spec_ref, twid_ref, fwd_ref, inv_ref, sems = refs[blocks + 6 :]
    twid_copy, fwd_copy, inv_copy, *held_copies = fetch(
        sources, (twid_ref, fwd_ref, inv_ref, *held_refs), sems
    )
    groups, bins_count, signals, chunk, _ = rows_ref.shape
    block_len = in_ref.shape[-1]
    me = lax.axis_index("ctx")
    for distance, ref in by_distance(in_refs):
        in_ref[me ^ distance] = ref[...]
    twid_copy.wait()

    def each(count, body):
        if blocks <= 8:
            for i in range(count):
                body(i)
        else:
            pl.loop(0, count)(body)

    def put(group, k, slot, re, im):
        rows_ref[group, k, slot, :, :block_len] = re.astype(jnp.bfloat16)
        rows_ref[group, k, slot, :, block_len:] = im.astype(jnp.bfloat16)

    def get(group, k, slot):
        return spec_ref[group, k, slot, :, :block_len], spec_ref[group, k, slot, :, block_len:]

    def analyse(group):
        rows = pl.ds(group * chunk, chunk)

        def one(signal):
            bins = half_spectrum(
                [in_ref[p, signal, rows, :].astype(jnp.float32) for p in range(blocks)]
            )
            for k, (re, im) in enumerate(bins):
                cos, sin = twid_ref[0, k : k + 1, :], twid_ref[1, k : k + 1, :]
                if k == 0:
                    put(group, k, signal, re, jnp.zeros_like(re))
                elif im is None:
                    put(group, k, signal, re * cos, -(re * sin))
                else:
                    put(group, k, signal, re * cos + im * sin, im * cos - re * sin)

        each(signals, one)

    def transform(group, table_ref):
        spec_ref[group] = jnp.dot(
            rows_ref[group].reshape(bins_count * signals * chunk, 2 * block_len),
            table_ref[...],
            preferred_element_type=jnp.float32,
        ).reshape(spec_ref.shape[1:])

    def forward(group):
        if group == 0:
            fwd_copy.wait()
        transform(group, fwd_ref)

    def combine(group):
        def one(k):
            prod_re, prod_im = get(group, k, 0)
            kern_re, kern_im = get(group, k, 1)
            grad_re, grad_im = get(group, k, 2)
            conv_re = prod_re * kern_re - prod_im * kern_im
            conv_im = prod_re * kern_im + prod_im * kern_re
            back_re = grad_re * kern_re + grad_im * kern_im
            back_im = grad_im * kern_re - grad_re * kern_im
            filt_re = grad_re * prod_re + grad_im * prod_im
            filt_im = grad_im * prod_re - grad_re * prod_im
            put(group, k, 0, conv_re, conv_im)
            put(group, k, 1, back_re, back_im)
            put(group, k, 2, filt_re, filt_im)

        each(bins_count, one)

    def inverse(group):
        if group == 0:
            inv_copy.wait()
        transform(group, inv_ref)

    def synthesise(group):
        rows = pl.ds(group * chunk, chunk)

        def one(signal):
            bins = []
            for k in range(bins_count):
                re, im = get(group, k, signal)
                cos, sin = twid_ref[2, k : k + 1, :], twid_ref[3, k : k + 1, :]
                if k == 0:
                    bins.append((re * cos, None))
                elif k == blocks:
                    bins.append((re * cos - im * sin, None))
                else:
                    bins.append((re * cos - im * sin, im * cos + re * sin))
            for p, value in enumerate(half_spectrum_adjoint(bins)):
                in_ref[p, signal, rows, :] = value.astype(jnp.bfloat16)

        each(signals, one)

    stages = (analyse, forward, combine, inverse, synthesise)
    for step in range(groups + len(stages) - 1):
        for depth, stage in reversed(list(enumerate(stages))):
            if 0 <= step - depth < groups:
                stage(step - depth)
    for distance, out_ref in by_distance(out_refs):
        out_ref[...] = in_ref[me ^ distance]
    for copy in held_copies:
        copy.wait()


def term(lhs_ref, weight_refs, group):
    part = weight_refs[0].shape[0] // lax.axis_size("tp")
    rows = pl.ds(pl.multiple_of(group * part, part), part)
    dims = (((1,), (1,)), ((), ()))
    total = None
    for slot, weight_ref in enumerate(weight_refs):
        piece = lax.dot_general(
            lhs_ref[slot], weight_ref[rows, :], dims, preferred_element_type=jnp.float32
        )
        total = piece if total is None else total + piece
    return total


def natural(back_refs, turn_ref, slots):
    blocks, _, channels, block_len = turn_ref.shape
    me = lax.axis_index("ctx")
    for distance, ref in by_distance(back_refs):
        for i, slot in enumerate(slots):
            turn_ref[me ^ distance, i] = ref[slot]
    return [
        turn_ref[:, i].reshape(blocks * channels, block_len).astype(jnp.float32).T
        for i in range(len(slots))
    ]


def mate_kernel(*refs):
    blocks = lax.axis_size("ctx")
    back_refs, (key_ref, value_ref, grad_ref) = refs[:blocks], refs[blocks : blocks + 3]
    weight_refs = refs[blocks + 3 : blocks + 6]
    lhs_ref, out_ref, turn_ref = refs[blocks + 6 :]
    conv_out, grad_product = natural(back_refs, turn_ref, (0, 1))
    lhs_ref[0] = (grad_product * value_ref[...].astype(jnp.float32)).astype(jnp.bfloat16)
    lhs_ref[1] = (conv_out * grad_ref[...].astype(jnp.float32)).astype(jnp.bfloat16)
    lhs_ref[2] = (grad_product * key_ref[...].astype(jnp.float32)).astype(jnp.bfloat16)
    out_ref[...] = term(lhs_ref, weight_refs, lax.axis_index("tp") ^ 3).astype(jnp.bfloat16)


def far_kernel(lhs_ref, wk_ref, wq_ref, wv_ref, far_ref, near_ref):
    group = lax.axis_index("tp")
    far_ref[...] = term(lhs_ref, (wk_ref, wq_ref, wv_ref), group ^ 2)
    near_ref[...] = term(lhs_ref, (wk_ref, wq_ref, wv_ref), group ^ 1).astype(jnp.bfloat16)


def own_kernel(lhs_ref, wk_ref, wq_ref, wv_ref, own_ref):
    own_ref[...] = term(lhs_ref, (wk_ref, wq_ref, wv_ref), lax.axis_index("tp"))


def turn_kernel(*refs):
    back_refs, (out_ref, turn_ref) = refs[:-2], refs[-2:]
    out_ref[...] = natural(back_refs, turn_ref, (2,))[0].astype(jnp.bfloat16)


def exchange(block, axis, distance):
    pairs = [(i, i ^ distance) for i in range(lax.axis_size(axis))]
    return lax.ppermute(block, axis, pairs)


def swap(pieces):
    return [
        exchange(piece, "ctx", distance) if distance else piece
        for distance, piece in by_distance(pieces)
    ]


def per_device(key_act, value_act, query_act, grad_out, long_filter, w_key, w_query, w_value):
    blocks = lax.axis_size("ctx")
    groups = lax.axis_size("tp")
    block_len, width = key_act.shape
    channels = width // blocks
    chunk = min(channels, 16)
    seq_len = blocks * block_len
    part = w_key.shape[0] // groups
    block_cost = pl.CostEstimate(
        flops=4 * block_len * 3 * width * part, bytes_accessed=1 << 22, transcendentals=0
    )

    def arrays(count, *shape, dtype=jnp.bfloat16):
        return [pltpu.VMEM(shape, dtype)] * count

    sent = pl.pallas_call(
        gate_kernel,
        in_specs=[HBM] * 5,
        out_shape=arrays(blocks, 3, channels, block_len),
        scratch_shapes=[
            pltpu.VMEM((blocks, 3, channels, block_len), jnp.bfloat16),
            pltpu.VMEM((5, block_len, width), jnp.bfloat16),
            pltpu.SemaphoreType.DMA((5,)),
        ],
        compiler_params=compiler_params(12),
        name="gate",
    )(*in_hbm(long_filter, key_act, value_act, query_act, grad_out))
    moved = swap(sent)

    forward, inverse, twiddle = dft_tables(
        blocks, block_len, 1.0 / (math.sqrt(seq_len) * 2 * seq_len)
    )
    tables = (twiddle, forward, inverse)
    held = (key_act, value_act, grad_out, w_key, w_query, w_value)
    results = pl.pallas_call(
        conv_kernel,
        in_specs=[VMEM] * blocks + [HBM] * 9,
        out_shape=arrays(blocks, 3, channels, block_len)
        + [pltpu.VMEM(array.shape, array.dtype) for array in held],
        scratch_shapes=[
            pltpu.VMEM((blocks, 3, channels, block_len), jnp.bfloat16),
            pltpu.VMEM((channels // chunk, blocks + 1, 3, chunk, 2 * block_len), jnp.bfloat16),
            pltpu.VMEM((channels // chunk, blocks + 1, 3, chunk, 2 * block_len), jnp.float32),
            *[pltpu.VMEM(array.shape, array.dtype) for array in tables],
            pltpu.SemaphoreType.DMA((9,)),
        ],
        compiler_params=compiler_params(28),
        name="conv",
    )(*moved, *in_hbm(*tables, *held))
    back, held = swap(results[:blocks]), results[blocks:]
    weights = held[3:]
    lhs, to_mate = pl.pallas_call(
        mate_kernel,
        in_specs=[VMEM] * (blocks + 6),
        out_shape=arrays(1, 3, block_len, width) + arrays(1, block_len, part),
        scratch_shapes=[pltpu.VMEM((blocks, 2, channels, block_len), jnp.bfloat16)],
        compiler_params=compiler_params(16),
        cost_estimate=block_cost,
        name="mate",
    )(*back, *held)
    from_mate = exchange(to_mate, "tp", 1)
    far, near = pl.pallas_call(
        far_kernel,
        in_specs=[VMEM] * 4,
        out_shape=arrays(1, block_len, part, dtype=jnp.float32) + arrays(1, block_len, part),
        compiler_params=compiler_params(16),
        cost_estimate=block_cost,
        name="far",
    )(lhs, *weights)
    far = (far + from_mate.astype(jnp.float32)).astype(jnp.bfloat16)
    far, near, lhs, back = lax.optimization_barrier((far, near, lhs, back))
    from_far = exchange(far, "tp", 2)
    from_near = exchange(near, "tp", 1)
    grad_filter = pl.pallas_call(
        turn_kernel,
        in_specs=[VMEM] * blocks,
        out_shape=jax.ShapeDtypeStruct((block_len, width), jnp.bfloat16),
        scratch_shapes=[pltpu.VMEM((blocks, 1, channels, block_len), jnp.bfloat16)],
        compiler_params=compiler_params(16),
        cost_estimate=block_cost,
        name="turn",
    )(*back)
    own = pl.pallas_call(
        own_kernel,
        in_specs=[VMEM] * 4,
        out_shape=arrays(1, block_len, part, dtype=jnp.float32)[0],
        compiler_params=compiler_params(16),
        cost_estimate=block_cost,
        name="own",
    )(lhs, *weights)
    total = from_far.astype(jnp.float32) + from_near.astype(jnp.float32) + own
    grad_input = total.astype(jnp.bfloat16)
    return (grad_input, grad_filter)


def solution(mesh):
    placed = (P("ctx", "tp"),) * 5 + (P(None, "tp"),) * 3
    return jax.shard_map(
        per_device,
        mesh=mesh,
        in_specs=placed,
        out_specs=(P("ctx", "tp"), P("ctx", "tp")),
        check_vma=False,
    )
```

```python
import math

import jax
import jax.numpy as jnp
import numpy as np
from jax import lax
from jax.experimental import pallas as pl
from jax.experimental.pallas import tpu as pltpu
from jax.sharding import PartitionSpec as P


def compiler_params(mib):
    return pltpu.CompilerParams(vmem_limit_bytes=int(mib * 1024 * 1024))


def dft_tables(blocks, block_len, scale):
    index = np.arange(block_len)
    angle = 2.0 * np.pi * (np.outer(index, index) % block_len) / block_len
    cos, sin = np.cos(angle), np.sin(angle)
    forward = np.block([[cos, -sin], [sin, cos]])
    inverse = forward.T
    rows = np.arange(blocks + 1)
    phase = 2.0 * np.pi * np.outer(rows, index) / (2 * blocks * block_len)
    weight = np.where((rows == 0) | (rows == blocks), 1.0, 2.0)[:, None] * scale
    twiddle = np.stack(
        [np.cos(phase), np.sin(phase), weight * np.cos(phase), weight * np.sin(phase)]
    )
    return (
        jnp.asarray(forward, jnp.bfloat16),
        jnp.asarray(inverse, jnp.bfloat16),
        jnp.asarray(twiddle, jnp.float32),
    )


def half_spectrum(values):
    size = len(values)
    if size == 1:
        return [(values[0], None), (values[0], None)]
    even, odd = half_spectrum(values[0::2]), half_spectrum(values[1::2])
    half = size // 2
    bins = [None] * (size + 1)
    bins[0] = (even[0][0] + odd[0][0], None)
    bins[size] = (even[0][0] - odd[0][0], None)
    bins[half] = (even[half][0], -odd[half][0])
    for k in range(1, half):
        angle = math.pi * k / size
        cos, sin = math.cos(angle), math.sin(angle)
        even_re, even_im = even[k]
        odd_re, odd_im = odd[k]
        if 2 * k == half:
            turn_re = cos * (odd_re + odd_im)
            turn_im = cos * (odd_im - odd_re)
        else:
            turn_re = cos * odd_re + sin * odd_im
            turn_im = cos * odd_im - sin * odd_re
        bins[k] = (even_re + turn_re, even_im + turn_im)
        bins[size - k] = (even_re - turn_re, turn_im - even_im)
    return bins


def half_spectrum_adjoint(bins):
    size = len(bins) - 1
    if size == 1:
        return [bins[0][0] + bins[1][0]]
    half = size // 2
    even, odd = [None] * (half + 1), [None] * (half + 1)
    even[0] = (bins[0][0] + bins[size][0], None)
    odd[0] = (bins[0][0] - bins[size][0], None)
    even[half] = (bins[half][0], None)
    odd[half] = (-bins[half][1], None)
    for k in range(1, half):
        angle = math.pi * k / size
        cos, sin = math.cos(angle), math.sin(angle)
        low_re, low_im = bins[k]
        high_re, high_im = bins[size - k]
        even[k] = (low_re + high_re, low_im - high_im)
        turn_re, turn_im = low_re - high_re, low_im + high_im
        if 2 * k == half:
            odd[k] = (cos * (turn_re - turn_im), cos * (turn_re + turn_im))
        else:
            odd[k] = (cos * turn_re - sin * turn_im, cos * turn_im + sin * turn_re)
    values = [None] * size
    values[0::2] = half_spectrum_adjoint(even)
    values[1::2] = half_spectrum_adjoint(odd)
    return values


HBM = pl.BlockSpec(memory_space=pltpu.HBM)
VMEM = pl.BlockSpec(memory_space=pltpu.VMEM)


def in_hbm(*arrays):
    return [pltpu.with_memory_space_constraint(array, pltpu.HBM) for array in arrays]


def distances(blocks):
    far, near = range(blocks - 1, blocks // 2 - 1, -1), range(1, blocks // 2)
    return [*near, *far, 0], [*far, *reversed(near), 0]


def by_distance(pieces):
    even, odd = distances(len(pieces))
    core = lax.axis_index("tp") % 2
    return [(a + core * (b - a), piece) for a, b, piece in zip(even, odd, pieces)]


def fetch(sources, targets, sems):
    copies = [
        pltpu.make_async_copy(source, target, sems.at[i])
        for i, (source, target) in enumerate(zip(sources, targets))
    ]
    for copy in copies:
        copy.start()
    return copies


def gate_kernel(*refs):
    sources, refs = refs[:5], refs[5:]
    out_refs, (turn_ref, held_ref, sems) = refs[:-3], refs[-3:]
    blocks, _, channels, block_len = turn_ref.shape
    filter_copy, *copies = fetch(sources, [held_ref.at[i] for i in range(5)], sems)

    def put(slot, wide):
        turned = wide.T.astype(jnp.bfloat16)
        turn_ref[:, slot] = turned.reshape(blocks, channels, block_len)

    filter_copy.wait()
    put(1, held_ref[0].astype(jnp.float32))
    for copy in copies[:2]:
        copy.wait()
    put(0, held_ref[1].astype(jnp.float32) * held_ref[2].astype(jnp.float32))
    for copy in copies[2:]:
        copy.wait()
    put(2, held_ref[3].astype(jnp.float32) * held_ref[4].astype(jnp.float32))
    me = lax.axis_index("ctx")
    for distance, out_ref in by_distance(out_refs):
        out_ref[...] = turn_ref[me ^ distance]


def conv_kernel(*refs):
    blocks = lax.axis_size("ctx")
    in_refs, sources, refs = refs[:blocks], refs[blocks : blocks + 9], refs[blocks + 9 :]
    out_refs, held_refs = refs[:blocks], refs[blocks : blocks + 6]
    in_ref, rows_ref, spec_ref, twid_ref, fwd_ref, inv_ref, sems = refs[blocks + 6 :]
    twid_copy, fwd_copy, inv_copy, *held_copies = fetch(
        sources, (twid_ref, fwd_ref, inv_ref, *held_refs), sems
    )
    groups, bins_count, signals, chunk, _ = rows_ref.shape
    block_len = in_ref.shape[-1]
    me = lax.axis_index("ctx")
    for distance, ref in by_distance(in_refs):
        in_ref[me ^ distance] = ref[...]
    twid_copy.wait()

    def each(count, body):
        if blocks <= 8:
            for i in range(count):
                body(i)
        else:
            pl.loop(0, count)(body)

    def put(group, k, slot, re, im):
        rows_ref[group, k, slot, :, :block_len] = re.astype(jnp.bfloat16)
        rows_ref[group, k, slot, :, block_len:] = im.astype(jnp.bfloat16)

    def get(group, k, slot):
        return spec_ref[group, k, slot, :, :block_len], spec_ref[group, k, slot, :, block_len:]

    def analyse(group):
        rows = pl.ds(group * chunk, chunk)

        def one(signal):
            bins = half_spectrum(
                [in_ref[p, signal, rows, :].astype(jnp.float32) for p in range(blocks)]
            )
            for k, (re, im) in enumerate(bins):
                cos, sin = twid_ref[0, k : k + 1, :], twid_ref[1, k : k + 1, :]
                if k == 0:
                    put(group, k, signal, re, jnp.zeros_like(re))
                elif im is None:
                    put(group, k, signal, re * cos, -(re * sin))
                else:
                    put(group, k, signal, re * cos + im * sin, im * cos - re * sin)

        each(signals, one)

    def transform(group, table_ref):
        spec_ref[group] = jnp.dot(
            rows_ref[group].reshape(bins_count * signals * chunk, 2 * block_len),
            table_ref[...],
            preferred_element_type=jnp.float32,
        ).reshape(spec_ref.shape[1:])

    def forward(group):
        if group == 0:
            fwd_copy.wait()
        transform(group, fwd_ref)

    def combine(group):
        def one(k):
            prod_re, prod_im = get(group, k, 0)
            kern_re, kern_im = get(group, k, 1)
            grad_re, grad_im = get(group, k, 2)
            conv_re = prod_re * kern_re - prod_im * kern_im
            conv_im = prod_re * kern_im + prod_im * kern_re
            back_re = grad_re * kern_re + grad_im * kern_im
            back_im = grad_im * kern_re - grad_re * kern_im
            filt_re = grad_re * prod_re + grad_im * prod_im
            filt_im = grad_im * prod_re - grad_re * prod_im
            put(group, k, 0, conv_re, conv_im)
            put(group, k, 1, back_re, back_im)
            put(group, k, 2, filt_re, filt_im)

        each(bins_count, one)

    def inverse(group):
        if group == 0:
            inv_copy.wait()
        transform(group, inv_ref)

    def synthesise(group):
        rows = pl.ds(group * chunk, chunk)

        def one(signal):
            bins = []
            for k in range(bins_count):
                re, im = get(group, k, signal)
                cos, sin = twid_ref[2, k : k + 1, :], twid_ref[3, k : k + 1, :]
                if k == 0:
                    bins.append((re * cos, None))
                elif k == blocks:
                    bins.append((re * cos - im * sin, None))
                else:
                    bins.append((re * cos - im * sin, im * cos + re * sin))
            for p, value in enumerate(half_spectrum_adjoint(bins)):
                in_ref[p, signal, rows, :] = value.astype(jnp.bfloat16)

        each(signals, one)

    stages = (analyse, forward, combine, inverse, synthesise)
    for step in range(groups + len(stages) - 1):
        for depth, stage in reversed(list(enumerate(stages))):
            if 0 <= step - depth < groups:
                stage(step - depth)
    for distance, out_ref in by_distance(out_refs):
        out_ref[...] = in_ref[me ^ distance]
    for copy in held_copies:
        copy.wait()


def term(lhs_ref, weight_refs, group):
    part = weight_refs[0].shape[0] // lax.axis_size("tp")
    rows = pl.ds(pl.multiple_of(group * part, part), part)
    dims = (((1,), (1,)), ((), ()))
    total = None
    for slot, weight_ref in enumerate(weight_refs):
        piece = lax.dot_general(
            lhs_ref[slot], weight_ref[rows, :], dims, preferred_element_type=jnp.float32
        )
        total = piece if total is None else total + piece
    return total


def natural(back_refs, turn_ref, slots):
    blocks, _, channels, block_len = turn_ref.shape
    me = lax.axis_index("ctx")
    for distance, ref in by_distance(back_refs):
        for i, slot in enumerate(slots):
            turn_ref[me ^ distance, i] = ref[slot]
    return [
        turn_ref[:, i].reshape(blocks * channels, block_len).astype(jnp.float32).T
        for i in range(len(slots))
    ]


def mate_kernel(*refs):
    blocks = lax.axis_size("ctx")
    back_refs, (key_ref, value_ref, grad_ref) = refs[:blocks], refs[blocks : blocks + 3]
    weight_refs = refs[blocks + 3 : blocks + 6]
    lhs_ref, out_ref, turn_ref = refs[blocks + 6 :]
    conv_out, grad_product = natural(back_refs, turn_ref, (0, 1))
    lhs_ref[0] = (grad_product * value_ref[...].astype(jnp.float32)).astype(jnp.bfloat16)
    lhs_ref[1] = (conv_out * grad_ref[...].astype(jnp.float32)).astype(jnp.bfloat16)
    lhs_ref[2] = (grad_product * key_ref[...].astype(jnp.float32)).astype(jnp.bfloat16)
    out_ref[...] = term(lhs_ref, weight_refs, lax.axis_index("tp") ^ 3).astype(jnp.bfloat16)


def far_kernel(lhs_ref, wk_ref, wq_ref, wv_ref, far_ref, near_ref):
    group = lax.axis_index("tp")
    far_ref[...] = term(lhs_ref, (wk_ref, wq_ref, wv_ref), group ^ 2)
    near_ref[...] = term(lhs_ref, (wk_ref, wq_ref, wv_ref), group ^ 1).astype(jnp.bfloat16)


def own_kernel(lhs_ref, wk_ref, wq_ref, wv_ref, own_ref):
    own_ref[...] = term(lhs_ref, (wk_ref, wq_ref, wv_ref), lax.axis_index("tp"))


def turn_kernel(*refs):
    back_refs, (out_ref, turn_ref) = refs[:-2], refs[-2:]
    out_ref[...] = natural(back_refs, turn_ref, (2,))[0].astype(jnp.bfloat16)


def exchange(block, axis, distance):
    pairs = [(i, i ^ distance) for i in range(lax.axis_size(axis))]
    return lax.ppermute(block, axis, pairs)


def swap(pieces):
    blocks, groups = lax.axis_size("ctx"), lax.axis_size("tp")
    orders = distances(blocks)
    moved = []
    for step, piece in enumerate(pieces[:-1]):
        pairs = [
            (i * groups + j, (i ^ orders[j % 2][step]) * groups + j)
            for i in range(blocks)
            for j in range(groups)
        ]
        moved.append(lax.ppermute(piece, ("ctx", "tp"), pairs))
    return [*moved, pieces[-1]]


def per_device(key_act, value_act, query_act, grad_out, long_filter, w_key, w_query, w_value):
    blocks = lax.axis_size("ctx")
    groups = lax.axis_size("tp")
    block_len, width = key_act.shape
    channels = width // blocks
    chunk = min(channels, 16)
    seq_len = blocks * block_len
    part = w_key.shape[0] // groups
    block_cost = pl.CostEstimate(
        flops=4 * block_len * 3 * width * part, bytes_accessed=1 << 22, transcendentals=0
    )

    def arrays(count, *shape, dtype=jnp.bfloat16):
        return [pltpu.VMEM(shape, dtype)] * count

    sent = pl.pallas_call(
        gate_kernel,
        in_specs=[HBM] * 5,
        out_shape=arrays(blocks, 3, channels, block_len),
        scratch_shapes=[
            pltpu.VMEM((blocks, 3, channels, block_len), jnp.bfloat16),
            pltpu.VMEM((5, block_len, width), jnp.bfloat16),
            pltpu.SemaphoreType.DMA((5,)),
        ],
        compiler_params=compiler_params(12),
        name="gate",
    )(*in_hbm(long_filter, key_act, value_act, query_act, grad_out))
    moved = swap(sent)

    forward, inverse, twiddle = dft_tables(
        blocks, block_len, 1.0 / (math.sqrt(seq_len) * 2 * seq_len)
    )
    tables = (twiddle, forward, inverse)
    held = (key_act, value_act, grad_out, w_key, w_query, w_value)
    results = pl.pallas_call(
        conv_kernel,
        in_specs=[VMEM] * blocks + [HBM] * 9,
        out_shape=arrays(blocks, 3, channels, block_len)
        + [pltpu.VMEM(array.shape, array.dtype) for array in held],
        scratch_shapes=[
            pltpu.VMEM((blocks, 3, channels, block_len), jnp.bfloat16),
            pltpu.VMEM((channels // chunk, blocks + 1, 3, chunk, 2 * block_len), jnp.bfloat16),
            pltpu.VMEM((channels // chunk, blocks + 1, 3, chunk, 2 * block_len), jnp.float32),
            *[pltpu.VMEM(array.shape, array.dtype) for array in tables],
            pltpu.SemaphoreType.DMA((9,)),
        ],
        compiler_params=compiler_params(28),
        name="conv",
    )(*moved, *in_hbm(*tables, *held))
    back, held = swap(results[:blocks]), results[blocks:]
    weights = held[3:]
    lhs, to_mate = pl.pallas_call(
        mate_kernel,
        in_specs=[VMEM] * (blocks + 6),
        out_shape=arrays(1, 3, block_len, width) + arrays(1, block_len, part),
        scratch_shapes=[pltpu.VMEM((blocks, 2, channels, block_len), jnp.bfloat16)],
        compiler_params=compiler_params(16),
        cost_estimate=block_cost,
        name="mate",
    )(*back, *held)
    from_mate = exchange(to_mate, "tp", 1)
    far, near = pl.pallas_call(
        far_kernel,
        in_specs=[VMEM] * 4,
        out_shape=arrays(1, block_len, part, dtype=jnp.float32) + arrays(1, block_len, part),
        compiler_params=compiler_params(16),
        cost_estimate=block_cost,
        name="far",
    )(lhs, *weights)
    far = (far + from_mate.astype(jnp.float32)).astype(jnp.bfloat16)
    far, near, lhs, back = lax.optimization_barrier((far, near, lhs, back))
    from_far = exchange(far, "tp", 2)
    from_near = exchange(near, "tp", 1)
    grad_filter = pl.pallas_call(
        turn_kernel,
        in_specs=[VMEM] * blocks,
        out_shape=jax.ShapeDtypeStruct((block_len, width), jnp.bfloat16),
        scratch_shapes=[pltpu.VMEM((blocks, 1, channels, block_len), jnp.bfloat16)],
        compiler_params=compiler_params(16),
        cost_estimate=block_cost,
        name="turn",
    )(*back)
    own = pl.pallas_call(
        own_kernel,
        in_specs=[VMEM] * 4,
        out_shape=arrays(1, block_len, part, dtype=jnp.float32)[0],
        compiler_params=compiler_params(16),
        cost_estimate=block_cost,
        name="own",
    )(lhs, *weights)
    total = from_far.astype(jnp.float32) + from_near.astype(jnp.float32) + own
    grad_input = total.astype(jnp.bfloat16)
    return (grad_input, grad_filter)


def solution(mesh):
    placed = (P("ctx", "tp"),) * 5 + (P(None, "tp"),) * 3
    return jax.shard_map(
        per_device,
        mesh=mesh,
        in_specs=placed,
        out_specs=(P("ctx", "tp"), P("ctx", "tp")),
        check_vma=False,
    )
```

```python
import math

import jax
import jax.numpy as jnp
import numpy as np
from jax import lax
from jax.experimental import pallas as pl
from jax.experimental.pallas import tpu as pltpu
from jax.sharding import PartitionSpec as P


def compiler_params(mib):
    return pltpu.CompilerParams(vmem_limit_bytes=int(mib * 1024 * 1024))


def dft_tables(blocks, block_len, scale):
    index = np.arange(block_len)
    angle = 2.0 * np.pi * (np.outer(index, index) % block_len) / block_len
    cos, sin = np.cos(angle), np.sin(angle)
    forward = np.block([[cos, -sin], [sin, cos]])
    inverse = forward.T
    rows = np.arange(blocks + 1)
    phase = 2.0 * np.pi * np.outer(rows, index) / (2 * blocks * block_len)
    weight = np.where((rows == 0) | (rows == blocks), 1.0, 2.0)[:, None] * scale
    twiddle = np.stack(
        [np.cos(phase), np.sin(phase), weight * np.cos(phase), weight * np.sin(phase)]
    )
    return (
        jnp.asarray(forward, jnp.bfloat16),
        jnp.asarray(inverse, jnp.bfloat16),
        jnp.asarray(twiddle, jnp.float32),
    )


def half_spectrum(values):
    size = len(values)
    if size == 1:
        return [(values[0], None), (values[0], None)]
    even, odd = half_spectrum(values[0::2]), half_spectrum(values[1::2])
    half = size // 2
    bins = [None] * (size + 1)
    bins[0] = (even[0][0] + odd[0][0], None)
    bins[size] = (even[0][0] - odd[0][0], None)
    bins[half] = (even[half][0], -odd[half][0])
    for k in range(1, half):
        angle = math.pi * k / size
        cos, sin = math.cos(angle), math.sin(angle)
        even_re, even_im = even[k]
        odd_re, odd_im = odd[k]
        if 2 * k == half:
            turn_re = cos * (odd_re + odd_im)
            turn_im = cos * (odd_im - odd_re)
        else:
            turn_re = cos * odd_re + sin * odd_im
            turn_im = cos * odd_im - sin * odd_re
        bins[k] = (even_re + turn_re, even_im + turn_im)
        bins[size - k] = (even_re - turn_re, turn_im - even_im)
    return bins


def half_spectrum_adjoint(bins):
    size = len(bins) - 1
    if size == 1:
        return [bins[0][0] + bins[1][0]]
    half = size // 2
    even, odd = [None] * (half + 1), [None] * (half + 1)
    even[0] = (bins[0][0] + bins[size][0], None)
    odd[0] = (bins[0][0] - bins[size][0], None)
    even[half] = (bins[half][0], None)
    odd[half] = (-bins[half][1], None)
    for k in range(1, half):
        angle = math.pi * k / size
        cos, sin = math.cos(angle), math.sin(angle)
        low_re, low_im = bins[k]
        high_re, high_im = bins[size - k]
        even[k] = (low_re + high_re, low_im - high_im)
        turn_re, turn_im = low_re - high_re, low_im + high_im
        if 2 * k == half:
            odd[k] = (cos * (turn_re - turn_im), cos * (turn_re + turn_im))
        else:
            odd[k] = (cos * turn_re - sin * turn_im, cos * turn_im + sin * turn_re)
    values = [None] * size
    values[0::2] = half_spectrum_adjoint(even)
    values[1::2] = half_spectrum_adjoint(odd)
    return values


HBM = pl.BlockSpec(memory_space=pltpu.HBM)
VMEM = pl.BlockSpec(memory_space=pltpu.VMEM)


def in_hbm(*arrays):
    return [pltpu.with_memory_space_constraint(array, pltpu.HBM) for array in arrays]


def distances(blocks):
    last = blocks - 1
    return [last - i // 2 if i % 2 == 0 else 1 + i // 2 for i in range(last)] + [0]


def late_steps(blocks):
    far = [step for step, distance in enumerate(distances(blocks)) if 2 * distance >= blocks]
    return far[len(far) // 2 :]


def by_distance(pieces):
    return zip(distances(len(pieces)), pieces)


def fetch(sources, targets, sems):
    copies = [
        pltpu.make_async_copy(source, target, sems.at[i])
        for i, (source, target) in enumerate(zip(sources, targets))
    ]
    for copy in copies:
        copy.start()
    return copies


def gate_kernel(*refs):
    sources, refs = refs[:5], refs[5:]
    out_refs, (turn_ref, held_ref, sems) = refs[:-3], refs[-3:]
    blocks, _, channels, block_len = turn_ref.shape
    filter_copy, *copies = fetch(sources, [held_ref.at[i] for i in range(5)], sems)

    def put(slot, wide):
        turned = wide.T.astype(jnp.bfloat16)
        turn_ref[:, slot] = turned.reshape(blocks, channels, block_len)

    filter_copy.wait()
    put(1, held_ref[0].astype(jnp.float32))
    for copy in copies[:2]:
        copy.wait()
    put(0, held_ref[1].astype(jnp.float32) * held_ref[2].astype(jnp.float32))
    for copy in copies[2:]:
        copy.wait()
    put(2, held_ref[3].astype(jnp.float32) * held_ref[4].astype(jnp.float32))
    me = lax.axis_index("ctx")
    for distance, out_ref in by_distance(out_refs):
        out_ref[...] = turn_ref[me ^ distance]


def conv_kernel(*refs):
    blocks = lax.axis_size("ctx")
    in_refs, sources, refs = refs[:blocks], refs[blocks : blocks + 9], refs[blocks + 9 :]
    late = late_steps(blocks)
    out_refs, late_refs, held_refs = refs[:blocks], refs[blocks : -13], refs[-13:-7]
    in_ref, rows_ref, spec_ref, twid_ref, fwd_ref, inv_ref, sems = refs[-7:]
    twid_copy, fwd_copy, inv_copy, *held_copies = fetch(
        sources, (twid_ref, fwd_ref, inv_ref, *held_refs), sems
    )
    groups, bins_count, signals, chunk, _ = rows_ref.shape
    block_len = in_ref.shape[-1]
    me = lax.axis_index("ctx")
    for distance, ref in by_distance(in_refs):
        in_ref[me ^ distance] = ref[...]
    twid_copy.wait()

    def each(count, body):
        if blocks <= 8:
            for i in range(count):
                body(i)
        else:
            pl.loop(0, count)(body)

    def put(group, k, slot, re, im):
        rows_ref[group, k, slot, :, :block_len] = re.astype(jnp.bfloat16)
        rows_ref[group, k, slot, :, block_len:] = im.astype(jnp.bfloat16)

    def get(group, k, slot):
        return spec_ref[group, k, slot, :, :block_len], spec_ref[group, k, slot, :, block_len:]

    def analyse(group):
        rows = pl.ds(group * chunk, chunk)

        def one(signal):
            bins = half_spectrum(
                [in_ref[p, signal, rows, :].astype(jnp.float32) for p in range(blocks)]
            )
            for k, (re, im) in enumerate(bins):
                cos, sin = twid_ref[0, k : k + 1, :], twid_ref[1, k : k + 1, :]
                if k == 0:
                    put(group, k, signal, re, jnp.zeros_like(re))
                elif im is None:
                    put(group, k, signal, re * cos, -(re * sin))
                else:
                    put(group, k, signal, re * cos + im * sin, im * cos - re * sin)

        each(signals, one)

    def transform(group, table_ref):
        spec_ref[group] = jnp.dot(
            rows_ref[group].reshape(bins_count * signals * chunk, 2 * block_len),
            table_ref[...],
            preferred_element_type=jnp.float32,
        ).reshape(spec_ref.shape[1:])

    def forward(group):
        if group == 0:
            fwd_copy.wait()
        transform(group, fwd_ref)

    def combine(group):
        def one(k):
            prod_re, prod_im = get(group, k, 0)
            kern_re, kern_im = get(group, k, 1)
            grad_re, grad_im = get(group, k, 2)
            conv_re = prod_re * kern_re - prod_im * kern_im
            conv_im = prod_re * kern_im + prod_im * kern_re
            back_re = grad_re * kern_re + grad_im * kern_im
            back_im = grad_im * kern_re - grad_re * kern_im
            filt_re = grad_re * prod_re + grad_im * prod_im
            filt_im = grad_im * prod_re - grad_re * prod_im
            put(group, k, 0, conv_re, conv_im)
            put(group, k, 1, back_re, back_im)
            put(group, k, 2, filt_re, filt_im)

        each(bins_count, one)

    def inverse(group):
        if group == 0:
            inv_copy.wait()
        transform(group, inv_ref)

    def synthesise(group):
        rows = pl.ds(group * chunk, chunk)

        def one(signal):
            bins = []
            for k in range(bins_count):
                re, im = get(group, k, signal)
                cos, sin = twid_ref[2, k : k + 1, :], twid_ref[3, k : k + 1, :]
                if k == 0:
                    bins.append((re * cos, None))
                elif k == blocks:
                    bins.append((re * cos - im * sin, None))
                else:
                    bins.append((re * cos - im * sin, im * cos + re * sin))
            for p, value in enumerate(half_spectrum_adjoint(bins)):
                in_ref[p, signal, rows, :] = value.astype(jnp.bfloat16)

        each(signals, one)

    stages = (analyse, forward, combine, inverse, synthesise)
    for step in range(groups + len(stages) - 1):
        for depth, stage in reversed(list(enumerate(stages))):
            if 0 <= step - depth < groups:
                stage(step - depth)
    for distance, out_ref in by_distance(out_refs):
        out_ref[...] = in_ref[me ^ distance, : out_ref.shape[0]]
    for step, late_ref in zip(late, late_refs):
        late_ref[...] = in_ref[me ^ distances(blocks)[step], 2:]
    for copy in held_copies:
        copy.wait()


def term(lhs_ref, weight_refs, group):
    part = weight_refs[0].shape[0] // lax.axis_size("tp")
    rows = pl.ds(pl.multiple_of(group * part, part), part)
    dims = (((1,), (1,)), ((), ()))
    total = None
    for slot, weight_ref in enumerate(weight_refs):
        piece = lax.dot_general(
            lhs_ref[slot], weight_ref[rows, :], dims, preferred_element_type=jnp.float32
        )
        total = piece if total is None else total + piece
    return total


def natural(back_refs, turn_ref, slots):
    blocks, _, channels, block_len = turn_ref.shape
    me = lax.axis_index("ctx")
    for distance, ref in by_distance(back_refs):
        for i, slot in enumerate(slots):
            turn_ref[me ^ distance, i] = ref[slot % ref.shape[0]]
    return [
        turn_ref[:, i].reshape(blocks * channels, block_len).astype(jnp.float32).T
        for i in range(len(slots))
    ]


def mate_kernel(*refs):
    blocks = lax.axis_size("ctx")
    back_refs, (key_ref, value_ref, grad_ref) = refs[:blocks], refs[blocks : blocks + 3]
    weight_refs = refs[blocks + 3 : blocks + 6]
    lhs_ref, out_ref, turn_ref = refs[blocks + 6 :]
    conv_out, grad_product = natural(back_refs, turn_ref, (0, 1))
    lhs_ref[0] = (grad_product * value_ref[...].astype(jnp.float32)).astype(jnp.bfloat16)
    lhs_ref[1] = (conv_out * grad_ref[...].astype(jnp.float32)).astype(jnp.bfloat16)
    lhs_ref[2] = (grad_product * key_ref[...].astype(jnp.float32)).astype(jnp.bfloat16)
    out_ref[...] = term(lhs_ref, weight_refs, lax.axis_index("tp") ^ 3).astype(jnp.bfloat16)


def far_kernel(lhs_ref, wk_ref, wq_ref, wv_ref, far_ref, near_ref):
    group = lax.axis_index("tp")
    far_ref[...] = term(lhs_ref, (wk_ref, wq_ref, wv_ref), group ^ 2)
    near_ref[...] = term(lhs_ref, (wk_ref, wq_ref, wv_ref), group ^ 1).astype(jnp.bfloat16)


def own_kernel(lhs_ref, wk_ref, wq_ref, wv_ref, own_ref):
    own_ref[...] = term(lhs_ref, (wk_ref, wq_ref, wv_ref), lax.axis_index("tp"))


def turn_kernel(*refs):
    back_refs, (out_ref, turn_ref) = refs[:-2], refs[-2:]
    out_ref[...] = natural(back_refs, turn_ref, (-1,))[0].astype(jnp.bfloat16)


def exchange(block, axis, distance):
    pairs = [(i, i ^ distance) for i in range(lax.axis_size(axis))]
    return lax.ppermute(block, axis, pairs)


def swap(pieces):
    return [
        exchange(piece, "ctx", distance) if distance else piece
        for distance, piece in by_distance(pieces)
    ]


def swap_late(pieces, blocks):
    return [
        exchange(piece, "ctx", distances(blocks)[step])
        for step, piece in zip(late_steps(blocks), pieces)
    ]


def per_device(key_act, value_act, query_act, grad_out, long_filter, w_key, w_query, w_value):
    blocks = lax.axis_size("ctx")
    groups = lax.axis_size("tp")
    block_len, width = key_act.shape
    channels = width // blocks
    chunk = min(channels, 16)
    seq_len = blocks * block_len
    part = w_key.shape[0] // groups
    block_cost = pl.CostEstimate(
        flops=4 * block_len * 3 * width * part, bytes_accessed=1 << 22, transcendentals=0
    )

    def arrays(count, *shape, dtype=jnp.bfloat16):
        return [pltpu.VMEM(shape, dtype)] * count

    sent = pl.pallas_call(
        gate_kernel,
        in_specs=[HBM] * 5,
        out_shape=arrays(blocks, 3, channels, block_len),
        scratch_shapes=[
            pltpu.VMEM((blocks, 3, channels, block_len), jnp.bfloat16),
            pltpu.VMEM((5, block_len, width), jnp.bfloat16),
            pltpu.SemaphoreType.DMA((5,)),
        ],
        compiler_params=compiler_params(12),
        name="gate",
    )(*in_hbm(long_filter, key_act, value_act, query_act, grad_out))
    moved = swap(sent)

    forward, inverse, twiddle = dft_tables(
        blocks, block_len, 1.0 / (math.sqrt(seq_len) * 2 * seq_len)
    )
    tables = (twiddle, forward, inverse)
    held = (key_act, value_act, grad_out, w_key, w_query, w_value)
    late = late_steps(blocks)
    results = pl.pallas_call(
        conv_kernel,
        in_specs=[VMEM] * blocks + [HBM] * 9,
        out_shape=[
            pltpu.VMEM((2 if step in late else 3, channels, block_len), jnp.bfloat16)
            for step in range(blocks)
        ]
        + arrays(len(late), 1, channels, block_len)
        + [pltpu.VMEM(array.shape, array.dtype) for array in held],
        scratch_shapes=[
            pltpu.VMEM((blocks, 3, channels, block_len), jnp.bfloat16),
            pltpu.VMEM((channels // chunk, blocks + 1, 3, chunk, 2 * block_len), jnp.bfloat16),
            pltpu.VMEM((channels // chunk, blocks + 1, 3, chunk, 2 * block_len), jnp.float32),
            *[pltpu.VMEM(array.shape, array.dtype) for array in tables],
            pltpu.SemaphoreType.DMA((9,)),
        ],
        compiler_params=compiler_params(28),
        name="conv",
    )(*moved, *in_hbm(*tables, *held))
    back, late_back, held = swap(results[:blocks]), results[blocks:-6], results[-6:]
    weights = held[3:]
    lhs, to_mate = pl.pallas_call(
        mate_kernel,
        in_specs=[VMEM] * (blocks + 6),
        out_shape=arrays(1, 3, block_len, width) + arrays(1, block_len, part),
        scratch_shapes=[pltpu.VMEM((blocks, 2, channels, block_len), jnp.bfloat16)],
        compiler_params=compiler_params(16),
        cost_estimate=block_cost,
        name="mate",
    )(*back, *held)
    from_mate = exchange(to_mate, "tp", 1)
    far, near = pl.pallas_call(
        far_kernel,
        in_specs=[VMEM] * 4,
        out_shape=arrays(1, block_len, part, dtype=jnp.float32) + arrays(1, block_len, part),
        compiler_params=compiler_params(16),
        cost_estimate=block_cost,
        name="far",
    )(lhs, *weights)
    far = (far + from_mate.astype(jnp.float32)).astype(jnp.bfloat16)
    far, near, lhs, back, late_back = lax.optimization_barrier((far, near, lhs, back, late_back))
    from_far = exchange(far, "tp", 2)
    from_near = exchange(near, "tp", 1)
    own = pl.pallas_call(
        own_kernel,
        in_specs=[VMEM] * 4,
        out_shape=arrays(1, block_len, part, dtype=jnp.float32)[0],
        compiler_params=compiler_params(16),
        cost_estimate=block_cost,
        name="own",
    )(lhs, *weights)
    own, late_back = lax.optimization_barrier((own, late_back))
    for step, piece in zip(late, swap_late(late_back, blocks)):
        back[step] = piece
    grad_filter = pl.pallas_call(
        turn_kernel,
        in_specs=[VMEM] * blocks,
        out_shape=jax.ShapeDtypeStruct((block_len, width), jnp.bfloat16),
        scratch_shapes=[pltpu.VMEM((blocks, 1, channels, block_len), jnp.bfloat16)],
        compiler_params=compiler_params(16),
        cost_estimate=block_cost,
        name="turn",
    )(*back)
    total = from_far.astype(jnp.float32) + from_near.astype(jnp.float32) + own
    grad_input = total.astype(jnp.bfloat16)
    return (grad_input, grad_filter)


def solution(mesh):
    placed = (P("ctx", "tp"),) * 5 + (P(None, "tp"),) * 3
    return jax.shard_map(
        per_device,
        mesh=mesh,
        in_specs=placed,
        out_specs=(P("ctx", "tp"), P("ctx", "tp")),
        check_vma=False,
    )
```

```python
import math

import jax
import jax.numpy as jnp
import numpy as np
from jax import lax
from jax.experimental import pallas as pl
from jax.experimental.pallas import tpu as pltpu
from jax.sharding import PartitionSpec as P


def compiler_params(mib):
    return pltpu.CompilerParams(vmem_limit_bytes=int(mib * 1024 * 1024))


def dft_tables(blocks, block_len, scale):
    index = np.arange(block_len)
    angle = 2.0 * np.pi * (np.outer(index, index) % block_len) / block_len
    cos, sin = np.cos(angle), np.sin(angle)
    forward = np.block([[cos, -sin], [sin, cos]])
    inverse = forward.T
    rows = np.arange(blocks + 1)
    phase = 2.0 * np.pi * np.outer(rows, index) / (2 * blocks * block_len)
    weight = np.where((rows == 0) | (rows == blocks), 1.0, 2.0)[:, None] * scale
    twiddle = np.stack(
        [np.cos(phase), np.sin(phase), weight * np.cos(phase), weight * np.sin(phase)]
    )
    return (
        jnp.asarray(forward, jnp.bfloat16),
        jnp.asarray(inverse, jnp.bfloat16),
        jnp.asarray(twiddle, jnp.float32),
    )


def half_spectrum(values):
    size = len(values)
    if size == 1:
        return [(values[0], None), (values[0], None)]
    even, odd = half_spectrum(values[0::2]), half_spectrum(values[1::2])
    half = size // 2
    bins = [None] * (size + 1)
    bins[0] = (even[0][0] + odd[0][0], None)
    bins[size] = (even[0][0] - odd[0][0], None)
    bins[half] = (even[half][0], -odd[half][0])
    for k in range(1, half):
        angle = math.pi * k / size
        cos, sin = math.cos(angle), math.sin(angle)
        even_re, even_im = even[k]
        odd_re, odd_im = odd[k]
        if 2 * k == half:
            turn_re = cos * (odd_re + odd_im)
            turn_im = cos * (odd_im - odd_re)
        else:
            turn_re = cos * odd_re + sin * odd_im
            turn_im = cos * odd_im - sin * odd_re
        bins[k] = (even_re + turn_re, even_im + turn_im)
        bins[size - k] = (even_re - turn_re, turn_im - even_im)
    return bins


def half_spectrum_adjoint(bins):
    size = len(bins) - 1
    if size == 1:
        return [bins[0][0] + bins[1][0]]
    half = size // 2
    even, odd = [None] * (half + 1), [None] * (half + 1)
    even[0] = (bins[0][0] + bins[size][0], None)
    odd[0] = (bins[0][0] - bins[size][0], None)
    even[half] = (bins[half][0], None)
    odd[half] = (-bins[half][1], None)
    for k in range(1, half):
        angle = math.pi * k / size
        cos, sin = math.cos(angle), math.sin(angle)
        low_re, low_im = bins[k]
        high_re, high_im = bins[size - k]
        even[k] = (low_re + high_re, low_im - high_im)
        turn_re, turn_im = low_re - high_re, low_im + high_im
        if 2 * k == half:
            odd[k] = (cos * (turn_re - turn_im), cos * (turn_re + turn_im))
        else:
            odd[k] = (cos * turn_re - sin * turn_im, cos * turn_im + sin * turn_re)
    values = [None] * size
    values[0::2] = half_spectrum_adjoint(even)
    values[1::2] = half_spectrum_adjoint(odd)
    return values


HBM = pl.BlockSpec(memory_space=pltpu.HBM)
VMEM = pl.BlockSpec(memory_space=pltpu.VMEM)


def in_hbm(*arrays):
    return [pltpu.with_memory_space_constraint(array, pltpu.HBM) for array in arrays]


def distances(blocks):
    last = blocks - 1
    return [last - i // 2 if i % 2 == 0 else 1 + i // 2 for i in range(last)] + [0]


def late_steps(blocks):
    far = [step for step, distance in enumerate(distances(blocks)) if 2 * distance >= blocks]
    return far[: len(far) // 2]


def by_distance(pieces):
    return zip(distances(len(pieces)), pieces)


def fetch(sources, targets, sems):
    copies = [
        pltpu.make_async_copy(source, target, sems.at[i])
        for i, (source, target) in enumerate(zip(sources, targets))
    ]
    for copy in copies:
        copy.start()
    return copies


def gate_kernel(*refs):
    sources, refs = refs[:5], refs[5:]
    out_refs, (turn_ref, held_ref, sems) = refs[:-3], refs[-3:]
    blocks, _, channels, block_len = turn_ref.shape
    filter_copy, *copies = fetch(sources, [held_ref.at[i] for i in range(5)], sems)

    def put(slot, wide):
        turned = wide.T.astype(jnp.bfloat16)
        turn_ref[:, slot] = turned.reshape(blocks, channels, block_len)

    filter_copy.wait()
    put(1, held_ref[0].astype(jnp.float32))
    for copy in copies[:2]:
        copy.wait()
    put(0, held_ref[1].astype(jnp.float32) * held_ref[2].astype(jnp.float32))
    for copy in copies[2:]:
        copy.wait()
    put(2, held_ref[3].astype(jnp.float32) * held_ref[4].astype(jnp.float32))
    me = lax.axis_index("ctx")
    for distance, out_ref in by_distance(out_refs):
        out_ref[...] = turn_ref[me ^ distance]


def conv_kernel(*refs):
    blocks = lax.axis_size("ctx")
    in_refs, sources, refs = refs[:blocks], refs[blocks : blocks + 9], refs[blocks + 9 :]
    late = late_steps(blocks)
    out_refs, late_refs, held_refs = refs[:blocks], refs[blocks : -13], refs[-13:-7]
    in_ref, rows_ref, spec_ref, twid_ref, fwd_ref, inv_ref, sems = refs[-7:]
    twid_copy, fwd_copy, inv_copy, *held_copies = fetch(
        sources, (twid_ref, fwd_ref, inv_ref, *held_refs), sems
    )
    groups, bins_count, signals, chunk, _ = rows_ref.shape
    block_len = in_ref.shape[-1]
    me = lax.axis_index("ctx")
    for distance, ref in by_distance(in_refs):
        in_ref[me ^ distance] = ref[...]
    twid_copy.wait()

    def each(count, body):
        if blocks <= 8:
            for i in range(count):
                body(i)
        else:
            pl.loop(0, count)(body)

    def put(group, k, slot, re, im):
        rows_ref[group, k, slot, :, :block_len] = re.astype(jnp.bfloat16)
        rows_ref[group, k, slot, :, block_len:] = im.astype(jnp.bfloat16)

    def get(group, k, slot):
        return spec_ref[group, k, slot, :, :block_len], spec_ref[group, k, slot, :, block_len:]

    def analyse(group):
        rows = pl.ds(group * chunk, chunk)

        def one(signal):
            bins = half_spectrum(
                [in_ref[p, signal, rows, :].astype(jnp.float32) for p in range(blocks)]
            )
            for k, (re, im) in enumerate(bins):
                cos, sin = twid_ref[0, k : k + 1, :], twid_ref[1, k : k + 1, :]
                if k == 0:
                    put(group, k, signal, re, jnp.zeros_like(re))
                elif im is None:
                    put(group, k, signal, re * cos, -(re * sin))
                else:
                    put(group, k, signal, re * cos + im * sin, im * cos - re * sin)

        each(signals, one)

    def transform(group, table_ref):
        spec_ref[group] = jnp.dot(
            rows_ref[group].reshape(bins_count * signals * chunk, 2 * block_len),
            table_ref[...],
            preferred_element_type=jnp.float32,
        ).reshape(spec_ref.shape[1:])

    def forward(group):
        if group == 0:
            fwd_copy.wait()
        transform(group, fwd_ref)

    def combine(group):
        def one(k):
            prod_re, prod_im = get(group, k, 0)
            kern_re, kern_im = get(group, k, 1)
            grad_re, grad_im = get(group, k, 2)
            conv_re = prod_re * kern_re - prod_im * kern_im
            conv_im = prod_re * kern_im + prod_im * kern_re
            back_re = grad_re * kern_re + grad_im * kern_im
            back_im = grad_im * kern_re - grad_re * kern_im
            filt_re = grad_re * prod_re + grad_im * prod_im
            filt_im = grad_im * prod_re - grad_re * prod_im
            put(group, k, 0, conv_re, conv_im)
            put(group, k, 1, back_re, back_im)
            put(group, k, 2, filt_re, filt_im)

        each(bins_count, one)

    def inverse(group):
        if group == 0:
            inv_copy.wait()
        transform(group, inv_ref)

    def synthesise(group):
        rows = pl.ds(group * chunk, chunk)

        def one(signal):
            bins = []
            for k in range(bins_count):
                re, im = get(group, k, signal)
                cos, sin = twid_ref[2, k : k + 1, :], twid_ref[3, k : k + 1, :]
                if k == 0:
                    bins.append((re * cos, None))
                elif k == blocks:
                    bins.append((re * cos - im * sin, None))
                else:
                    bins.append((re * cos - im * sin, im * cos + re * sin))
            for p, value in enumerate(half_spectrum_adjoint(bins)):
                in_ref[p, signal, rows, :] = value.astype(jnp.bfloat16)

        each(signals, one)

    stages = (analyse, forward, combine, inverse, synthesise)
    for step in range(groups + len(stages) - 1):
        for depth, stage in reversed(list(enumerate(stages))):
            if 0 <= step - depth < groups:
                stage(step - depth)
    for distance, out_ref in by_distance(out_refs):
        out_ref[...] = in_ref[me ^ distance, : out_ref.shape[0]]
    for step, late_ref in zip(late, late_refs):
        late_ref[...] = in_ref[me ^ distances(blocks)[step], 2:]
    for copy in held_copies:
        copy.wait()


def term(lhs_ref, weight_refs, group):
    part = weight_refs[0].shape[0] // lax.axis_size("tp")
    rows = pl.ds(pl.multiple_of(group * part, part), part)
    dims = (((1,), (1,)), ((), ()))
    total = None
    for slot, weight_ref in enumerate(weight_refs):
        piece = lax.dot_general(
            lhs_ref[slot], weight_ref[rows, :], dims, preferred_element_type=jnp.float32
        )
        total = piece if total is None else total + piece
    return total


def natural(back_refs, turn_ref, slots):
    blocks, _, channels, block_len = turn_ref.shape
    me = lax.axis_index("ctx")
    for distance, ref in by_distance(back_refs):
        for i, slot in enumerate(slots):
            turn_ref[me ^ distance, i] = ref[slot % ref.shape[0]]
    return [
        turn_ref[:, i].reshape(blocks * channels, block_len).astype(jnp.float32).T
        for i in range(len(slots))
    ]


def mate_kernel(*refs):
    blocks = lax.axis_size("ctx")
    back_refs, (key_ref, value_ref, grad_ref) = refs[:blocks], refs[blocks : blocks + 3]
    weight_refs = refs[blocks + 3 : blocks + 6]
    lhs_ref, out_ref, turn_ref = refs[blocks + 6 :]
    conv_out, grad_product = natural(back_refs, turn_ref, (0, 1))
    lhs_ref[0] = (grad_product * value_ref[...].astype(jnp.float32)).astype(jnp.bfloat16)
    lhs_ref[1] = (conv_out * grad_ref[...].astype(jnp.float32)).astype(jnp.bfloat16)
    lhs_ref[2] = (grad_product * key_ref[...].astype(jnp.float32)).astype(jnp.bfloat16)
    out_ref[...] = term(lhs_ref, weight_refs, lax.axis_index("tp") ^ 3).astype(jnp.bfloat16)


def far_kernel(lhs_ref, wk_ref, wq_ref, wv_ref, far_ref, near_ref):
    group = lax.axis_index("tp")
    far_ref[...] = term(lhs_ref, (wk_ref, wq_ref, wv_ref), group ^ 2)
    near_ref[...] = term(lhs_ref, (wk_ref, wq_ref, wv_ref), group ^ 1).astype(jnp.bfloat16)


def own_kernel(lhs_ref, wk_ref, wq_ref, wv_ref, own_ref):
    own_ref[...] = term(lhs_ref, (wk_ref, wq_ref, wv_ref), lax.axis_index("tp"))


def turn_kernel(*refs):
    blocks = lax.axis_size("ctx")
    back_refs, late_refs, (out_ref, turn_ref) = list(refs[:blocks]), refs[blocks:-2], refs[-2:]
    for step, ref in zip(late_steps(blocks), late_refs):
        back_refs[step] = ref
    out_ref[...] = natural(back_refs, turn_ref, (-1,))[0].astype(jnp.bfloat16)


def exchange(block, axis, distance):
    pairs = [(i, i ^ distance) for i in range(lax.axis_size(axis))]
    return lax.ppermute(block, axis, pairs)


def swap(pieces):
    return [
        exchange(piece, "ctx", distance) if distance else piece
        for distance, piece in by_distance(pieces)
    ]


def swap_late(pieces, blocks):
    return [
        exchange(piece, "ctx", distances(blocks)[step])
        for step, piece in zip(late_steps(blocks), pieces)
    ]


def per_device(key_act, value_act, query_act, grad_out, long_filter, w_key, w_query, w_value):
    blocks = lax.axis_size("ctx")
    groups = lax.axis_size("tp")
    block_len, width = key_act.shape
    channels = width // blocks
    chunk = min(channels, 16)
    seq_len = blocks * block_len
    part = w_key.shape[0] // groups
    block_cost = pl.CostEstimate(
        flops=4 * block_len * 3 * width * part, bytes_accessed=1 << 22, transcendentals=0
    )

    def arrays(count, *shape, dtype=jnp.bfloat16):
        return [pltpu.VMEM(shape, dtype)] * count

    sent = pl.pallas_call(
        gate_kernel,
        in_specs=[HBM] * 5,
        out_shape=arrays(blocks, 3, channels, block_len),
        scratch_shapes=[
            pltpu.VMEM((blocks, 3, channels, block_len), jnp.bfloat16),
            pltpu.VMEM((5, block_len, width), jnp.bfloat16),
            pltpu.SemaphoreType.DMA((5,)),
        ],
        compiler_params=compiler_params(12),
        name="gate",
    )(*in_hbm(long_filter, key_act, value_act, query_act, grad_out))
    moved = swap(sent)

    forward, inverse, twiddle = dft_tables(
        blocks, block_len, 1.0 / (math.sqrt(seq_len) * 2 * seq_len)
    )
    tables = (twiddle, forward, inverse)
    held = (key_act, value_act, grad_out, w_key, w_query, w_value)
    late = late_steps(blocks)
    results = pl.pallas_call(
        conv_kernel,
        in_specs=[VMEM] * blocks + [HBM] * 9,
        out_shape=[
            pltpu.VMEM((2 if step in late else 3, channels, block_len), jnp.bfloat16)
            for step in range(blocks)
        ]
        + arrays(len(late), 1, channels, block_len)
        + [pltpu.VMEM(array.shape, array.dtype) for array in held],
        scratch_shapes=[
            pltpu.VMEM((blocks, 3, channels, block_len), jnp.bfloat16),
            pltpu.VMEM((channels // chunk, blocks + 1, 3, chunk, 2 * block_len), jnp.bfloat16),
            pltpu.VMEM((channels // chunk, blocks + 1, 3, chunk, 2 * block_len), jnp.float32),
            *[pltpu.VMEM(array.shape, array.dtype) for array in tables],
            pltpu.SemaphoreType.DMA((9,)),
        ],
        compiler_params=compiler_params(28),
        name="conv",
    )(*moved, *in_hbm(*tables, *held))
    back, late_back, held = swap(results[:blocks]), results[blocks:-6], results[-6:]
    weights = held[3:]
    lhs, to_mate = pl.pallas_call(
        mate_kernel,
        in_specs=[VMEM] * (blocks + 6),
        out_shape=arrays(1, 3, block_len, width) + arrays(1, block_len, part),
        scratch_shapes=[pltpu.VMEM((blocks, 2, channels, block_len), jnp.bfloat16)],
        compiler_params=compiler_params(16),
        cost_estimate=block_cost,
        name="mate",
    )(*back, *held)
    from_mate = exchange(to_mate, "tp", 1)
    far, near = pl.pallas_call(
        far_kernel,
        in_specs=[VMEM] * 4,
        out_shape=arrays(1, block_len, part, dtype=jnp.float32) + arrays(1, block_len, part),
        compiler_params=compiler_params(16),
        cost_estimate=block_cost,
        name="far",
    )(lhs, *weights)
    far = (far + from_mate.astype(jnp.float32)).astype(jnp.bfloat16)
    far, near, lhs, late_back = lax.optimization_barrier((far, near, lhs, late_back))
    from_far = exchange(far, "tp", 2)
    from_near = exchange(near, "tp", 1)
    own = pl.pallas_call(
        own_kernel,
        in_specs=[VMEM] * 4,
        out_shape=arrays(1, block_len, part, dtype=jnp.float32)[0],
        compiler_params=compiler_params(16),
        cost_estimate=block_cost,
        name="own",
    )(lhs, *weights)
    own, late_back = lax.optimization_barrier((own, late_back))
    grad_filter = pl.pallas_call(
        turn_kernel,
        in_specs=[VMEM] * (blocks + len(late)),
        out_shape=jax.ShapeDtypeStruct((block_len, width), jnp.bfloat16),
        scratch_shapes=[pltpu.VMEM((blocks, 1, channels, block_len), jnp.bfloat16)],
        compiler_params=compiler_params(16),
        cost_estimate=block_cost,
        name="turn",
    )(*back, *swap_late(late_back, blocks))
    total = from_far.astype(jnp.float32) + from_near.astype(jnp.float32) + own
    grad_input = total.astype(jnp.bfloat16)
    return (grad_input, grad_filter)


def solution(mesh):
    placed = (P("ctx", "tp"),) * 5 + (P(None, "tp"),) * 3
    return jax.shard_map(
        per_device,
        mesh=mesh,
        in_specs=placed,
        out_specs=(P("ctx", "tp"), P("ctx", "tp")),
        check_vma=False,
    )
```

```python
import math

import jax
import jax.numpy as jnp
import numpy as np
from jax import lax
from jax.experimental import pallas as pl
from jax.experimental.pallas import tpu as pltpu
from jax.sharding import PartitionSpec as P


def compiler_params(mib):
    return pltpu.CompilerParams(vmem_limit_bytes=int(mib * 1024 * 1024))


def dft_tables(blocks, block_len, scale):
    index = np.arange(block_len)
    angle = 2.0 * np.pi * (np.outer(index, index) % block_len) / block_len
    cos, sin = np.cos(angle), np.sin(angle)
    forward = np.block([[cos, -sin], [sin, cos]])
    inverse = forward.T
    rows = np.arange(blocks + 1)
    phase = 2.0 * np.pi * np.outer(rows, index) / (2 * blocks * block_len)
    weight = np.where((rows == 0) | (rows == blocks), 1.0, 2.0)[:, None] * scale
    twiddle = np.stack(
        [np.cos(phase), np.sin(phase), weight * np.cos(phase), weight * np.sin(phase)]
    )
    return (
        jnp.asarray(forward, jnp.bfloat16),
        jnp.asarray(inverse, jnp.bfloat16),
        jnp.asarray(twiddle, jnp.float32),
    )


def half_spectrum(values):
    size = len(values)
    if size == 1:
        return [(values[0], None), (values[0], None)]
    even, odd = half_spectrum(values[0::2]), half_spectrum(values[1::2])
    half = size // 2
    bins = [None] * (size + 1)
    bins[0] = (even[0][0] + odd[0][0], None)
    bins[size] = (even[0][0] - odd[0][0], None)
    bins[half] = (even[half][0], -odd[half][0])
    for k in range(1, half):
        angle = math.pi * k / size
        cos, sin = math.cos(angle), math.sin(angle)
        even_re, even_im = even[k]
        odd_re, odd_im = odd[k]
        if 2 * k == half:
            turn_re = cos * (odd_re + odd_im)
            turn_im = cos * (odd_im - odd_re)
        else:
            turn_re = cos * odd_re + sin * odd_im
            turn_im = cos * odd_im - sin * odd_re
        bins[k] = (even_re + turn_re, even_im + turn_im)
        bins[size - k] = (even_re - turn_re, turn_im - even_im)
    return bins


def half_spectrum_adjoint(bins):
    size = len(bins) - 1
    if size == 1:
        return [bins[0][0] + bins[1][0]]
    half = size // 2
    even, odd = [None] * (half + 1), [None] * (half + 1)
    even[0] = (bins[0][0] + bins[size][0], None)
    odd[0] = (bins[0][0] - bins[size][0], None)
    even[half] = (bins[half][0], None)
    odd[half] = (-bins[half][1], None)
    for k in range(1, half):
        angle = math.pi * k / size
        cos, sin = math.cos(angle), math.sin(angle)
        low_re, low_im = bins[k]
        high_re, high_im = bins[size - k]
        even[k] = (low_re + high_re, low_im - high_im)
        turn_re, turn_im = low_re - high_re, low_im + high_im
        if 2 * k == half:
            odd[k] = (cos * (turn_re - turn_im), cos * (turn_re + turn_im))
        else:
            odd[k] = (cos * turn_re - sin * turn_im, cos * turn_im + sin * turn_re)
    values = [None] * size
    values[0::2] = half_spectrum_adjoint(even)
    values[1::2] = half_spectrum_adjoint(odd)
    return values


HBM = pl.BlockSpec(memory_space=pltpu.HBM)
VMEM = pl.BlockSpec(memory_space=pltpu.VMEM)


def in_hbm(*arrays):
    return [pltpu.with_memory_space_constraint(array, pltpu.HBM) for array in arrays]


def out_distances(blocks):
    far, near = range(blocks - 1, blocks // 2 - 1, -1), range(1, blocks // 2)
    return [*near, *far, 0], [*far, *reversed(near), 0]


def back_distances(blocks):
    last = blocks - 1
    order = [last - i // 2 if i % 2 == 0 else 1 + i // 2 for i in range(last)] + [0]
    return order, order


def by_distance(pieces, orders):
    even, odd = orders(len(pieces))
    core = lax.axis_index("tp") % 2
    return [
        (a if a == b else a + core * (b - a), piece) for a, b, piece in zip(even, odd, pieces)
    ]


def fetch(sources, targets, sems):
    copies = [
        pltpu.make_async_copy(source, target, sems.at[i])
        for i, (source, target) in enumerate(zip(sources, targets))
    ]
    for copy in copies:
        copy.start()
    return copies


def gate_kernel(*refs):
    sources, refs = refs[:5], refs[5:]
    out_refs, (turn_ref, held_ref, sems) = refs[:-3], refs[-3:]
    blocks, _, channels, block_len = turn_ref.shape
    filter_copy, *copies = fetch(sources, [held_ref.at[i] for i in range(5)], sems)

    def put(slot, wide):
        turned = wide.T.astype(jnp.bfloat16)
        turn_ref[:, slot] = turned.reshape(blocks, channels, block_len)

    filter_copy.wait()
    put(1, held_ref[0].astype(jnp.float32))
    for copy in copies[:2]:
        copy.wait()
    put(0, held_ref[1].astype(jnp.float32) * held_ref[2].astype(jnp.float32))
    for copy in copies[2:]:
        copy.wait()
    put(2, held_ref[3].astype(jnp.float32) * held_ref[4].astype(jnp.float32))
    me = lax.axis_index("ctx")
    for distance, out_ref in by_distance(out_refs, out_distances):
        out_ref[...] = turn_ref[me ^ distance]


def conv_kernel(*refs):
    blocks = lax.axis_size("ctx")
    in_refs, sources, refs = refs[:blocks], refs[blocks + 1 : blocks + 10], refs[blocks + 10 :]
    out_refs, held_refs = refs[:blocks], refs[blocks : blocks + 6]
    in_ref, rows_ref, spec_ref, twid_ref, fwd_ref, inv_ref, sems = refs[blocks + 6 :]
    twid_copy, fwd_copy, inv_copy, *held_copies = fetch(
        sources, (twid_ref, fwd_ref, inv_ref, *held_refs), sems
    )
    groups, bins_count, signals, chunk, _ = rows_ref.shape
    block_len = in_ref.shape[-1]
    me = lax.axis_index("ctx")
    for distance, ref in by_distance(in_refs, out_distances):
        in_ref[me ^ distance] = ref[...]
    twid_copy.wait()

    def each(count, body):
        if blocks <= 8:
            for i in range(count):
                body(i)
        else:
            pl.loop(0, count)(body)

    def put(group, k, slot, re, im):
        rows_ref[group, k, slot, :, :block_len] = re.astype(jnp.bfloat16)
        rows_ref[group, k, slot, :, block_len:] = im.astype(jnp.bfloat16)

    def get(group, k, slot):
        return spec_ref[group, k, slot, :, :block_len], spec_ref[group, k, slot, :, block_len:]

    def analyse(group):
        rows = pl.ds(group * chunk, chunk)

        def one(signal):
            bins = half_spectrum(
                [in_ref[p, signal, rows, :].astype(jnp.float32) for p in range(blocks)]
            )
            for k, (re, im) in enumerate(bins):
                cos, sin = twid_ref[0, k : k + 1, :], twid_ref[1, k : k + 1, :]
                if k == 0:
                    put(group, k, signal, re, jnp.zeros_like(re))
                elif im is None:
                    put(group, k, signal, re * cos, -(re * sin))
                else:
                    put(group, k, signal, re * cos + im * sin, im * cos - re * sin)

        each(signals, one)

    def transform(group, table_ref):
        spec_ref[group] = jnp.dot(
            rows_ref[group].reshape(bins_count * signals * chunk, 2 * block_len),
            table_ref[...],
            preferred_element_type=jnp.float32,
        ).reshape(spec_ref.shape[1:])

    def forward(group):
        if group == 0:
            fwd_copy.wait()
        transform(group, fwd_ref)

    def combine(group):
        def one(k):
            prod_re, prod_im = get(group, k, 0)
            kern_re, kern_im = get(group, k, 1)
            grad_re, grad_im = get(group, k, 2)
            conv_re = prod_re * kern_re - prod_im * kern_im
            conv_im = prod_re * kern_im + prod_im * kern_re
            back_re = grad_re * kern_re + grad_im * kern_im
            back_im = grad_im * kern_re - grad_re * kern_im
            filt_re = grad_re * prod_re + grad_im * prod_im
            filt_im = grad_im * prod_re - grad_re * prod_im
            put(group, k, 0, conv_re, conv_im)
            put(group, k, 1, back_re, back_im)
            put(group, k, 2, filt_re, filt_im)

        each(bins_count, one)

    def inverse(group):
        if group == 0:
            inv_copy.wait()
        transform(group, inv_ref)

    def synthesise(group):
        rows = pl.ds(group * chunk, chunk)

        def one(signal):
            bins = []
            for k in range(bins_count):
                re, im = get(group, k, signal)
                cos, sin = twid_ref[2, k : k + 1, :], twid_ref[3, k : k + 1, :]
                if k == 0:
                    bins.append((re * cos, None))
                elif k == blocks:
                    bins.append((re * cos - im * sin, None))
                else:
                    bins.append((re * cos - im * sin, im * cos + re * sin))
            for p, value in enumerate(half_spectrum_adjoint(bins)):
                in_ref[p, signal, rows, :] = value.astype(jnp.bfloat16)

        each(signals, one)

    stages = (analyse, forward, combine, inverse, synthesise)
    for step in range(groups + len(stages) - 1):
        for depth, stage in reversed(list(enumerate(stages))):
            if 0 <= step - depth < groups:
                stage(step - depth)
    for distance, out_ref in by_distance(out_refs, back_distances):
        out_ref[...] = in_ref[me ^ distance]
    for copy in held_copies:
        copy.wait()


def term(lhs_ref, weight_refs, group):
    part = weight_refs[0].shape[0] // lax.axis_size("tp")
    rows = pl.ds(pl.multiple_of(group * part, part), part)
    dims = (((1,), (1,)), ((), ()))
    total = None
    for slot, weight_ref in enumerate(weight_refs):
        piece = lax.dot_general(
            lhs_ref[slot], weight_ref[rows, :], dims, preferred_element_type=jnp.float32
        )
        total = piece if total is None else total + piece
    return total


def natural(back_refs, turn_ref, slots):
    blocks, _, channels, block_len = turn_ref.shape
    me = lax.axis_index("ctx")
    for distance, ref in by_distance(back_refs, back_distances):
        for i, slot in enumerate(slots):
            turn_ref[me ^ distance, i] = ref[slot]
    return [
        turn_ref[:, i].reshape(blocks * channels, block_len).astype(jnp.float32).T
        for i in range(len(slots))
    ]


def mate_kernel(*refs):
    blocks = lax.axis_size("ctx")
    back_refs, (key_ref, value_ref, grad_ref) = refs[:blocks], refs[blocks : blocks + 3]
    weight_refs = refs[blocks + 3 : blocks + 6]
    lhs_ref, out_ref, turn_ref = refs[blocks + 6 :]
    conv_out, grad_product = natural(back_refs, turn_ref, (0, 1))
    lhs_ref[0] = (grad_product * value_ref[...].astype(jnp.float32)).astype(jnp.bfloat16)
    lhs_ref[1] = (conv_out * grad_ref[...].astype(jnp.float32)).astype(jnp.bfloat16)
    lhs_ref[2] = (grad_product * key_ref[...].astype(jnp.float32)).astype(jnp.bfloat16)
    out_ref[...] = term(lhs_ref, weight_refs, lax.axis_index("tp") ^ 3).astype(jnp.bfloat16)


def far_kernel(lhs_ref, wk_ref, wq_ref, wv_ref, far_ref, near_ref):
    group = lax.axis_index("tp")
    far_ref[...] = term(lhs_ref, (wk_ref, wq_ref, wv_ref), group ^ 2)
    near_ref[...] = term(lhs_ref, (wk_ref, wq_ref, wv_ref), group ^ 1).astype(jnp.bfloat16)


def own_kernel(lhs_ref, wk_ref, wq_ref, wv_ref, own_ref):
    own_ref[...] = term(lhs_ref, (wk_ref, wq_ref, wv_ref), lax.axis_index("tp"))


def turn_kernel(*refs):
    back_refs, (out_ref, turn_ref) = refs[:-2], refs[-2:]
    out_ref[...] = natural(back_refs, turn_ref, (2,))[0].astype(jnp.bfloat16)


def exchange(block, axis, distance):
    pairs = [(i, i ^ distance) for i in range(lax.axis_size(axis))]
    return lax.ppermute(block, axis, pairs)


def send(piece, step, orders):
    blocks, groups = lax.axis_size("ctx"), lax.axis_size("tp")
    chosen = orders(blocks)
    pairs = [
        (i * groups + j, (i ^ chosen[j % 2][step]) * groups + j)
        for i in range(blocks)
        for j in range(groups)
    ]
    return lax.ppermute(piece, ("ctx", "tp"), pairs)


def swap_out(pieces):
    near = len(pieces) // 2 - 1
    moved = [send(piece, step, out_distances) for step, piece in enumerate(pieces[:near])]
    pairs = [(j, j - 1) for j in range(1, lax.axis_size("tp"), 2)]
    token = lax.ppermute((moved or pieces)[0][:1, :16, :128], "tp", pairs)
    *pieces, token = lax.optimization_barrier((*pieces, token))
    for step, piece in enumerate(pieces[near:-1], near):
        moved.append(send(piece, step, out_distances))
    return [*moved, pieces[-1]], token


def swap_back(pieces):
    moved = [send(piece, step, back_distances) for step, piece in enumerate(pieces[:-1])]
    return [*moved, pieces[-1]]


def per_device(key_act, value_act, query_act, grad_out, long_filter, w_key, w_query, w_value):
    blocks = lax.axis_size("ctx")
    groups = lax.axis_size("tp")
    block_len, width = key_act.shape
    channels = width // blocks
    chunk = min(channels, 16)
    seq_len = blocks * block_len
    part = w_key.shape[0] // groups
    block_cost = pl.CostEstimate(
        flops=4 * block_len * 3 * width * part, bytes_accessed=1 << 22, transcendentals=0
    )

    def arrays(count, *shape, dtype=jnp.bfloat16):
        return [pltpu.VMEM(shape, dtype)] * count

    sent = pl.pallas_call(
        gate_kernel,
        in_specs=[HBM] * 5,
        out_shape=arrays(blocks, 3, channels, block_len),
        scratch_shapes=[
            pltpu.VMEM((blocks, 3, channels, block_len), jnp.bfloat16),
            pltpu.VMEM((5, block_len, width), jnp.bfloat16),
            pltpu.SemaphoreType.DMA((5,)),
        ],
        compiler_params=compiler_params(12),
        name="gate",
    )(*in_hbm(long_filter, key_act, value_act, query_act, grad_out))
    moved, token = swap_out(sent)

    forward, inverse, twiddle = dft_tables(
        blocks, block_len, 1.0 / (math.sqrt(seq_len) * 2 * seq_len)
    )
    tables = (twiddle, forward, inverse)
    held = (key_act, value_act, grad_out, w_key, w_query, w_value)
    results = pl.pallas_call(
        conv_kernel,
        in_specs=[VMEM] * (blocks + 1) + [HBM] * 9,
        out_shape=arrays(blocks, 3, channels, block_len)
        + [pltpu.VMEM(array.shape, array.dtype) for array in held],
        scratch_shapes=[
            pltpu.VMEM((blocks, 3, channels, block_len), jnp.bfloat16),
            pltpu.VMEM((channels // chunk, blocks + 1, 3, chunk, 2 * block_len), jnp.bfloat16),
            pltpu.VMEM((channels // chunk, blocks + 1, 3, chunk, 2 * block_len), jnp.float32),
            *[pltpu.VMEM(array.shape, array.dtype) for array in tables],
            pltpu.SemaphoreType.DMA((9,)),
        ],
        compiler_params=compiler_params(28),
        name="conv",
    )(*moved, token, *in_hbm(*tables, *held))
    back, held = swap_back(results[:blocks]), results[blocks:]
    weights = held[3:]
    lhs, to_mate = pl.pallas_call(
        mate_kernel,
        in_specs=[VMEM] * (blocks + 6),
        out_shape=arrays(1, 3, block_len, width) + arrays(1, block_len, part),
        scratch_shapes=[pltpu.VMEM((blocks, 2, channels, block_len), jnp.bfloat16)],
        compiler_params=compiler_params(16),
        cost_estimate=block_cost,
        name="mate",
    )(*back, *held)
    from_mate = exchange(to_mate, "tp", 1)
    far, near = pl.pallas_call(
        far_kernel,
        in_specs=[VMEM] * 4,
        out_shape=arrays(1, block_len, part, dtype=jnp.float32) + arrays(1, block_len, part),
        compiler_params=compiler_params(16),
        cost_estimate=block_cost,
        name="far",
    )(lhs, *weights)
    far = (far + from_mate.astype(jnp.float32)).astype(jnp.bfloat16)
    far, near, lhs, back = lax.optimization_barrier((far, near, lhs, back))
    from_far = exchange(far, "tp", 2)
    from_near = exchange(near, "tp", 1)
    grad_filter = pl.pallas_call(
        turn_kernel,
        in_specs=[VMEM] * blocks,
        out_shape=jax.ShapeDtypeStruct((block_len, width), jnp.bfloat16),
        scratch_shapes=[pltpu.VMEM((blocks, 1, channels, block_len), jnp.bfloat16)],
        compiler_params=compiler_params(16),
        cost_estimate=block_cost,
        name="turn",
    )(*back)
    own = pl.pallas_call(
        own_kernel,
        in_specs=[VMEM] * 4,
        out_shape=arrays(1, block_len, part, dtype=jnp.float32)[0],
        compiler_params=compiler_params(16),
        cost_estimate=block_cost,
        name="own",
    )(lhs, *weights)
    total = from_far.astype(jnp.float32) + from_near.astype(jnp.float32) + own
    grad_input = total.astype(jnp.bfloat16)
    return (grad_input, grad_filter)


def solution(mesh):
    placed = (P("ctx", "tp"),) * 5 + (P(None, "tp"),) * 3
    return jax.shard_map(
        per_device,
        mesh=mesh,
        in_specs=placed,
        out_specs=(P("ctx", "tp"), P("ctx", "tp")),
        check_vma=False,
    )
```

```python
import math

import jax
import jax.numpy as jnp
import numpy as np
from jax import lax
from jax.experimental import pallas as pl
from jax.experimental.pallas import tpu as pltpu
from jax.sharding import PartitionSpec as P


def compiler_params(mib):
    return pltpu.CompilerParams(vmem_limit_bytes=int(mib * 1024 * 1024))


def dft_tables(blocks, block_len, scale):
    index = np.arange(block_len)
    angle = 2.0 * np.pi * (np.outer(index, index) % block_len) / block_len
    cos, sin = np.cos(angle), np.sin(angle)
    forward = np.block([[cos, -sin], [sin, cos]])
    inverse = forward.T
    rows = np.arange(blocks + 1)
    phase = 2.0 * np.pi * np.outer(rows, index) / (2 * blocks * block_len)
    weight = np.where((rows == 0) | (rows == blocks), 1.0, 2.0)[:, None] * scale
    twiddle = np.stack(
        [np.cos(phase), np.sin(phase), weight * np.cos(phase), weight * np.sin(phase)]
    )
    return (
        jnp.asarray(forward, jnp.bfloat16),
        jnp.asarray(inverse, jnp.bfloat16),
        jnp.asarray(twiddle, jnp.float32),
    )


def half_spectrum(values):
    size = len(values)
    if size == 1:
        return [(values[0], None), (values[0], None)]
    even, odd = half_spectrum(values[0::2]), half_spectrum(values[1::2])
    half = size // 2
    bins = [None] * (size + 1)
    bins[0] = (even[0][0] + odd[0][0], None)
    bins[size] = (even[0][0] - odd[0][0], None)
    bins[half] = (even[half][0], -odd[half][0])
    for k in range(1, half):
        angle = math.pi * k / size
        cos, sin = math.cos(angle), math.sin(angle)
        even_re, even_im = even[k]
        odd_re, odd_im = odd[k]
        if 2 * k == half:
            turn_re = cos * (odd_re + odd_im)
            turn_im = cos * (odd_im - odd_re)
        else:
            turn_re = cos * odd_re + sin * odd_im
            turn_im = cos * odd_im - sin * odd_re
        bins[k] = (even_re + turn_re, even_im + turn_im)
        bins[size - k] = (even_re - turn_re, turn_im - even_im)
    return bins


def half_spectrum_adjoint(bins):
    size = len(bins) - 1
    if size == 1:
        return [bins[0][0] + bins[1][0]]
    half = size // 2
    even, odd = [None] * (half + 1), [None] * (half + 1)
    even[0] = (bins[0][0] + bins[size][0], None)
    odd[0] = (bins[0][0] - bins[size][0], None)
    even[half] = (bins[half][0], None)
    odd[half] = (-bins[half][1], None)
    for k in range(1, half):
        angle = math.pi * k / size
        cos, sin = math.cos(angle), math.sin(angle)
        low_re, low_im = bins[k]
        high_re, high_im = bins[size - k]
        even[k] = (low_re + high_re, low_im - high_im)
        turn_re, turn_im = low_re - high_re, low_im + high_im
        if 2 * k == half:
            odd[k] = (cos * (turn_re - turn_im), cos * (turn_re + turn_im))
        else:
            odd[k] = (cos * turn_re - sin * turn_im, cos * turn_im + sin * turn_re)
    values = [None] * size
    values[0::2] = half_spectrum_adjoint(even)
    values[1::2] = half_spectrum_adjoint(odd)
    return values


HBM = pl.BlockSpec(memory_space=pltpu.HBM)
VMEM = pl.BlockSpec(memory_space=pltpu.VMEM)


def in_hbm(*arrays):
    return [pltpu.with_memory_space_constraint(array, pltpu.HBM) for array in arrays]


def offsets(blocks):
    half = blocks // 2
    shifts = sorted(range(1, half), key=lambda shift: (abs(2 * shift - half), shift))
    return [(shift, flip) for flip in (1, 0) for shift in shifts] + [(0, 1), (0, 0)]


def target(index, offset, blocks, sign=1):
    high = (index // 2 + sign * offset[0] + blocks // 2) % (blocks // 2)
    return 2 * high + (index % 2 ^ offset[1])


def to_send(refs):
    me, blocks = lax.axis_index("ctx"), len(refs)
    return [(target(me, offset, blocks), ref) for offset, ref in zip(offsets(blocks), refs)]


def received(refs):
    me, blocks = lax.axis_index("ctx"), len(refs)
    return [(target(me, offset, blocks, -1), ref) for offset, ref in zip(offsets(blocks), refs)]


def fetch(sources, targets, sems):
    copies = [
        pltpu.make_async_copy(source, target, sems.at[i])
        for i, (source, target) in enumerate(zip(sources, targets))
    ]
    for copy in copies:
        copy.start()
    return copies


def gate_kernel(*refs):
    sources, refs = refs[:5], refs[5:]
    out_refs, (turn_ref, held_ref, sems) = refs[:-3], refs[-3:]
    blocks, _, channels, block_len = turn_ref.shape
    filter_copy, *copies = fetch(sources, [held_ref.at[i] for i in range(5)], sems)

    def put(slot, wide):
        turned = wide.T.astype(jnp.bfloat16)
        turn_ref[:, slot] = turned.reshape(blocks, channels, block_len)

    filter_copy.wait()
    put(1, held_ref[0].astype(jnp.float32))
    for copy in copies[:2]:
        copy.wait()
    put(0, held_ref[1].astype(jnp.float32) * held_ref[2].astype(jnp.float32))
    for copy in copies[2:]:
        copy.wait()
    put(2, held_ref[3].astype(jnp.float32) * held_ref[4].astype(jnp.float32))
    for block, out_ref in to_send(out_refs):
        out_ref[...] = turn_ref[block]


def conv_kernel(*refs):
    blocks = lax.axis_size("ctx")
    in_refs, sources, refs = refs[:blocks], refs[blocks : blocks + 9], refs[blocks + 9 :]
    out_refs, held_refs = refs[:blocks], refs[blocks : blocks + 6]
    in_ref, rows_ref, spec_ref, twid_ref, fwd_ref, inv_ref, sems = refs[blocks + 6 :]
    twid_copy, fwd_copy, inv_copy, *held_copies = fetch(
        sources, (twid_ref, fwd_ref, inv_ref, *held_refs), sems
    )
    groups, bins_count, signals, chunk, _ = rows_ref.shape
    block_len = in_ref.shape[-1]
    for block, ref in received(in_refs):
        in_ref[block] = ref[...]
    twid_copy.wait()

    def each(count, body):
        if blocks <= 8:
            for i in range(count):
                body(i)
        else:
            pl.loop(0, count)(body)

    def put(group, k, slot, re, im):
        rows_ref[group, k, slot, :, :block_len] = re.astype(jnp.bfloat16)
        rows_ref[group, k, slot, :, block_len:] = im.astype(jnp.bfloat16)

    def get(group, k, slot):
        return spec_ref[group, k, slot, :, :block_len], spec_ref[group, k, slot, :, block_len:]

    def analyse(group):
        rows = pl.ds(group * chunk, chunk)

        def one(signal):
            bins = half_spectrum(
                [in_ref[p, signal, rows, :].astype(jnp.float32) for p in range(blocks)]
            )
            for k, (re, im) in enumerate(bins):
                cos, sin = twid_ref[0, k : k + 1, :], twid_ref[1, k : k + 1, :]
                if k == 0:
                    put(group, k, signal, re, jnp.zeros_like(re))
                elif im is None:
                    put(group, k, signal, re * cos, -(re * sin))
                else:
                    put(group, k, signal, re * cos + im * sin, im * cos - re * sin)

        each(signals, one)

    def transform(group, table_ref):
        spec_ref[group] = jnp.dot(
            rows_ref[group].reshape(bins_count * signals * chunk, 2 * block_len),
            table_ref[...],
            preferred_element_type=jnp.float32,
        ).reshape(spec_ref.shape[1:])

    def forward(group):
        if group == 0:
            fwd_copy.wait()
        transform(group, fwd_ref)

    def combine(group):
        def one(k):
            prod_re, prod_im = get(group, k, 0)
            kern_re, kern_im = get(group, k, 1)
            grad_re, grad_im = get(group, k, 2)
            conv_re = prod_re * kern_re - prod_im * kern_im
            conv_im = prod_re * kern_im + prod_im * kern_re
            back_re = grad_re * kern_re + grad_im * kern_im
            back_im = grad_im * kern_re - grad_re * kern_im
            filt_re = grad_re * prod_re + grad_im * prod_im
            filt_im = grad_im * prod_re - grad_re * prod_im
            put(group, k, 0, conv_re, conv_im)
            put(group, k, 1, back_re, back_im)
            put(group, k, 2, filt_re, filt_im)

        each(bins_count, one)

    def inverse(group):
        if group == 0:
            inv_copy.wait()
        transform(group, inv_ref)

    def synthesise(group):
        rows = pl.ds(group * chunk, chunk)

        def one(signal):
            bins = []
            for k in range(bins_count):
                re, im = get(group, k, signal)
                cos, sin = twid_ref[2, k : k + 1, :], twid_ref[3, k : k + 1, :]
                if k == 0:
                    bins.append((re * cos, None))
                elif k == blocks:
                    bins.append((re * cos - im * sin, None))
                else:
                    bins.append((re * cos - im * sin, im * cos + re * sin))
            for p, value in enumerate(half_spectrum_adjoint(bins)):
                in_ref[p, signal, rows, :] = value.astype(jnp.bfloat16)

        each(signals, one)

    stages = (analyse, forward, combine, inverse, synthesise)
    for step in range(groups + len(stages) - 1):
        for depth, stage in reversed(list(enumerate(stages))):
            if 0 <= step - depth < groups:
                stage(step - depth)
    for block, out_ref in to_send(out_refs):
        out_ref[...] = in_ref[block]
    for copy in held_copies:
        copy.wait()


def term(lhs_ref, weight_refs, group):
    part = weight_refs[0].shape[0] // lax.axis_size("tp")
    rows = pl.ds(pl.multiple_of(group * part, part), part)
    dims = (((1,), (1,)), ((), ()))
    total = None
    for slot, weight_ref in enumerate(weight_refs):
        piece = lax.dot_general(
            lhs_ref[slot], weight_ref[rows, :], dims, preferred_element_type=jnp.float32
        )
        total = piece if total is None else total + piece
    return total


def natural(back_refs, turn_ref, slots):
    blocks, _, channels, block_len = turn_ref.shape
    for block, ref in received(back_refs):
        for i, slot in enumerate(slots):
            turn_ref[block, i] = ref[slot]
    return [
        turn_ref[:, i].reshape(blocks * channels, block_len).astype(jnp.float32).T
        for i in range(len(slots))
    ]


def mate_kernel(*refs):
    blocks = lax.axis_size("ctx")
    back_refs, (key_ref, value_ref, grad_ref) = refs[:blocks], refs[blocks : blocks + 3]
    weight_refs = refs[blocks + 3 : blocks + 6]
    lhs_ref, out_ref, turn_ref = refs[blocks + 6 :]
    conv_out, grad_product = natural(back_refs, turn_ref, (0, 1))
    lhs_ref[0] = (grad_product * value_ref[...].astype(jnp.float32)).astype(jnp.bfloat16)
    lhs_ref[1] = (conv_out * grad_ref[...].astype(jnp.float32)).astype(jnp.bfloat16)
    lhs_ref[2] = (grad_product * key_ref[...].astype(jnp.float32)).astype(jnp.bfloat16)
    out_ref[...] = term(lhs_ref, weight_refs, lax.axis_index("tp") ^ 3).astype(jnp.bfloat16)


def far_kernel(lhs_ref, wk_ref, wq_ref, wv_ref, far_ref, near_ref):
    group = lax.axis_index("tp")
    far_ref[...] = term(lhs_ref, (wk_ref, wq_ref, wv_ref), group ^ 2)
    near_ref[...] = term(lhs_ref, (wk_ref, wq_ref, wv_ref), group ^ 1).astype(jnp.bfloat16)


def own_kernel(lhs_ref, wk_ref, wq_ref, wv_ref, own_ref):
    own_ref[...] = term(lhs_ref, (wk_ref, wq_ref, wv_ref), lax.axis_index("tp"))


def turn_kernel(*refs):
    back_refs, (out_ref, turn_ref) = refs[:-2], refs[-2:]
    out_ref[...] = natural(back_refs, turn_ref, (2,))[0].astype(jnp.bfloat16)


def exchange(block, distance):
    pairs = [(i, i ^ distance) for i in range(lax.axis_size("tp"))]
    return lax.ppermute(block, "tp", pairs)


def swap(pieces):
    blocks = len(pieces)
    moved = [
        lax.ppermute(piece, "ctx", [(i, target(i, offset, blocks)) for i in range(blocks)])
        for offset, piece in zip(offsets(blocks)[:-1], pieces)
    ]
    return [*moved, pieces[-1]]


def per_device(key_act, value_act, query_act, grad_out, long_filter, w_key, w_query, w_value):
    blocks = lax.axis_size("ctx")
    groups = lax.axis_size("tp")
    block_len, width = key_act.shape
    channels = width // blocks
    chunk = min(channels, 16)
    seq_len = blocks * block_len
    part = w_key.shape[0] // groups
    block_cost = pl.CostEstimate(
        flops=4 * block_len * 3 * width * part, bytes_accessed=1 << 22, transcendentals=0
    )

    def arrays(count, *shape, dtype=jnp.bfloat16):
        return [pltpu.VMEM(shape, dtype)] * count

    sent = pl.pallas_call(
        gate_kernel,
        in_specs=[HBM] * 5,
        out_shape=arrays(blocks, 3, channels, block_len),
        scratch_shapes=[
            pltpu.VMEM((blocks, 3, channels, block_len), jnp.bfloat16),
            pltpu.VMEM((5, block_len, width), jnp.bfloat16),
            pltpu.SemaphoreType.DMA((5,)),
        ],
        compiler_params=compiler_params(12),
        name="gate",
    )(*in_hbm(long_filter, key_act, value_act, query_act, grad_out))
    moved = swap(sent)

    forward, inverse, twiddle = dft_tables(
        blocks, block_len, 1.0 / (math.sqrt(seq_len) * 2 * seq_len)
    )
    tables = (twiddle, forward, inverse)
    held = (key_act, value_act, grad_out, w_key, w_query, w_value)
    results = pl.pallas_call(
        conv_kernel,
        in_specs=[VMEM] * blocks + [HBM] * 9,
        out_shape=arrays(blocks, 3, channels, block_len)
        + [pltpu.VMEM(array.shape, array.dtype) for array in held],
        scratch_shapes=[
            pltpu.VMEM((blocks, 3, channels, block_len), jnp.bfloat16),
            pltpu.VMEM((channels // chunk, blocks + 1, 3, chunk, 2 * block_len), jnp.bfloat16),
            pltpu.VMEM((channels // chunk, blocks + 1, 3, chunk, 2 * block_len), jnp.float32),
            *[pltpu.VMEM(array.shape, array.dtype) for array in tables],
            pltpu.SemaphoreType.DMA((9,)),
        ],
        compiler_params=compiler_params(28),
        name="conv",
    )(*moved, *in_hbm(*tables, *held))
    back, held = swap(results[:blocks]), results[blocks:]
    weights = held[3:]
    lhs, to_mate = pl.pallas_call(
        mate_kernel,
        in_specs=[VMEM] * (blocks + 6),
        out_shape=arrays(1, 3, block_len, width) + arrays(1, block_len, part),
        scratch_shapes=[pltpu.VMEM((blocks, 2, channels, block_len), jnp.bfloat16)],
        compiler_params=compiler_params(16),
        cost_estimate=block_cost,
        name="mate",
    )(*back, *held)
    from_mate = exchange(to_mate, 1)
    far, near = pl.pallas_call(
        far_kernel,
        in_specs=[VMEM] * 4,
        out_shape=arrays(1, block_len, part, dtype=jnp.float32) + arrays(1, block_len, part),
        compiler_params=compiler_params(16),
        cost_estimate=block_cost,
        name="far",
    )(lhs, *weights)
    far = (far + from_mate.astype(jnp.float32)).astype(jnp.bfloat16)
    far, near, lhs, back = lax.optimization_barrier((far, near, lhs, back))
    from_far = exchange(far, 2)
    from_near = exchange(near, 1)
    grad_filter = pl.pallas_call(
        turn_kernel,
        in_specs=[VMEM] * blocks,
        out_shape=jax.ShapeDtypeStruct((block_len, width), jnp.bfloat16),
        scratch_shapes=[pltpu.VMEM((blocks, 1, channels, block_len), jnp.bfloat16)],
        compiler_params=compiler_params(16),
        cost_estimate=block_cost,
        name="turn",
    )(*back)
    own = pl.pallas_call(
        own_kernel,
        in_specs=[VMEM] * 4,
        out_shape=arrays(1, block_len, part, dtype=jnp.float32)[0],
        compiler_params=compiler_params(16),
        cost_estimate=block_cost,
        name="own",
    )(lhs, *weights)
    total = from_far.astype(jnp.float32) + from_near.astype(jnp.float32) + own
    grad_input = total.astype(jnp.bfloat16)
    return (grad_input, grad_filter)


def solution(mesh):
    placed = (P("ctx", "tp"),) * 5 + (P(None, "tp"),) * 3
    return jax.shard_map(
        per_device,
        mesh=mesh,
        in_specs=placed,
        out_specs=(P("ctx", "tp"), P("ctx", "tp")),
        check_vma=False,
    )
```

```python
import math

import jax
import jax.numpy as jnp
import numpy as np
from jax import lax
from jax.experimental import pallas as pl
from jax.experimental.pallas import tpu as pltpu
from jax.sharding import PartitionSpec as P


def compiler_params(mib):
    return pltpu.CompilerParams(vmem_limit_bytes=int(mib * 1024 * 1024))


def dft_tables(blocks, block_len, scale):
    index = np.arange(block_len)
    angle = 2.0 * np.pi * (np.outer(index, index) % block_len) / block_len
    cos, sin = np.cos(angle), np.sin(angle)
    forward = np.block([[cos, -sin], [sin, cos]])
    inverse = forward.T
    rows = np.arange(blocks + 1)
    phase = 2.0 * np.pi * np.outer(rows, index) / (2 * blocks * block_len)
    weight = np.where((rows == 0) | (rows == blocks), 1.0, 2.0)[:, None] * scale
    twiddle = np.stack(
        [np.cos(phase), np.sin(phase), weight * np.cos(phase), weight * np.sin(phase)]
    )
    return (
        jnp.asarray(forward, jnp.bfloat16),
        jnp.asarray(inverse, jnp.bfloat16),
        jnp.asarray(twiddle, jnp.float32),
    )


def half_spectrum(values):
    size = len(values)
    if size == 1:
        return [(values[0], None), (values[0], None)]
    even, odd = half_spectrum(values[0::2]), half_spectrum(values[1::2])
    half = size // 2
    bins = [None] * (size + 1)
    bins[0] = (even[0][0] + odd[0][0], None)
    bins[size] = (even[0][0] - odd[0][0], None)
    bins[half] = (even[half][0], -odd[half][0])
    for k in range(1, half):
        angle = math.pi * k / size
        cos, sin = math.cos(angle), math.sin(angle)
        even_re, even_im = even[k]
        odd_re, odd_im = odd[k]
        if 2 * k == half:
            turn_re = cos * (odd_re + odd_im)
            turn_im = cos * (odd_im - odd_re)
        else:
            turn_re = cos * odd_re + sin * odd_im
            turn_im = cos * odd_im - sin * odd_re
        bins[k] = (even_re + turn_re, even_im + turn_im)
        bins[size - k] = (even_re - turn_re, turn_im - even_im)
    return bins


def half_spectrum_adjoint(bins):
    size = len(bins) - 1
    if size == 1:
        return [bins[0][0] + bins[1][0]]
    half = size // 2
    even, odd = [None] * (half + 1), [None] * (half + 1)
    even[0] = (bins[0][0] + bins[size][0], None)
    odd[0] = (bins[0][0] - bins[size][0], None)
    even[half] = (bins[half][0], None)
    odd[half] = (-bins[half][1], None)
    for k in range(1, half):
        angle = math.pi * k / size
        cos, sin = math.cos(angle), math.sin(angle)
        low_re, low_im = bins[k]
        high_re, high_im = bins[size - k]
        even[k] = (low_re + high_re, low_im - high_im)
        turn_re, turn_im = low_re - high_re, low_im + high_im
        if 2 * k == half:
            odd[k] = (cos * (turn_re - turn_im), cos * (turn_re + turn_im))
        else:
            odd[k] = (cos * turn_re - sin * turn_im, cos * turn_im + sin * turn_re)
    values = [None] * size
    values[0::2] = half_spectrum_adjoint(even)
    values[1::2] = half_spectrum_adjoint(odd)
    return values


HBM = pl.BlockSpec(memory_space=pltpu.HBM)
VMEM = pl.BlockSpec(memory_space=pltpu.VMEM)


def in_hbm(*arrays):
    return [pltpu.with_memory_space_constraint(array, pltpu.HBM) for array in arrays]


def distances(blocks):
    last = blocks - 1
    return [last - i // 2 if i % 2 == 0 else 1 + i // 2 for i in range(last)] + [0]


def late_steps(blocks):
    far = [step for step, distance in enumerate(distances(blocks)) if 2 * distance >= blocks]
    return far[len(far) // 2 : len(far) // 2 + 1]


def by_distance(pieces):
    return zip(distances(len(pieces)), pieces)


def fetch(sources, targets, sems):
    copies = [
        pltpu.make_async_copy(source, target, sems.at[i])
        for i, (source, target) in enumerate(zip(sources, targets))
    ]
    for copy in copies:
        copy.start()
    return copies


def gate_kernel(*refs):
    sources, refs = refs[:5], refs[5:]
    out_refs, (turn_ref, held_ref, sems) = refs[:-3], refs[-3:]
    blocks, _, channels, block_len = turn_ref.shape
    filter_copy, *copies = fetch(sources, [held_ref.at[i] for i in range(5)], sems)

    def put(slot, wide):
        turned = wide.T.astype(jnp.bfloat16)
        turn_ref[:, slot] = turned.reshape(blocks, channels, block_len)

    filter_copy.wait()
    put(1, held_ref[0].astype(jnp.float32))
    for copy in copies[:2]:
        copy.wait()
    put(0, held_ref[1].astype(jnp.float32) * held_ref[2].astype(jnp.float32))
    for copy in copies[2:]:
        copy.wait()
    put(2, held_ref[3].astype(jnp.float32) * held_ref[4].astype(jnp.float32))
    me = lax.axis_index("ctx")
    for distance, out_ref in by_distance(out_refs):
        out_ref[...] = turn_ref[me ^ distance]


def conv_kernel(*refs):
    blocks = lax.axis_size("ctx")
    in_refs, sources, refs = refs[:blocks], refs[blocks : blocks + 9], refs[blocks + 9 :]
    late = late_steps(blocks)
    out_refs, late_refs, held_refs = refs[:blocks], refs[blocks : -13], refs[-13:-7]
    in_ref, rows_ref, spec_ref, twid_ref, fwd_ref, inv_ref, sems = refs[-7:]
    twid_copy, fwd_copy, inv_copy, *held_copies = fetch(
        sources, (twid_ref, fwd_ref, inv_ref, *held_refs), sems
    )
    groups, bins_count, signals, chunk, _ = rows_ref.shape
    block_len = in_ref.shape[-1]
    me = lax.axis_index("ctx")
    for distance, ref in by_distance(in_refs):
        in_ref[me ^ distance] = ref[...]
    twid_copy.wait()

    def each(count, body):
        if blocks <= 8:
            for i in range(count):
                body(i)
        else:
            pl.loop(0, count)(body)

    def put(group, k, slot, re, im):
        rows_ref[group, k, slot, :, :block_len] = re.astype(jnp.bfloat16)
        rows_ref[group, k, slot, :, block_len:] = im.astype(jnp.bfloat16)

    def get(group, k, slot):
        return spec_ref[group, k, slot, :, :block_len], spec_ref[group, k, slot, :, block_len:]

    def analyse(group):
        rows = pl.ds(group * chunk, chunk)

        def one(signal):
            bins = half_spectrum(
                [in_ref[p, signal, rows, :].astype(jnp.float32) for p in range(blocks)]
            )
            for k, (re, im) in enumerate(bins):
                cos, sin = twid_ref[0, k : k + 1, :], twid_ref[1, k : k + 1, :]
                if k == 0:
                    put(group, k, signal, re, jnp.zeros_like(re))
                elif im is None:
                    put(group, k, signal, re * cos, -(re * sin))
                else:
                    put(group, k, signal, re * cos + im * sin, im * cos - re * sin)

        each(signals, one)

    def transform(group, table_ref):
        spec_ref[group] = jnp.dot(
            rows_ref[group].reshape(bins_count * signals * chunk, 2 * block_len),
            table_ref[...],
            preferred_element_type=jnp.float32,
        ).reshape(spec_ref.shape[1:])

    def forward(group):
        if group == 0:
            fwd_copy.wait()
        transform(group, fwd_ref)

    def combine(group):
        def one(k):
            prod_re, prod_im = get(group, k, 0)
            kern_re, kern_im = get(group, k, 1)
            grad_re, grad_im = get(group, k, 2)
            conv_re = prod_re * kern_re - prod_im * kern_im
            conv_im = prod_re * kern_im + prod_im * kern_re
            back_re = grad_re * kern_re + grad_im * kern_im
            back_im = grad_im * kern_re - grad_re * kern_im
            filt_re = grad_re * prod_re + grad_im * prod_im
            filt_im = grad_im * prod_re - grad_re * prod_im
            put(group, k, 0, conv_re, conv_im)
            put(group, k, 1, back_re, back_im)
            put(group, k, 2, filt_re, filt_im)

        each(bins_count, one)

    def inverse(group):
        if group == 0:
            inv_copy.wait()
        transform(group, inv_ref)

    def synthesise(group):
        rows = pl.ds(group * chunk, chunk)

        def one(signal):
            bins = []
            for k in range(bins_count):
                re, im = get(group, k, signal)
                cos, sin = twid_ref[2, k : k + 1, :], twid_ref[3, k : k + 1, :]
                if k == 0:
                    bins.append((re * cos, None))
                elif k == blocks:
                    bins.append((re * cos - im * sin, None))
                else:
                    bins.append((re * cos - im * sin, im * cos + re * sin))
            for p, value in enumerate(half_spectrum_adjoint(bins)):
                in_ref[p, signal, rows, :] = value.astype(jnp.bfloat16)

        each(signals, one)

    stages = (analyse, forward, combine, inverse, synthesise)
    for step in range(groups + len(stages) - 1):
        for depth, stage in reversed(list(enumerate(stages))):
            if 0 <= step - depth < groups:
                stage(step - depth)
    for distance, out_ref in by_distance(out_refs):
        out_ref[...] = in_ref[me ^ distance, : out_ref.shape[0]]
    for step, late_ref in zip(late, late_refs):
        late_ref[...] = in_ref[me ^ distances(blocks)[step], 2:]
    for copy in held_copies:
        copy.wait()


def term(lhs_ref, weight_refs, group):
    part = weight_refs[0].shape[0] // lax.axis_size("tp")
    rows = pl.ds(pl.multiple_of(group * part, part), part)
    dims = (((1,), (1,)), ((), ()))
    total = None
    for slot, weight_ref in enumerate(weight_refs):
        piece = lax.dot_general(
            lhs_ref[slot], weight_ref[rows, :], dims, preferred_element_type=jnp.float32
        )
        total = piece if total is None else total + piece
    return total


def natural(back_refs, turn_ref, slots):
    blocks, _, channels, block_len = turn_ref.shape
    me = lax.axis_index("ctx")
    for distance, ref in by_distance(back_refs):
        for i, slot in enumerate(slots):
            turn_ref[me ^ distance, i] = ref[slot % ref.shape[0]]
    return [
        turn_ref[:, i].reshape(blocks * channels, block_len).astype(jnp.float32).T
        for i in range(len(slots))
    ]


def mate_kernel(*refs):
    blocks = lax.axis_size("ctx")
    back_refs, (key_ref, value_ref, grad_ref) = refs[:blocks], refs[blocks : blocks + 3]
    weight_refs = refs[blocks + 3 : blocks + 6]
    lhs_ref, out_ref, turn_ref = refs[blocks + 6 :]
    conv_out, grad_product = natural(back_refs, turn_ref, (0, 1))
    lhs_ref[0] = (grad_product * value_ref[...].astype(jnp.float32)).astype(jnp.bfloat16)
    lhs_ref[1] = (conv_out * grad_ref[...].astype(jnp.float32)).astype(jnp.bfloat16)
    lhs_ref[2] = (grad_product * key_ref[...].astype(jnp.float32)).astype(jnp.bfloat16)
    out_ref[...] = term(lhs_ref, weight_refs, lax.axis_index("tp") ^ 3).astype(jnp.bfloat16)


def far_kernel(lhs_ref, wk_ref, wq_ref, wv_ref, far_ref, near_ref):
    group = lax.axis_index("tp")
    far_ref[...] = term(lhs_ref, (wk_ref, wq_ref, wv_ref), group ^ 2)
    near_ref[...] = term(lhs_ref, (wk_ref, wq_ref, wv_ref), group ^ 1).astype(jnp.bfloat16)


def own_kernel(lhs_ref, wk_ref, wq_ref, wv_ref, own_ref):
    own_ref[...] = term(lhs_ref, (wk_ref, wq_ref, wv_ref), lax.axis_index("tp"))


def turn_kernel(*refs):
    blocks = lax.axis_size("ctx")
    back_refs, late_refs, (out_ref, turn_ref) = list(refs[:blocks]), refs[blocks:-2], refs[-2:]
    for step, ref in zip(late_steps(blocks), late_refs):
        back_refs[step] = ref
    out_ref[...] = natural(back_refs, turn_ref, (-1,))[0].astype(jnp.bfloat16)


def exchange(block, axis, distance):
    pairs = [(i, i ^ distance) for i in range(lax.axis_size(axis))]
    return lax.ppermute(block, axis, pairs)


def swap(pieces):
    return [
        exchange(piece, "ctx", distance) if distance else piece
        for distance, piece in by_distance(pieces)
    ]


def swap_late(pieces, blocks):
    return [
        exchange(piece, "ctx", distances(blocks)[step])
        for step, piece in zip(late_steps(blocks), pieces)
    ]


def per_device(key_act, value_act, query_act, grad_out, long_filter, w_key, w_query, w_value):
    blocks = lax.axis_size("ctx")
    groups = lax.axis_size("tp")
    block_len, width = key_act.shape
    channels = width // blocks
    chunk = min(channels, 16)
    seq_len = blocks * block_len
    part = w_key.shape[0] // groups
    block_cost = pl.CostEstimate(
        flops=4 * block_len * 3 * width * part, bytes_accessed=1 << 22, transcendentals=0
    )

    def arrays(count, *shape, dtype=jnp.bfloat16):
        return [pltpu.VMEM(shape, dtype)] * count

    sent = pl.pallas_call(
        gate_kernel,
        in_specs=[HBM] * 5,
        out_shape=arrays(blocks, 3, channels, block_len),
        scratch_shapes=[
            pltpu.VMEM((blocks, 3, channels, block_len), jnp.bfloat16),
            pltpu.VMEM((5, block_len, width), jnp.bfloat16),
            pltpu.SemaphoreType.DMA((5,)),
        ],
        compiler_params=compiler_params(12),
        name="gate",
    )(*in_hbm(long_filter, key_act, value_act, query_act, grad_out))
    moved = swap(sent)

    forward, inverse, twiddle = dft_tables(
        blocks, block_len, 1.0 / (math.sqrt(seq_len) * 2 * seq_len)
    )
    tables = (twiddle, forward, inverse)
    held = (key_act, value_act, grad_out, w_key, w_query, w_value)
    late = late_steps(blocks)
    results = pl.pallas_call(
        conv_kernel,
        in_specs=[VMEM] * blocks + [HBM] * 9,
        out_shape=[
            pltpu.VMEM((2 if step in late else 3, channels, block_len), jnp.bfloat16)
            for step in range(blocks)
        ]
        + arrays(len(late), 1, channels, block_len)
        + [pltpu.VMEM(array.shape, array.dtype) for array in held],
        scratch_shapes=[
            pltpu.VMEM((blocks, 3, channels, block_len), jnp.bfloat16),
            pltpu.VMEM((channels // chunk, blocks + 1, 3, chunk, 2 * block_len), jnp.bfloat16),
            pltpu.VMEM((channels // chunk, blocks + 1, 3, chunk, 2 * block_len), jnp.float32),
            *[pltpu.VMEM(array.shape, array.dtype) for array in tables],
            pltpu.SemaphoreType.DMA((9,)),
        ],
        compiler_params=compiler_params(28),
        name="conv",
    )(*moved, *in_hbm(*tables, *held))
    back, late_back, held = swap(results[:blocks]), results[blocks:-6], results[-6:]
    weights = held[3:]
    lhs, to_mate = pl.pallas_call(
        mate_kernel,
        in_specs=[VMEM] * (blocks + 6),
        out_shape=arrays(1, 3, block_len, width) + arrays(1, block_len, part),
        scratch_shapes=[pltpu.VMEM((blocks, 2, channels, block_len), jnp.bfloat16)],
        compiler_params=compiler_params(16),
        cost_estimate=block_cost,
        name="mate",
    )(*back, *held)
    from_mate = exchange(to_mate, "tp", 1)
    far, near = pl.pallas_call(
        far_kernel,
        in_specs=[VMEM] * 4,
        out_shape=arrays(1, block_len, part, dtype=jnp.float32) + arrays(1, block_len, part),
        compiler_params=compiler_params(16),
        cost_estimate=block_cost,
        name="far",
    )(lhs, *weights)
    far = (far + from_mate.astype(jnp.float32)).astype(jnp.bfloat16)
    far, near, lhs, late_back = lax.optimization_barrier((far, near, lhs, late_back))
    from_far = exchange(far, "tp", 2)
    from_near = exchange(near, "tp", 1)
    own = pl.pallas_call(
        own_kernel,
        in_specs=[VMEM] * 4,
        out_shape=arrays(1, block_len, part, dtype=jnp.float32)[0],
        compiler_params=compiler_params(16),
        cost_estimate=block_cost,
        name="own",
    )(lhs, *weights)
    own, late_back = lax.optimization_barrier((own, late_back))
    grad_filter = pl.pallas_call(
        turn_kernel,
        in_specs=[VMEM] * (blocks + len(late)),
        out_shape=jax.ShapeDtypeStruct((block_len, width), jnp.bfloat16),
        scratch_shapes=[pltpu.VMEM((blocks, 1, channels, block_len), jnp.bfloat16)],
        compiler_params=compiler_params(16),
        cost_estimate=block_cost,
        name="turn",
    )(*back, *swap_late(late_back, blocks))
    total = from_far.astype(jnp.float32) + from_near.astype(jnp.float32) + own
    grad_input = total.astype(jnp.bfloat16)
    return (grad_input, grad_filter)


def solution(mesh):
    placed = (P("ctx", "tp"),) * 5 + (P(None, "tp"),) * 3
    return jax.shard_map(
        per_device,
        mesh=mesh,
        in_specs=placed,
        out_specs=(P("ctx", "tp"), P("ctx", "tp")),
        check_vma=False,
    )
```

```python
import math

import jax
import jax.numpy as jnp
import numpy as np
from jax import lax
from jax.experimental import pallas as pl
from jax.experimental.pallas import tpu as pltpu
from jax.sharding import PartitionSpec as P


def compiler_params(mib):
    return pltpu.CompilerParams(vmem_limit_bytes=int(mib * 1024 * 1024))


def dft_tables(blocks, block_len, scale, rows_count):
    index = np.arange(block_len)
    angle = 2.0 * np.pi * (np.outer(index, index) % block_len) / block_len
    cos, sin = np.cos(angle), np.sin(angle)
    forward = np.block([[cos, -sin], [sin, cos]])
    inverse = forward.T
    rows = np.arange(blocks + 1)
    phase = 2.0 * np.pi * np.outer(rows, index) / (2 * blocks * block_len)
    weight = np.where((rows == 0) | (rows == blocks), 1.0, 2.0)[:, None] * scale
    twiddle = np.stack([np.cos(phase), np.sin(phase)])
    untwiddle = np.repeat((weight * twiddle)[:, :, None, :], rows_count, axis=2)
    return (
        jnp.asarray(forward, jnp.bfloat16),
        jnp.asarray(inverse, jnp.bfloat16),
        jnp.asarray(twiddle, jnp.float32),
        jnp.asarray(untwiddle, jnp.bfloat16),
    )


def half_spectrum(values):
    size = len(values)
    if size == 1:
        return [(values[0], None), (values[0], None)]
    even, odd = half_spectrum(values[0::2]), half_spectrum(values[1::2])
    half = size // 2
    bins = [None] * (size + 1)
    bins[0] = (even[0][0] + odd[0][0], None)
    bins[size] = (even[0][0] - odd[0][0], None)
    bins[half] = (even[half][0], -odd[half][0])
    for k in range(1, half):
        angle = math.pi * k / size
        cos, sin = math.cos(angle), math.sin(angle)
        even_re, even_im = even[k]
        odd_re, odd_im = odd[k]
        if 2 * k == half:
            turn_re = cos * (odd_re + odd_im)
            turn_im = cos * (odd_im - odd_re)
        else:
            turn_re = cos * odd_re + sin * odd_im
            turn_im = cos * odd_im - sin * odd_re
        bins[k] = (even_re + turn_re, even_im + turn_im)
        bins[size - k] = (even_re - turn_re, turn_im - even_im)
    return bins


def half_spectrum_adjoint(bins):
    size = len(bins) - 1
    if size == 1:
        return [bins[0][0] + bins[1][0]]
    half = size // 2
    even, odd = [None] * (half + 1), [None] * (half + 1)
    even[0] = (bins[0][0] + bins[size][0], None)
    odd[0] = (bins[0][0] - bins[size][0], None)
    even[half] = (bins[half][0], None)
    odd[half] = (-bins[half][1], None)
    for k in range(1, half):
        angle = math.pi * k / size
        cos, sin = math.cos(angle), math.sin(angle)
        low_re, low_im = bins[k]
        high_re, high_im = bins[size - k]
        even[k] = (low_re + high_re, low_im - high_im)
        turn_re, turn_im = low_re - high_re, low_im + high_im
        if 2 * k == half:
            odd[k] = (cos * (turn_re - turn_im), cos * (turn_re + turn_im))
        else:
            odd[k] = (cos * turn_re - sin * turn_im, cos * turn_im + sin * turn_re)
    values = [None] * size
    values[0::2] = half_spectrum_adjoint(even)
    values[1::2] = half_spectrum_adjoint(odd)
    return values


HBM = pl.BlockSpec(memory_space=pltpu.HBM)
VMEM = pl.BlockSpec(memory_space=pltpu.VMEM)


def in_hbm(*arrays):
    return [pltpu.with_memory_space_constraint(array, pltpu.HBM) for array in arrays]


def by_distance(pieces):
    last = len(pieces) - 1
    order = [last - i // 2 if i % 2 == 0 else 1 + i // 2 for i in range(last)]
    return zip([*order, 0], pieces)


def fetch(sources, targets, sems):
    copies = [
        pltpu.make_async_copy(source, target, sems.at[i])
        for i, (source, target) in enumerate(zip(sources, targets))
    ]
    for copy in copies:
        copy.start()
    return copies


def gate_kernel(*refs):
    sources, refs = refs[:5], refs[5:]
    out_refs, (turn_ref, held_ref, sems) = refs[:-3], refs[-3:]
    blocks, _, channels, block_len = turn_ref.shape
    filter_copy, *copies = fetch(sources, [held_ref.at[i] for i in range(5)], sems)

    def put(slot, wide):
        turned = wide.T.astype(jnp.bfloat16)
        turn_ref[:, slot] = turned.reshape(blocks, channels, block_len)

    filter_copy.wait()
    put(1, held_ref[0].astype(jnp.float32))
    for copy in copies[:2]:
        copy.wait()
    put(0, held_ref[1].astype(jnp.float32) * held_ref[2].astype(jnp.float32))
    for copy in copies[2:]:
        copy.wait()
    put(2, held_ref[3].astype(jnp.float32) * held_ref[4].astype(jnp.float32))
    me = lax.axis_index("ctx")
    for distance, out_ref in by_distance(out_refs):
        out_ref[...] = turn_ref[me ^ distance]


def conv_kernel(*refs):
    blocks = lax.axis_size("ctx")
    in_refs, sources, refs = refs[:blocks], refs[blocks : blocks + 10], refs[blocks + 10 :]
    out_refs, held_refs = refs[:blocks], refs[blocks : blocks + 6]
    in_ref, rows_ref, spec_ref, twid_ref, back_ref, fwd_ref, inv_ref, sems = refs[blocks + 6 :]
    twid_copy, back_copy, fwd_copy, inv_copy, *held_copies = fetch(
        sources, (twid_ref, back_ref, fwd_ref, inv_ref, *held_refs), sems
    )
    groups, bins_count, signals, chunk, _ = rows_ref.shape
    block_len = in_ref.shape[-1]
    me = lax.axis_index("ctx")
    for distance, ref in by_distance(in_refs):
        in_ref[me ^ distance] = ref[...]
    twid_copy.wait()

    def each(count, body):
        if blocks <= 8:
            for i in range(count):
                body(i)
        else:
            pl.loop(0, count)(body)

    def put(group, k, slot, re, im):
        rows_ref[group, k, slot, :, :block_len] = re.astype(jnp.bfloat16)
        rows_ref[group, k, slot, :, block_len:] = im.astype(jnp.bfloat16)

    def get(group, k, slot):
        re, im = spec_ref[group, k, slot, :, :block_len], spec_ref[group, k, slot, :, block_len:]
        return re.astype(jnp.bfloat16), im.astype(jnp.bfloat16)

    def analyse(group):
        rows = pl.ds(group * chunk, chunk)

        def one(signal):
            bins = half_spectrum(
                [in_ref[p, signal, rows, :].astype(jnp.float32) for p in range(blocks)]
            )
            for k, (re, im) in enumerate(bins):
                cos, sin = twid_ref[0, k : k + 1, :], twid_ref[1, k : k + 1, :]
                if k == 0:
                    put(group, k, signal, re, jnp.zeros_like(re))
                elif im is None:
                    put(group, k, signal, re * cos, -(re * sin))
                else:
                    put(group, k, signal, re * cos + im * sin, im * cos - re * sin)

        each(signals, one)

    def transform(group, table_ref):
        spec_ref[group] = jnp.dot(
            rows_ref[group].reshape(bins_count * signals * chunk, 2 * block_len),
            table_ref[...],
            preferred_element_type=jnp.float32,
        ).reshape(spec_ref.shape[1:])

    def forward(group):
        if group == 0:
            fwd_copy.wait()
        transform(group, fwd_ref)

    def combine(group):
        def one(k):
            prod_re, prod_im = get(group, k, 0)
            kern_re, kern_im = get(group, k, 1)
            grad_re, grad_im = get(group, k, 2)
            conv_re = prod_re * kern_re - prod_im * kern_im
            conv_im = prod_re * kern_im + prod_im * kern_re
            back_re = grad_re * kern_re + grad_im * kern_im
            back_im = grad_im * kern_re - grad_re * kern_im
            filt_re = grad_re * prod_re + grad_im * prod_im
            filt_im = grad_im * prod_re - grad_re * prod_im
            put(group, k, 0, conv_re, conv_im)
            put(group, k, 1, back_re, back_im)
            put(group, k, 2, filt_re, filt_im)

        each(bins_count, one)

    def inverse(group):
        if group == 0:
            inv_copy.wait()
            back_copy.wait()
        transform(group, inv_ref)

    def synthesise(group):
        rows = pl.ds(group * chunk, chunk)

        def one(signal):
            bins = []
            for k in range(bins_count):
                re, im = get(group, k, signal)
                cos, sin = back_ref[0, k], back_ref[1, k]
                if k == 0:
                    bins.append((re * cos, None))
                elif k == blocks:
                    bins.append((re * cos - im * sin, None))
                else:
                    bins.append((re * cos - im * sin, im * cos + re * sin))
            for p, value in enumerate(half_spectrum_adjoint(bins)):
                in_ref[p, signal, rows, :] = value

        each(signals, one)

    stages = (analyse, forward, combine, inverse, synthesise)
    for step in range(groups + len(stages) - 1):
        for depth, stage in reversed(list(enumerate(stages))):
            if 0 <= step - depth < groups:
                stage(step - depth)
    for distance, out_ref in by_distance(out_refs):
        out_ref[...] = in_ref[me ^ distance]
    for copy in held_copies:
        copy.wait()


def term(lhs_ref, weight_refs, group):
    part = weight_refs[0].shape[0] // lax.axis_size("tp")
    rows = pl.ds(pl.multiple_of(group * part, part), part)
    dims = (((1,), (1,)), ((), ()))
    total = None
    for slot, weight_ref in enumerate(weight_refs):
        piece = lax.dot_general(
            lhs_ref[slot], weight_ref[rows, :], dims, preferred_element_type=jnp.float32
        )
        total = piece if total is None else total + piece
    return total


def natural(back_refs, turn_ref, slots):
    blocks, _, channels, block_len = turn_ref.shape
    me = lax.axis_index("ctx")
    for distance, ref in by_distance(back_refs):
        for i, slot in enumerate(slots):
            turn_ref[me ^ distance, i] = ref[slot]
    return [
        turn_ref[:, i].reshape(blocks * channels, block_len).astype(jnp.float32).T
        for i in range(len(slots))
    ]


def mate_kernel(*refs):
    blocks = lax.axis_size("ctx")
    back_refs, (key_ref, value_ref, grad_ref) = refs[:blocks], refs[blocks : blocks + 3]
    weight_refs = refs[blocks + 3 : blocks + 6]
    lhs_ref, out_ref, turn_ref = refs[blocks + 6 :]
    conv_out, grad_product = natural(back_refs, turn_ref, (0, 1))
    lhs_ref[0] = (grad_product * value_ref[...].astype(jnp.float32)).astype(jnp.bfloat16)
    lhs_ref[1] = (conv_out * grad_ref[...].astype(jnp.float32)).astype(jnp.bfloat16)
    lhs_ref[2] = (grad_product * key_ref[...].astype(jnp.float32)).astype(jnp.bfloat16)
    out_ref[...] = term(lhs_ref, weight_refs, lax.axis_index("tp") ^ 3).astype(jnp.bfloat16)


def far_kernel(lhs_ref, wk_ref, wq_ref, wv_ref, far_ref, near_ref):
    group = lax.axis_index("tp")
    far_ref[...] = term(lhs_ref, (wk_ref, wq_ref, wv_ref), group ^ 2)
    near_ref[...] = term(lhs_ref, (wk_ref, wq_ref, wv_ref), group ^ 1).astype(jnp.bfloat16)


def own_kernel(lhs_ref, wk_ref, wq_ref, wv_ref, own_ref):
    own_ref[...] = term(lhs_ref, (wk_ref, wq_ref, wv_ref), lax.axis_index("tp"))


def turn_kernel(*refs):
    back_refs, (out_ref, turn_ref) = refs[:-2], refs[-2:]
    out_ref[...] = natural(back_refs, turn_ref, (2,))[0].astype(jnp.bfloat16)


def exchange(block, axis, distance):
    pairs = [(i, i ^ distance) for i in range(lax.axis_size(axis))]
    return lax.ppermute(block, axis, pairs)


def swap(pieces):
    return [
        exchange(piece, "ctx", distance) if distance else piece
        for distance, piece in by_distance(pieces)
    ]


def per_device(key_act, value_act, query_act, grad_out, long_filter, w_key, w_query, w_value):
    blocks = lax.axis_size("ctx")
    groups = lax.axis_size("tp")
    block_len, width = key_act.shape
    channels = width // blocks
    chunk = min(channels, 16)
    seq_len = blocks * block_len
    part = w_key.shape[0] // groups
    block_cost = pl.CostEstimate(
        flops=4 * block_len * 3 * width * part, bytes_accessed=1 << 22, transcendentals=0
    )

    def arrays(count, *shape, dtype=jnp.bfloat16):
        return [pltpu.VMEM(shape, dtype)] * count

    sent = pl.pallas_call(
        gate_kernel,
        in_specs=[HBM] * 5,
        out_shape=arrays(blocks, 3, channels, block_len),
        scratch_shapes=[
            pltpu.VMEM((blocks, 3, channels, block_len), jnp.bfloat16),
            pltpu.VMEM((5, block_len, width), jnp.bfloat16),
            pltpu.SemaphoreType.DMA((5,)),
        ],
        compiler_params=compiler_params(12),
        name="gate",
    )(*in_hbm(long_filter, key_act, value_act, query_act, grad_out))
    moved = swap(sent)

    forward, inverse, twiddle, untwiddle = dft_tables(
        blocks, block_len, 1.0 / (math.sqrt(seq_len) * 2 * seq_len), chunk
    )
    tables = (twiddle, untwiddle, forward, inverse)
    held = (key_act, value_act, grad_out, w_key, w_query, w_value)
    results = pl.pallas_call(
        conv_kernel,
        in_specs=[VMEM] * blocks + [HBM] * 10,
        out_shape=arrays(blocks, 3, channels, block_len)
        + [pltpu.VMEM(array.shape, array.dtype) for array in held],
        scratch_shapes=[
            pltpu.VMEM((blocks, 3, channels, block_len), jnp.bfloat16),
            pltpu.VMEM((channels // chunk, blocks + 1, 3, chunk, 2 * block_len), jnp.bfloat16),
            pltpu.VMEM((channels // chunk, blocks + 1, 3, chunk, 2 * block_len), jnp.float32),
            *[pltpu.VMEM(array.shape, array.dtype) for array in tables],
            pltpu.SemaphoreType.DMA((10,)),
        ],
        compiler_params=compiler_params(28),
        name="conv",
    )(*moved, *in_hbm(*tables, *held))
    back, held = swap(results[:blocks]), results[blocks:]
    weights = held[3:]
    lhs, to_mate = pl.pallas_call(
        mate_kernel,
        in_specs=[VMEM] * (blocks + 6),
        out_shape=arrays(1, 3, block_len, width) + arrays(1, block_len, part),
        scratch_shapes=[pltpu.VMEM((blocks, 2, channels, block_len), jnp.bfloat16)],
        compiler_params=compiler_params(16),
        cost_estimate=block_cost,
        name="mate",
    )(*back, *held)
    from_mate = exchange(to_mate, "tp", 1)
    far, near = pl.pallas_call(
        far_kernel,
        in_specs=[VMEM] * 4,
        out_shape=arrays(1, block_len, part, dtype=jnp.float32) + arrays(1, block_len, part),
        compiler_params=compiler_params(16),
        cost_estimate=block_cost,
        name="far",
    )(lhs, *weights)
    far = (far + from_mate.astype(jnp.float32)).astype(jnp.bfloat16)
    far, near, lhs, back = lax.optimization_barrier((far, near, lhs, back))
    from_far = exchange(far, "tp", 2)
    from_near = exchange(near, "tp", 1)
    grad_filter = pl.pallas_call(
        turn_kernel,
        in_specs=[VMEM] * blocks,
        out_shape=jax.ShapeDtypeStruct((block_len, width), jnp.bfloat16),
        scratch_shapes=[pltpu.VMEM((blocks, 1, channels, block_len), jnp.bfloat16)],
        compiler_params=compiler_params(16),
        cost_estimate=block_cost,
        name="turn",
    )(*back)
    own = pl.pallas_call(
        own_kernel,
        in_specs=[VMEM] * 4,
        out_shape=arrays(1, block_len, part, dtype=jnp.float32)[0],
        compiler_params=compiler_params(16),
        cost_estimate=block_cost,
        name="own",
    )(lhs, *weights)
    total = from_far.astype(jnp.float32) + from_near.astype(jnp.float32) + own
    grad_input = total.astype(jnp.bfloat16)
    return (grad_input, grad_filter)


def solution(mesh):
    placed = (P("ctx", "tp"),) * 5 + (P(None, "tp"),) * 3
    return jax.shard_map(
        per_device,
        mesh=mesh,
        in_specs=placed,
        out_specs=(P("ctx", "tp"), P("ctx", "tp")),
        check_vma=False,
    )
```

```python
import math

import jax
import jax.numpy as jnp
import numpy as np
from jax import lax
from jax.experimental import pallas as pl
from jax.experimental.pallas import tpu as pltpu
from jax.sharding import PartitionSpec as P


def compiler_params(mib):
    return pltpu.CompilerParams(vmem_limit_bytes=int(mib * 1024 * 1024))


def dft_tables(blocks, block_len, scale, rows_count):
    index, half = np.arange(block_len), np.arange(block_len // 2)
    bins = 2 * half[None, :] + np.arange(2)[:, None]
    angle = 2.0 * np.pi * (half[None, :, None] * bins[:, None, :] % block_len) / block_len
    cos, sin = np.cos(angle), np.sin(angle)
    forward = np.block([[cos, -sin], [sin, cos]])
    inverse = forward.transpose(0, 2, 1)
    rows = np.arange(blocks + 1)
    phase = 2.0 * np.pi * np.outer(rows, index) / (2 * blocks * block_len)
    weight = np.where((rows == 0) | (rows == blocks), 1.0, 2.0)[:, None] * scale
    twiddle = np.stack([np.cos(phase), np.sin(phase)])
    untwiddle = np.repeat((weight * twiddle)[:, :, None, :], rows_count, axis=2)
    return (
        jnp.asarray(forward, jnp.bfloat16),
        jnp.asarray(inverse, jnp.bfloat16),
        jnp.asarray(twiddle, jnp.float32),
        jnp.asarray(untwiddle, jnp.bfloat16),
    )


def half_spectrum(values):
    size = len(values)
    if size == 1:
        return [(values[0], None), (values[0], None)]
    even, odd = half_spectrum(values[0::2]), half_spectrum(values[1::2])
    half = size // 2
    bins = [None] * (size + 1)
    bins[0] = (even[0][0] + odd[0][0], None)
    bins[size] = (even[0][0] - odd[0][0], None)
    bins[half] = (even[half][0], -odd[half][0])
    for k in range(1, half):
        angle = math.pi * k / size
        cos, sin = math.cos(angle), math.sin(angle)
        even_re, even_im = even[k]
        odd_re, odd_im = odd[k]
        if 2 * k == half:
            turn_re = cos * (odd_re + odd_im)
            turn_im = cos * (odd_im - odd_re)
        else:
            turn_re = cos * odd_re + sin * odd_im
            turn_im = cos * odd_im - sin * odd_re
        bins[k] = (even_re + turn_re, even_im + turn_im)
        bins[size - k] = (even_re - turn_re, turn_im - even_im)
    return bins


def half_spectrum_adjoint(bins):
    size = len(bins) - 1
    if size == 1:
        return [bins[0][0] + bins[1][0]]
    half = size // 2
    even, odd = [None] * (half + 1), [None] * (half + 1)
    even[0] = (bins[0][0] + bins[size][0], None)
    odd[0] = (bins[0][0] - bins[size][0], None)
    even[half] = (bins[half][0], None)
    odd[half] = (-bins[half][1], None)
    for k in range(1, half):
        angle = math.pi * k / size
        cos, sin = math.cos(angle), math.sin(angle)
        low_re, low_im = bins[k]
        high_re, high_im = bins[size - k]
        even[k] = (low_re + high_re, low_im - high_im)
        turn_re, turn_im = low_re - high_re, low_im + high_im
        if 2 * k == half:
            odd[k] = (cos * (turn_re - turn_im), cos * (turn_re + turn_im))
        else:
            odd[k] = (cos * turn_re - sin * turn_im, cos * turn_im + sin * turn_re)
    values = [None] * size
    values[0::2] = half_spectrum_adjoint(even)
    values[1::2] = half_spectrum_adjoint(odd)
    return values


HBM = pl.BlockSpec(memory_space=pltpu.HBM)
VMEM = pl.BlockSpec(memory_space=pltpu.VMEM)


def in_hbm(*arrays):
    return [pltpu.with_memory_space_constraint(array, pltpu.HBM) for array in arrays]


def by_distance(pieces):
    last = len(pieces) - 1
    order = [last - i // 2 if i % 2 == 0 else 1 + i // 2 for i in range(last)]
    return zip([*order, 0], pieces)


def fetch(sources, targets, sems):
    copies = [
        pltpu.make_async_copy(source, target, sems.at[i])
        for i, (source, target) in enumerate(zip(sources, targets))
    ]
    for copy in copies:
        copy.start()
    return copies


def gate_kernel(*refs):
    sources, refs = refs[:5], refs[5:]
    out_refs, (turn_ref, held_ref, sems) = refs[:-3], refs[-3:]
    blocks, _, channels, block_len = turn_ref.shape
    filter_copy, *copies = fetch(sources, [held_ref.at[i] for i in range(5)], sems)

    def put(slot, wide):
        turned = wide.T.astype(jnp.bfloat16)
        turn_ref[:, slot] = turned.reshape(blocks, channels, block_len)

    filter_copy.wait()
    put(1, held_ref[0].astype(jnp.float32))
    for copy in copies[:2]:
        copy.wait()
    put(0, held_ref[1].astype(jnp.float32) * held_ref[2].astype(jnp.float32))
    for copy in copies[2:]:
        copy.wait()
    put(2, held_ref[3].astype(jnp.float32) * held_ref[4].astype(jnp.float32))
    me = lax.axis_index("ctx")
    for distance, out_ref in by_distance(out_refs):
        out_ref[...] = turn_ref[me ^ distance]


def conv_kernel(*refs):
    blocks = lax.axis_size("ctx")
    in_refs, sources, refs = refs[:blocks], refs[blocks : blocks + 10], refs[blocks + 10 :]
    out_refs, held_refs = refs[:blocks], refs[blocks : blocks + 6]
    in_ref, rows_ref, spec_ref, twid_ref, back_ref, fwd_ref, inv_ref, sems = refs[blocks + 6 :]
    twid_copy, back_copy, fwd_copy, inv_copy, *held_copies = fetch(
        sources, (twid_ref, back_ref, fwd_ref, inv_ref, *held_refs), sems
    )
    groups, bins_count, signals, chunk, _ = rows_ref.shape
    block_len = in_ref.shape[-1]
    me = lax.axis_index("ctx")
    for distance, ref in by_distance(in_refs):
        in_ref[me ^ distance] = ref[...]
    twid_copy.wait()

    def each(count, body):
        if blocks <= 8:
            for i in range(count):
                body(i)
        else:
            pl.loop(0, count)(body)

    half = block_len // 2

    def put(group, k, slot, part, re, im):
        rows_ref[group, k, slot, :, part * block_len : part * block_len + half] = re.astype(
            jnp.bfloat16
        )
        rows_ref[group, k, slot, :, part * block_len + half : (part + 1) * block_len] = im.astype(
            jnp.bfloat16
        )

    def get(group, k, slot, part):
        re = spec_ref[group, k, slot, :, part * block_len : part * block_len + half]
        im = spec_ref[group, k, slot, :, part * block_len + half : (part + 1) * block_len]
        return re, im

    def put_halves(group, k, slot, re, im):
        put(group, k, slot, 0, re[:, :half] + re[:, half:], im[:, :half] + im[:, half:])
        put(group, k, slot, 1, re[:, :half] - re[:, half:], im[:, :half] - im[:, half:])

    def get_halves(group, k, slot):
        even_re, even_im = get(group, k, slot, 0)
        odd_re, odd_im = get(group, k, slot, 1)
        re = jnp.concatenate([even_re + odd_re, even_re - odd_re], axis=1)
        im = jnp.concatenate([even_im + odd_im, even_im - odd_im], axis=1)
        return re.astype(jnp.bfloat16), im.astype(jnp.bfloat16)

    def analyse(group):
        rows = pl.ds(group * chunk, chunk)

        def one(signal):
            bins = half_spectrum(
                [in_ref[p, signal, rows, :].astype(jnp.float32) for p in range(blocks)]
            )
            for k, (re, im) in enumerate(bins):
                cos, sin = twid_ref[0, k : k + 1, :], twid_ref[1, k : k + 1, :]
                if k == 0:
                    put_halves(group, k, signal, re, jnp.zeros_like(re))
                elif im is None:
                    put_halves(group, k, signal, re * cos, -(re * sin))
                else:
                    put_halves(group, k, signal, re * cos + im * sin, im * cos - re * sin)

        each(signals, one)

    def transform(group, table_ref):
        for part in range(2):
            lanes = slice(part * block_len, (part + 1) * block_len)
            spec_ref[group, :, :, :, lanes] = jnp.dot(
                rows_ref[group, :, :, :, lanes].reshape(bins_count * signals * chunk, block_len),
                table_ref[part],
                preferred_element_type=jnp.float32,
            ).reshape(bins_count, signals, chunk, block_len)

    def forward(group):
        if group == 0:
            fwd_copy.wait()
        transform(group, fwd_ref)

    def combine(group):
        def product(k, part):
            (prod_re, prod_im), (kern_re, kern_im), (grad_re, grad_im) = [
                [value.astype(jnp.bfloat16) for value in get(group, k, slot, part)]
                for slot in range(3)
            ]
            conv_re = prod_re * kern_re - prod_im * kern_im
            conv_im = prod_re * kern_im + prod_im * kern_re
            back_re = grad_re * kern_re + grad_im * kern_im
            back_im = grad_im * kern_re - grad_re * kern_im
            filt_re = grad_re * prod_re + grad_im * prod_im
            filt_im = grad_im * prod_re - grad_re * prod_im
            put(group, k, 0, part, conv_re, conv_im)
            put(group, k, 1, part, back_re, back_im)
            put(group, k, 2, part, filt_re, filt_im)

        def one(k):
            product(k, 0)
            product(k, 1)

        each(bins_count, one)

    def inverse(group):
        if group == 0:
            inv_copy.wait()
            back_copy.wait()
        transform(group, inv_ref)

    def synthesise(group):
        rows = pl.ds(group * chunk, chunk)

        def one(signal):
            bins = []
            for k in range(bins_count):
                re, im = get_halves(group, k, signal)
                cos, sin = back_ref[0, k], back_ref[1, k]
                if k == 0:
                    bins.append((re * cos, None))
                elif k == blocks:
                    bins.append((re * cos - im * sin, None))
                else:
                    bins.append((re * cos - im * sin, im * cos + re * sin))
            for p, value in enumerate(half_spectrum_adjoint(bins)):
                in_ref[p, signal, rows, :] = value

        each(signals, one)

    stages = (analyse, forward, combine, inverse, synthesise)
    for step in range(groups + len(stages) - 1):
        for depth, stage in reversed(list(enumerate(stages))):
            if 0 <= step - depth < groups:
                stage(step - depth)
    for distance, out_ref in by_distance(out_refs):
        out_ref[...] = in_ref[me ^ distance]
    for copy in held_copies:
        copy.wait()


def term(lhs_ref, weight_refs, group):
    part = weight_refs[0].shape[0] // lax.axis_size("tp")
    rows = pl.ds(pl.multiple_of(group * part, part), part)
    dims = (((1,), (1,)), ((), ()))
    total = None
    for slot, weight_ref in enumerate(weight_refs):
        piece = lax.dot_general(
            lhs_ref[slot], weight_ref[rows, :], dims, preferred_element_type=jnp.float32
        )
        total = piece if total is None else total + piece
    return total


def natural(back_refs, turn_ref, slots):
    blocks, _, channels, block_len = turn_ref.shape
    me = lax.axis_index("ctx")
    for distance, ref in by_distance(back_refs):
        for i, slot in enumerate(slots):
            turn_ref[me ^ distance, i] = ref[slot]
    return [
        turn_ref[:, i].reshape(blocks * channels, block_len).astype(jnp.float32).T
        for i in range(len(slots))
    ]


def mate_kernel(*refs):
    blocks = lax.axis_size("ctx")
    back_refs, (key_ref, value_ref, grad_ref) = refs[:blocks], refs[blocks : blocks + 3]
    weight_refs = refs[blocks + 3 : blocks + 6]
    lhs_ref, out_ref, turn_ref = refs[blocks + 6 :]
    conv_out, grad_product = natural(back_refs, turn_ref, (0, 1))
    lhs_ref[0] = (grad_product * value_ref[...].astype(jnp.float32)).astype(jnp.bfloat16)
    lhs_ref[1] = (conv_out * grad_ref[...].astype(jnp.float32)).astype(jnp.bfloat16)
    lhs_ref[2] = (grad_product * key_ref[...].astype(jnp.float32)).astype(jnp.bfloat16)
    out_ref[...] = term(lhs_ref, weight_refs, lax.axis_index("tp") ^ 3).astype(jnp.bfloat16)


def far_kernel(lhs_ref, wk_ref, wq_ref, wv_ref, far_ref, near_ref):
    group = lax.axis_index("tp")
    far_ref[...] = term(lhs_ref, (wk_ref, wq_ref, wv_ref), group ^ 2)
    near_ref[...] = term(lhs_ref, (wk_ref, wq_ref, wv_ref), group ^ 1).astype(jnp.bfloat16)


def own_kernel(lhs_ref, wk_ref, wq_ref, wv_ref, own_ref):
    own_ref[...] = term(lhs_ref, (wk_ref, wq_ref, wv_ref), lax.axis_index("tp"))


def turn_kernel(*refs):
    back_refs, (out_ref, turn_ref) = refs[:-2], refs[-2:]
    out_ref[...] = natural(back_refs, turn_ref, (2,))[0].astype(jnp.bfloat16)


def exchange(block, axis, distance):
    pairs = [(i, i ^ distance) for i in range(lax.axis_size(axis))]
    return lax.ppermute(block, axis, pairs)


def swap(pieces):
    return [
        exchange(piece, "ctx", distance) if distance else piece
        for distance, piece in by_distance(pieces)
    ]


def per_device(key_act, value_act, query_act, grad_out, long_filter, w_key, w_query, w_value):
    blocks = lax.axis_size("ctx")
    groups = lax.axis_size("tp")
    block_len, width = key_act.shape
    channels = width // blocks
    chunk = min(channels, 16)
    seq_len = blocks * block_len
    part = w_key.shape[0] // groups
    block_cost = pl.CostEstimate(
        flops=4 * block_len * 3 * width * part, bytes_accessed=1 << 22, transcendentals=0
    )

    def arrays(count, *shape, dtype=jnp.bfloat16):
        return [pltpu.VMEM(shape, dtype)] * count

    sent = pl.pallas_call(
        gate_kernel,
        in_specs=[HBM] * 5,
        out_shape=arrays(blocks, 3, channels, block_len),
        scratch_shapes=[
            pltpu.VMEM((blocks, 3, channels, block_len), jnp.bfloat16),
            pltpu.VMEM((5, block_len, width), jnp.bfloat16),
            pltpu.SemaphoreType.DMA((5,)),
        ],
        compiler_params=compiler_params(12),
        name="gate",
    )(*in_hbm(long_filter, key_act, value_act, query_act, grad_out))
    moved = swap(sent)

    forward, inverse, twiddle, untwiddle = dft_tables(
        blocks, block_len, 1.0 / (math.sqrt(seq_len) * 2 * seq_len), chunk
    )
    tables = (twiddle, untwiddle, forward, inverse)
    held = (key_act, value_act, grad_out, w_key, w_query, w_value)
    results = pl.pallas_call(
        conv_kernel,
        in_specs=[VMEM] * blocks + [HBM] * 10,
        out_shape=arrays(blocks, 3, channels, block_len)
        + [pltpu.VMEM(array.shape, array.dtype) for array in held],
        scratch_shapes=[
            pltpu.VMEM((blocks, 3, channels, block_len), jnp.bfloat16),
            pltpu.VMEM((channels // chunk, blocks + 1, 3, chunk, 2 * block_len), jnp.bfloat16),
            pltpu.VMEM((channels // chunk, blocks + 1, 3, chunk, 2 * block_len), jnp.float32),
            *[pltpu.VMEM(array.shape, array.dtype) for array in tables],
            pltpu.SemaphoreType.DMA((10,)),
        ],
        compiler_params=compiler_params(28),
        name="conv",
    )(*moved, *in_hbm(*tables, *held))
    back, held = swap(results[:blocks]), results[blocks:]
    weights = held[3:]
    lhs, to_mate = pl.pallas_call(
        mate_kernel,
        in_specs=[VMEM] * (blocks + 6),
        out_shape=arrays(1, 3, block_len, width) + arrays(1, block_len, part),
        scratch_shapes=[pltpu.VMEM((blocks, 2, channels, block_len), jnp.bfloat16)],
        compiler_params=compiler_params(16),
        cost_estimate=block_cost,
        name="mate",
    )(*back, *held)
    from_mate = exchange(to_mate, "tp", 1)
    far, near = pl.pallas_call(
        far_kernel,
        in_specs=[VMEM] * 4,
        out_shape=arrays(1, block_len, part, dtype=jnp.float32) + arrays(1, block_len, part),
        compiler_params=compiler_params(16),
        cost_estimate=block_cost,
        name="far",
    )(lhs, *weights)
    far = (far + from_mate.astype(jnp.float32)).astype(jnp.bfloat16)
    far, near, lhs, back = lax.optimization_barrier((far, near, lhs, back))
    from_far = exchange(far, "tp", 2)
    from_near = exchange(near, "tp", 1)
    grad_filter = pl.pallas_call(
        turn_kernel,
        in_specs=[VMEM] * blocks,
        out_shape=jax.ShapeDtypeStruct((block_len, width), jnp.bfloat16),
        scratch_shapes=[pltpu.VMEM((blocks, 1, channels, block_len), jnp.bfloat16)],
        compiler_params=compiler_params(16),
        cost_estimate=block_cost,
        name="turn",
    )(*back)
    own = pl.pallas_call(
        own_kernel,
        in_specs=[VMEM] * 4,
        out_shape=arrays(1, block_len, part, dtype=jnp.float32)[0],
        compiler_params=compiler_params(16),
        cost_estimate=block_cost,
        name="own",
    )(lhs, *weights)
    total = from_far.astype(jnp.float32) + from_near.astype(jnp.float32) + own
    grad_input = total.astype(jnp.bfloat16)
    return (grad_input, grad_filter)


def solution(mesh):
    placed = (P("ctx", "tp"),) * 5 + (P(None, "tp"),) * 3
    return jax.shard_map(
        per_device,
        mesh=mesh,
        in_specs=placed,
        out_specs=(P("ctx", "tp"), P("ctx", "tp")),
        check_vma=False,
    )
```

```python
import math

import jax
import jax.numpy as jnp
import numpy as np
from jax import lax
from jax.experimental import pallas as pl
from jax.experimental.pallas import tpu as pltpu
from jax.sharding import PartitionSpec as P


def compiler_params(mib):
    return pltpu.CompilerParams(vmem_limit_bytes=int(mib * 1024 * 1024))


def dft_tables(blocks, block_len, scale, rows_count):
    index, half = np.arange(block_len), np.arange(block_len // 2)
    bins = 2 * half[None, :] + np.arange(2)[:, None]
    angle = 2.0 * np.pi * (half[None, :, None] * bins[:, None, :] % block_len) / block_len
    cos, sin = np.cos(angle), np.sin(angle)
    forward = np.block([[cos, -sin], [sin, cos]])
    inverse = forward.transpose(0, 2, 1)
    rows = np.arange(blocks + 1)
    phase = 2.0 * np.pi * np.outer(rows, index) / (2 * blocks * block_len)
    weight = np.where((rows == 0) | (rows == blocks), 1.0, 2.0)[:, None] * scale
    twiddle = np.stack([np.cos(phase), np.sin(phase)])
    untwiddle = np.repeat((weight * twiddle)[:, :, None, :], rows_count, axis=2)
    return (
        jnp.asarray(forward, jnp.bfloat16),
        jnp.asarray(inverse, jnp.bfloat16),
        jnp.asarray(twiddle, jnp.float32),
        jnp.asarray(untwiddle, jnp.bfloat16),
    )


def half_spectrum(values):
    size = len(values)
    if size == 1:
        return [(values[0], None), (values[0], None)]
    even, odd = half_spectrum(values[0::2]), half_spectrum(values[1::2])
    half = size // 2
    bins = [None] * (size + 1)
    bins[0] = (even[0][0] + odd[0][0], None)
    bins[size] = (even[0][0] - odd[0][0], None)
    bins[half] = (even[half][0], -odd[half][0])
    for k in range(1, half):
        angle = math.pi * k / size
        cos, sin = math.cos(angle), math.sin(angle)
        even_re, even_im = even[k]
        odd_re, odd_im = odd[k]
        if 2 * k == half:
            turn_re = cos * (odd_re + odd_im)
            turn_im = cos * (odd_im - odd_re)
        else:
            turn_re = cos * odd_re + sin * odd_im
            turn_im = cos * odd_im - sin * odd_re
        bins[k] = (even_re + turn_re, even_im + turn_im)
        bins[size - k] = (even_re - turn_re, turn_im - even_im)
    return bins


def half_spectrum_adjoint(bins):
    size = len(bins) - 1
    if size == 1:
        return [bins[0][0] + bins[1][0]]
    half = size // 2
    even, odd = [None] * (half + 1), [None] * (half + 1)
    even[0] = (bins[0][0] + bins[size][0], None)
    odd[0] = (bins[0][0] - bins[size][0], None)
    even[half] = (bins[half][0], None)
    odd[half] = (-bins[half][1], None)
    for k in range(1, half):
        angle = math.pi * k / size
        cos, sin = math.cos(angle), math.sin(angle)
        low_re, low_im = bins[k]
        high_re, high_im = bins[size - k]
        even[k] = (low_re + high_re, low_im - high_im)
        turn_re, turn_im = low_re - high_re, low_im + high_im
        if 2 * k == half:
            odd[k] = (cos * (turn_re - turn_im), cos * (turn_re + turn_im))
        else:
            odd[k] = (cos * turn_re - sin * turn_im, cos * turn_im + sin * turn_re)
    values = [None] * size
    values[0::2] = half_spectrum_adjoint(even)
    values[1::2] = half_spectrum_adjoint(odd)
    return values


HBM = pl.BlockSpec(memory_space=pltpu.HBM)
VMEM = pl.BlockSpec(memory_space=pltpu.VMEM)


def in_hbm(*arrays):
    return [pltpu.with_memory_space_constraint(array, pltpu.HBM) for array in arrays]


def by_distance(pieces):
    last = len(pieces) - 1
    order = [1 + i // 2 if i % 2 == 0 else last - i // 2 for i in range(last)]
    return zip([*order, 0], pieces)


def fetch(sources, targets, sems):
    copies = [
        pltpu.make_async_copy(source, target, sems.at[i])
        for i, (source, target) in enumerate(zip(sources, targets))
    ]
    for copy in copies:
        copy.start()
    return copies


def gate_kernel(*refs):
    sources, refs = refs[:5], refs[5:]
    out_refs, (turn_ref, held_ref, sems) = refs[:-3], refs[-3:]
    blocks, _, channels, block_len = turn_ref.shape
    filter_copy, *copies = fetch(sources, [held_ref.at[i] for i in range(5)], sems)

    def put(slot, wide):
        turned = wide.T.astype(jnp.bfloat16)
        turn_ref[:, slot] = turned.reshape(blocks, channels, block_len)

    filter_copy.wait()
    put(1, held_ref[0].astype(jnp.float32))
    for copy in copies[:2]:
        copy.wait()
    put(0, held_ref[1].astype(jnp.float32) * held_ref[2].astype(jnp.float32))
    for copy in copies[2:]:
        copy.wait()
    put(2, held_ref[3].astype(jnp.float32) * held_ref[4].astype(jnp.float32))
    me = lax.axis_index("ctx")
    for distance, out_ref in by_distance(out_refs):
        out_ref[...] = turn_ref[me ^ distance]


def conv_kernel(*refs):
    blocks = lax.axis_size("ctx")
    in_refs, sources, refs = refs[:blocks], refs[blocks : blocks + 10], refs[blocks + 10 :]
    out_refs, held_refs = refs[:blocks], refs[blocks : blocks + 6]
    in_ref, rows_ref, spec_ref, twid_ref, back_ref, fwd_ref, inv_ref, sems = refs[blocks + 6 :]
    twid_copy, back_copy, fwd_copy, inv_copy, *held_copies = fetch(
        sources, (twid_ref, back_ref, fwd_ref, inv_ref, *held_refs), sems
    )
    groups, bins_count, signals, chunk, _ = rows_ref.shape
    block_len = in_ref.shape[-1]
    me = lax.axis_index("ctx")
    for distance, ref in by_distance(in_refs):
        in_ref[me ^ distance] = ref[...]
    twid_copy.wait()

    def each(count, body):
        if blocks <= 8:
            for i in range(count):
                body(i)
        else:
            pl.loop(0, count)(body)

    half = block_len // 2

    def put(group, k, slot, part, re, im):
        rows_ref[group, k, slot, :, part * block_len : part * block_len + half] = re.astype(
            jnp.bfloat16
        )
        rows_ref[group, k, slot, :, part * block_len + half : (part + 1) * block_len] = im.astype(
            jnp.bfloat16
        )

    def get(group, k, slot, part):
        re = spec_ref[group, k, slot, :, part * block_len : part * block_len + half]
        im = spec_ref[group, k, slot, :, part * block_len + half : (part + 1) * block_len]
        return re, im

    def put_halves(group, k, slot, re, im):
        put(group, k, slot, 0, re[:, :half] + re[:, half:], im[:, :half] + im[:, half:])
        put(group, k, slot, 1, re[:, :half] - re[:, half:], im[:, :half] - im[:, half:])

    def get_halves(group, k, slot):
        even_re, even_im = get(group, k, slot, 0)
        odd_re, odd_im = get(group, k, slot, 1)
        re = jnp.concatenate([even_re + odd_re, even_re - odd_re], axis=1)
        im = jnp.concatenate([even_im + odd_im, even_im - odd_im], axis=1)
        return re.astype(jnp.bfloat16), im.astype(jnp.bfloat16)

    def analyse(group):
        rows = pl.ds(group * chunk, chunk)

        def one(signal):
            bins = half_spectrum(
                [in_ref[p, signal, rows, :].astype(jnp.float32) for p in range(blocks)]
            )
            for k, (re, im) in enumerate(bins):
                cos, sin = twid_ref[0, k : k + 1, :], twid_ref[1, k : k + 1, :]
                if k == 0:
                    put_halves(group, k, signal, re, jnp.zeros_like(re))
                elif im is None:
                    put_halves(group, k, signal, re * cos, -(re * sin))
                else:
                    put_halves(group, k, signal, re * cos + im * sin, im * cos - re * sin)

        each(signals, one)

    def transform(group, table_ref):
        for part in range(2):
            lanes = slice(part * block_len, (part + 1) * block_len)
            spec_ref[group, :, :, :, lanes] = jnp.dot(
                rows_ref[group, :, :, :, lanes].reshape(bins_count * signals * chunk, block_len),
                table_ref[part],
                preferred_element_type=jnp.float32,
            ).reshape(bins_count, signals, chunk, block_len)

    def forward(group):
        if group == 0:
            fwd_copy.wait()
        transform(group, fwd_ref)

    def combine(group):
        def product(k, part):
            (prod_re, prod_im), (kern_re, kern_im), (grad_re, grad_im) = [
                [value.astype(jnp.bfloat16) for value in get(group, k, slot, part)]
                for slot in range(3)
            ]
            conv_re = prod_re * kern_re - prod_im * kern_im
            conv_im = prod_re * kern_im + prod_im * kern_re
            back_re = grad_re * kern_re + grad_im * kern_im
            back_im = grad_im * kern_re - grad_re * kern_im
            filt_re = grad_re * prod_re + grad_im * prod_im
            filt_im = grad_im * prod_re - grad_re * prod_im
            put(group, k, 0, part, conv_re, conv_im)
            put(group, k, 1, part, back_re, back_im)
            put(group, k, 2, part, filt_re, filt_im)

        def one(k):
            product(k, 0)
            product(k, 1)

        each(bins_count, one)

    def inverse(group):
        if group == 0:
            inv_copy.wait()
            back_copy.wait()
        transform(group, inv_ref)

    def synthesise(group):
        rows = pl.ds(group * chunk, chunk)

        def one(signal):
            bins = []
            for k in range(bins_count):
                re, im = get_halves(group, k, signal)
                cos, sin = back_ref[0, k], back_ref[1, k]
                if k == 0:
                    bins.append((re * cos, None))
                elif k == blocks:
                    bins.append((re * cos - im * sin, None))
                else:
                    bins.append((re * cos - im * sin, im * cos + re * sin))
            for p, value in enumerate(half_spectrum_adjoint(bins)):
                in_ref[p, signal, rows, :] = value

        each(signals, one)

    stages = (analyse, forward, combine, inverse, synthesise)
    for step in range(groups + len(stages) - 1):
        for depth, stage in reversed(list(enumerate(stages))):
            if 0 <= step - depth < groups:
                stage(step - depth)
    for distance, out_ref in by_distance(out_refs):
        out_ref[...] = in_ref[me ^ distance]
    for copy in held_copies:
        copy.wait()


def term(lhs_ref, weight_refs, group):
    part = weight_refs[0].shape[0] // lax.axis_size("tp")
    rows = pl.ds(pl.multiple_of(group * part, part), part)
    dims = (((1,), (1,)), ((), ()))
    total = None
    for slot, weight_ref in enumerate(weight_refs):
        piece = lax.dot_general(
            lhs_ref[slot], weight_ref[rows, :], dims, preferred_element_type=jnp.float32
        )
        total = piece if total is None else total + piece
    return total


def natural(back_refs, turn_ref, slots):
    blocks, _, channels, block_len = turn_ref.shape
    me = lax.axis_index("ctx")
    for distance, ref in by_distance(back_refs):
        for i, slot in enumerate(slots):
            turn_ref[me ^ distance, i] = ref[slot]
    return [
        turn_ref[:, i].reshape(blocks * channels, block_len).astype(jnp.float32).T
        for i in range(len(slots))
    ]


def mate_kernel(*refs):
    blocks = lax.axis_size("ctx")
    back_refs, (key_ref, value_ref, grad_ref) = refs[:blocks], refs[blocks : blocks + 3]
    weight_refs = refs[blocks + 3 : blocks + 6]
    lhs_ref, out_ref, turn_ref = refs[blocks + 6 :]
    conv_out, grad_product = natural(back_refs, turn_ref, (0, 1))
    lhs_ref[0] = (grad_product * value_ref[...].astype(jnp.float32)).astype(jnp.bfloat16)
    lhs_ref[1] = (conv_out * grad_ref[...].astype(jnp.float32)).astype(jnp.bfloat16)
    lhs_ref[2] = (grad_product * key_ref[...].astype(jnp.float32)).astype(jnp.bfloat16)
    out_ref[...] = term(lhs_ref, weight_refs, lax.axis_index("tp") ^ 3).astype(jnp.bfloat16)


def far_kernel(lhs_ref, wk_ref, wq_ref, wv_ref, far_ref, near_ref):
    group = lax.axis_index("tp")
    far_ref[...] = term(lhs_ref, (wk_ref, wq_ref, wv_ref), group ^ 2)
    near_ref[...] = term(lhs_ref, (wk_ref, wq_ref, wv_ref), group ^ 1).astype(jnp.bfloat16)


def own_kernel(lhs_ref, wk_ref, wq_ref, wv_ref, own_ref):
    own_ref[...] = term(lhs_ref, (wk_ref, wq_ref, wv_ref), lax.axis_index("tp"))


def turn_kernel(*refs):
    back_refs, (out_ref, turn_ref) = refs[:-2], refs[-2:]
    out_ref[...] = natural(back_refs, turn_ref, (2,))[0].astype(jnp.bfloat16)


def exchange(block, axis, distance):
    pairs = [(i, i ^ distance) for i in range(lax.axis_size(axis))]
    return lax.ppermute(block, axis, pairs)


def swap(pieces):
    return [
        exchange(piece, "ctx", distance) if distance else piece
        for distance, piece in by_distance(pieces)
    ]


def per_device(key_act, value_act, query_act, grad_out, long_filter, w_key, w_query, w_value):
    blocks = lax.axis_size("ctx")
    groups = lax.axis_size("tp")
    block_len, width = key_act.shape
    channels = width // blocks
    chunk = min(channels, 16)
    seq_len = blocks * block_len
    part = w_key.shape[0] // groups
    block_cost = pl.CostEstimate(
        flops=4 * block_len * 3 * width * part, bytes_accessed=1 << 22, transcendentals=0
    )

    def arrays(count, *shape, dtype=jnp.bfloat16):
        return [pltpu.VMEM(shape, dtype)] * count

    sent = pl.pallas_call(
        gate_kernel,
        in_specs=[HBM] * 5,
        out_shape=arrays(blocks, 3, channels, block_len),
        scratch_shapes=[
            pltpu.VMEM((blocks, 3, channels, block_len), jnp.bfloat16),
            pltpu.VMEM((5, block_len, width), jnp.bfloat16),
            pltpu.SemaphoreType.DMA((5,)),
        ],
        compiler_params=compiler_params(12),
        name="gate",
    )(*in_hbm(long_filter, key_act, value_act, query_act, grad_out))
    moved = swap(sent)

    forward, inverse, twiddle, untwiddle = dft_tables(
        blocks, block_len, 1.0 / (math.sqrt(seq_len) * 2 * seq_len), chunk
    )
    tables = (twiddle, untwiddle, forward, inverse)
    held = (key_act, value_act, grad_out, w_key, w_query, w_value)
    results = pl.pallas_call(
        conv_kernel,
        in_specs=[VMEM] * blocks + [HBM] * 10,
        out_shape=arrays(blocks, 3, channels, block_len)
        + [pltpu.VMEM(array.shape, array.dtype) for array in held],
        scratch_shapes=[
            pltpu.VMEM((blocks, 3, channels, block_len), jnp.bfloat16),
            pltpu.VMEM((channels // chunk, blocks + 1, 3, chunk, 2 * block_len), jnp.bfloat16),
            pltpu.VMEM((channels // chunk, blocks + 1, 3, chunk, 2 * block_len), jnp.float32),
            *[pltpu.VMEM(array.shape, array.dtype) for array in tables],
            pltpu.SemaphoreType.DMA((10,)),
        ],
        compiler_params=compiler_params(28),
        name="conv",
    )(*moved, *in_hbm(*tables, *held))
    back, held = swap(results[:blocks]), results[blocks:]
    weights = held[3:]
    lhs, to_mate = pl.pallas_call(
        mate_kernel,
        in_specs=[VMEM] * (blocks + 6),
        out_shape=arrays(1, 3, block_len, width) + arrays(1, block_len, part),
        scratch_shapes=[pltpu.VMEM((blocks, 2, channels, block_len), jnp.bfloat16)],
        compiler_params=compiler_params(16),
        cost_estimate=block_cost,
        name="mate",
    )(*back, *held)
    from_mate = exchange(to_mate, "tp", 1)
    far, near = pl.pallas_call(
        far_kernel,
        in_specs=[VMEM] * 4,
        out_shape=arrays(1, block_len, part, dtype=jnp.float32) + arrays(1, block_len, part),
        compiler_params=compiler_params(16),
        cost_estimate=block_cost,
        name="far",
    )(lhs, *weights)
    far = (far + from_mate.astype(jnp.float32)).astype(jnp.bfloat16)
    far, near, lhs, back = lax.optimization_barrier((far, near, lhs, back))
    from_far = exchange(far, "tp", 2)
    from_near = exchange(near, "tp", 1)
    grad_filter = pl.pallas_call(
        turn_kernel,
        in_specs=[VMEM] * blocks,
        out_shape=jax.ShapeDtypeStruct((block_len, width), jnp.bfloat16),
        scratch_shapes=[pltpu.VMEM((blocks, 1, channels, block_len), jnp.bfloat16)],
        compiler_params=compiler_params(16),
        cost_estimate=block_cost,
        name="turn",
    )(*back)
    own = pl.pallas_call(
        own_kernel,
        in_specs=[VMEM] * 4,
        out_shape=arrays(1, block_len, part, dtype=jnp.float32)[0],
        compiler_params=compiler_params(16),
        cost_estimate=block_cost,
        name="own",
    )(lhs, *weights)
    total = from_far.astype(jnp.float32) + from_near.astype(jnp.float32) + own
    grad_input = total.astype(jnp.bfloat16)
    return (grad_input, grad_filter)


def solution(mesh):
    placed = (P("ctx", "tp"),) * 5 + (P(None, "tp"),) * 3
    return jax.shard_map(
        per_device,
        mesh=mesh,
        in_specs=placed,
        out_specs=(P("ctx", "tp"), P("ctx", "tp")),
        check_vma=False,
    )
```

```python
import math

import jax
import jax.numpy as jnp
import numpy as np
from jax import lax
from jax.experimental import pallas as pl
from jax.experimental.pallas import tpu as pltpu
from jax.sharding import PartitionSpec as P


def compiler_params(mib):
    return pltpu.CompilerParams(vmem_limit_bytes=int(mib * 1024 * 1024))


def dft_tables(blocks, block_len, scale, rows_count):
    index, half = np.arange(block_len), np.arange(block_len // 2)
    bins = 2 * half[None, :] + np.arange(2)[:, None]
    angle = 2.0 * np.pi * (half[None, :, None] * bins[:, None, :] % block_len) / block_len
    cos, sin = np.cos(angle), np.sin(angle)
    forward = np.block([[cos, -sin], [sin, cos]])
    inverse = forward.transpose(0, 2, 1)
    rows = np.arange(blocks + 1)
    phase = 2.0 * np.pi * np.outer(rows, index) / (2 * blocks * block_len)
    weight = np.where((rows == 0) | (rows == blocks), 1.0, 2.0)[:, None] * scale
    twiddle = np.stack([np.cos(phase), np.sin(phase)])
    untwiddle = np.repeat((weight * twiddle)[:, :, None, :], rows_count, axis=2)
    return (
        jnp.asarray(forward, jnp.bfloat16),
        jnp.asarray(inverse, jnp.bfloat16),
        jnp.asarray(twiddle, jnp.float32),
        jnp.asarray(untwiddle, jnp.bfloat16),
    )


def half_spectrum(values):
    size = len(values)
    if size == 1:
        return [(values[0], None), (values[0], None)]
    even, odd = half_spectrum(values[0::2]), half_spectrum(values[1::2])
    half = size // 2
    bins = [None] * (size + 1)
    bins[0] = (even[0][0] + odd[0][0], None)
    bins[size] = (even[0][0] - odd[0][0], None)
    bins[half] = (even[half][0], -odd[half][0])
    for k in range(1, half):
        angle = math.pi * k / size
        cos, sin = math.cos(angle), math.sin(angle)
        even_re, even_im = even[k]
        odd_re, odd_im = odd[k]
        if 2 * k == half:
            turn_re = cos * (odd_re + odd_im)
            turn_im = cos * (odd_im - odd_re)
        else:
            turn_re = cos * odd_re + sin * odd_im
            turn_im = cos * odd_im - sin * odd_re
        bins[k] = (even_re + turn_re, even_im + turn_im)
        bins[size - k] = (even_re - turn_re, turn_im - even_im)
    return bins


def half_spectrum_adjoint(bins):
    size = len(bins) - 1
    if size == 1:
        return [bins[0][0] + bins[1][0]]
    half = size // 2
    even, odd = [None] * (half + 1), [None] * (half + 1)
    even[0] = (bins[0][0] + bins[size][0], None)
    odd[0] = (bins[0][0] - bins[size][0], None)
    even[half] = (bins[half][0], None)
    odd[half] = (-bins[half][1], None)
    for k in range(1, half):
        angle = math.pi * k / size
        cos, sin = math.cos(angle), math.sin(angle)
        low_re, low_im = bins[k]
        high_re, high_im = bins[size - k]
        even[k] = (low_re + high_re, low_im - high_im)
        turn_re, turn_im = low_re - high_re, low_im + high_im
        if 2 * k == half:
            odd[k] = (cos * (turn_re - turn_im), cos * (turn_re + turn_im))
        else:
            odd[k] = (cos * turn_re - sin * turn_im, cos * turn_im + sin * turn_re)
    values = [None] * size
    values[0::2] = half_spectrum_adjoint(even)
    values[1::2] = half_spectrum_adjoint(odd)
    return values


HBM = pl.BlockSpec(memory_space=pltpu.HBM)
VMEM = pl.BlockSpec(memory_space=pltpu.VMEM)


def in_hbm(*arrays):
    return [pltpu.with_memory_space_constraint(array, pltpu.HBM) for array in arrays]


def by_distance(pieces):
    blocks, last = len(pieces), len(pieces) - 1
    far, near = list(range(last, blocks // 2 - 1, -1)), list(range(1, blocks // 2))
    far.insert(0, far.pop(len(far) // 2))
    order = [far[i // 2] if i % 2 == 0 else near[i // 2] for i in range(last)]
    return zip([*order, 0], pieces)


def fetch(sources, targets, sems):
    copies = [
        pltpu.make_async_copy(source, target, sems.at[i])
        for i, (source, target) in enumerate(zip(sources, targets))
    ]
    for copy in copies:
        copy.start()
    return copies


def gate_kernel(*refs):
    sources, refs = refs[:5], refs[5:]
    out_refs, (turn_ref, held_ref, sems) = refs[:-3], refs[-3:]
    blocks, _, channels, block_len = turn_ref.shape
    filter_copy, *copies = fetch(sources, [held_ref.at[i] for i in range(5)], sems)

    def put(slot, wide):
        turned = wide.T.astype(jnp.bfloat16)
        turn_ref[:, slot] = turned.reshape(blocks, channels, block_len)

    filter_copy.wait()
    put(1, held_ref[0].astype(jnp.float32))
    for copy in copies[:2]:
        copy.wait()
    put(0, held_ref[1].astype(jnp.float32) * held_ref[2].astype(jnp.float32))
    for copy in copies[2:]:
        copy.wait()
    put(2, held_ref[3].astype(jnp.float32) * held_ref[4].astype(jnp.float32))
    me = lax.axis_index("ctx")
    for distance, out_ref in by_distance(out_refs):
        out_ref[...] = turn_ref[me ^ distance]


def conv_kernel(*refs):
    blocks = lax.axis_size("ctx")
    in_refs, sources, refs = refs[:blocks], refs[blocks : blocks + 10], refs[blocks + 10 :]
    out_refs, held_refs = refs[:blocks], refs[blocks : blocks + 6]
    in_ref, rows_ref, spec_ref, twid_ref, back_ref, fwd_ref, inv_ref, sems = refs[blocks + 6 :]
    twid_copy, back_copy, fwd_copy, inv_copy, *held_copies = fetch(
        sources, (twid_ref, back_ref, fwd_ref, inv_ref, *held_refs), sems
    )
    groups, bins_count, signals, chunk, _ = rows_ref.shape
    block_len = in_ref.shape[-1]
    me = lax.axis_index("ctx")
    for distance, ref in by_distance(in_refs):
        in_ref[me ^ distance] = ref[...]
    twid_copy.wait()

    def each(count, body):
        if blocks <= 8:
            for i in range(count):
                body(i)
        else:
            pl.loop(0, count)(body)

    half = block_len // 2

    def put(group, k, slot, part, re, im):
        rows_ref[group, k, slot, :, part * block_len : part * block_len + half] = re.astype(
            jnp.bfloat16
        )
        rows_ref[group, k, slot, :, part * block_len + half : (part + 1) * block_len] = im.astype(
            jnp.bfloat16
        )

    def get(group, k, slot, part):
        re = spec_ref[group, k, slot, :, part * block_len : part * block_len + half]
        im = spec_ref[group, k, slot, :, part * block_len + half : (part + 1) * block_len]
        return re, im

    def put_halves(group, k, slot, re, im):
        put(group, k, slot, 0, re[:, :half] + re[:, half:], im[:, :half] + im[:, half:])
        put(group, k, slot, 1, re[:, :half] - re[:, half:], im[:, :half] - im[:, half:])

    def get_halves(group, k, slot):
        even_re, even_im = get(group, k, slot, 0)
        odd_re, odd_im = get(group, k, slot, 1)
        re = jnp.concatenate([even_re + odd_re, even_re - odd_re], axis=1)
        im = jnp.concatenate([even_im + odd_im, even_im - odd_im], axis=1)
        return re.astype(jnp.bfloat16), im.astype(jnp.bfloat16)

    def analyse(group):
        rows = pl.ds(group * chunk, chunk)

        def one(signal):
            bins = half_spectrum(
                [in_ref[p, signal, rows, :].astype(jnp.float32) for p in range(blocks)]
            )
            for k, (re, im) in enumerate(bins):
                cos, sin = twid_ref[0, k : k + 1, :], twid_ref[1, k : k + 1, :]
                if k == 0:
                    put_halves(group, k, signal, re, jnp.zeros_like(re))
                elif im is None:
                    put_halves(group, k, signal, re * cos, -(re * sin))
                else:
                    put_halves(group, k, signal, re * cos + im * sin, im * cos - re * sin)

        each(signals, one)

    def transform(group, table_ref):
        for part in range(2):
            lanes = slice(part * block_len, (part + 1) * block_len)
            spec_ref[group, :, :, :, lanes] = jnp.dot(
                rows_ref[group, :, :, :, lanes].reshape(bins_count * signals * chunk, block_len),
                table_ref[part],
                preferred_element_type=jnp.float32,
            ).reshape(bins_count, signals, chunk, block_len)

    def forward(group):
        if group == 0:
            fwd_copy.wait()
        transform(group, fwd_ref)

    def combine(group):
        def product(k, part):
            (prod_re, prod_im), (kern_re, kern_im), (grad_re, grad_im) = [
                [value.astype(jnp.bfloat16) for value in get(group, k, slot, part)]
                for slot in range(3)
            ]
            conv_re = prod_re * kern_re - prod_im * kern_im
            conv_im = prod_re * kern_im + prod_im * kern_re
            back_re = grad_re * kern_re + grad_im * kern_im
            back_im = grad_im * kern_re - grad_re * kern_im
            filt_re = grad_re * prod_re + grad_im * prod_im
            filt_im = grad_im * prod_re - grad_re * prod_im
            put(group, k, 0, part, conv_re, conv_im)
            put(group, k, 1, part, back_re, back_im)
            put(group, k, 2, part, filt_re, filt_im)

        def one(k):
            product(k, 0)
            product(k, 1)

        each(bins_count, one)

    def inverse(group):
        if group == 0:
            inv_copy.wait()
            back_copy.wait()
        transform(group, inv_ref)

    def synthesise(group):
        rows = pl.ds(group * chunk, chunk)

        def one(signal):
            bins = []
            for k in range(bins_count):
                re, im = get_halves(group, k, signal)
                cos, sin = back_ref[0, k], back_ref[1, k]
                if k == 0:
                    bins.append((re * cos, None))
                elif k == blocks:
                    bins.append((re * cos - im * sin, None))
                else:
                    bins.append((re * cos - im * sin, im * cos + re * sin))
            for p, value in enumerate(half_spectrum_adjoint(bins)):
                in_ref[p, signal, rows, :] = value

        each(signals, one)

    stages = (analyse, forward, combine, inverse, synthesise)
    for step in range(groups + len(stages) - 1):
        for depth, stage in reversed(list(enumerate(stages))):
            if 0 <= step - depth < groups:
                stage(step - depth)
    for distance, out_ref in by_distance(out_refs):
        out_ref[...] = in_ref[me ^ distance]
    for copy in held_copies:
        copy.wait()


def term(lhs_ref, weight_refs, group):
    part = weight_refs[0].shape[0] // lax.axis_size("tp")
    rows = pl.ds(pl.multiple_of(group * part, part), part)
    dims = (((1,), (1,)), ((), ()))
    total = None
    for slot, weight_ref in enumerate(weight_refs):
        piece = lax.dot_general(
            lhs_ref[slot], weight_ref[rows, :], dims, preferred_element_type=jnp.float32
        )
        total = piece if total is None else total + piece
    return total


def natural(back_refs, turn_ref, slots):
    blocks, _, channels, block_len = turn_ref.shape
    me = lax.axis_index("ctx")
    for distance, ref in by_distance(back_refs):
        for i, slot in enumerate(slots):
            turn_ref[me ^ distance, i] = ref[slot]
    return [
        turn_ref[:, i].reshape(blocks * channels, block_len).astype(jnp.float32).T
        for i in range(len(slots))
    ]


def mate_kernel(*refs):
    blocks = lax.axis_size("ctx")
    back_refs, (key_ref, value_ref, grad_ref) = refs[:blocks], refs[blocks : blocks + 3]
    weight_refs = refs[blocks + 3 : blocks + 6]
    lhs_ref, out_ref, turn_ref = refs[blocks + 6 :]
    conv_out, grad_product = natural(back_refs, turn_ref, (0, 1))
    lhs_ref[0] = (grad_product * value_ref[...].astype(jnp.float32)).astype(jnp.bfloat16)
    lhs_ref[1] = (conv_out * grad_ref[...].astype(jnp.float32)).astype(jnp.bfloat16)
    lhs_ref[2] = (grad_product * key_ref[...].astype(jnp.float32)).astype(jnp.bfloat16)
    out_ref[...] = term(lhs_ref, weight_refs, lax.axis_index("tp") ^ 3).astype(jnp.bfloat16)


def far_kernel(lhs_ref, wk_ref, wq_ref, wv_ref, far_ref, near_ref):
    group = lax.axis_index("tp")
    far_ref[...] = term(lhs_ref, (wk_ref, wq_ref, wv_ref), group ^ 2)
    near_ref[...] = term(lhs_ref, (wk_ref, wq_ref, wv_ref), group ^ 1).astype(jnp.bfloat16)


def own_kernel(lhs_ref, wk_ref, wq_ref, wv_ref, own_ref):
    own_ref[...] = term(lhs_ref, (wk_ref, wq_ref, wv_ref), lax.axis_index("tp"))


def turn_kernel(*refs):
    back_refs, (out_ref, turn_ref) = refs[:-2], refs[-2:]
    out_ref[...] = natural(back_refs, turn_ref, (2,))[0].astype(jnp.bfloat16)


def exchange(block, axis, distance):
    pairs = [(i, i ^ distance) for i in range(lax.axis_size(axis))]
    return lax.ppermute(block, axis, pairs)


def swap(pieces):
    return [
        exchange(piece, "ctx", distance) if distance else piece
        for distance, piece in by_distance(pieces)
    ]


def per_device(key_act, value_act, query_act, grad_out, long_filter, w_key, w_query, w_value):
    blocks = lax.axis_size("ctx")
    groups = lax.axis_size("tp")
    block_len, width = key_act.shape
    channels = width // blocks
    chunk = min(channels, 16)
    seq_len = blocks * block_len
    part = w_key.shape[0] // groups
    block_cost = pl.CostEstimate(
        flops=4 * block_len * 3 * width * part, bytes_accessed=1 << 22, transcendentals=0
    )

    def arrays(count, *shape, dtype=jnp.bfloat16):
        return [pltpu.VMEM(shape, dtype)] * count

    sent = pl.pallas_call(
        gate_kernel,
        in_specs=[HBM] * 5,
        out_shape=arrays(blocks, 3, channels, block_len),
        scratch_shapes=[
            pltpu.VMEM((blocks, 3, channels, block_len), jnp.bfloat16),
            pltpu.VMEM((5, block_len, width), jnp.bfloat16),
            pltpu.SemaphoreType.DMA((5,)),
        ],
        compiler_params=compiler_params(12),
        name="gate",
    )(*in_hbm(long_filter, key_act, value_act, query_act, grad_out))
    moved = swap(sent)

    forward, inverse, twiddle, untwiddle = dft_tables(
        blocks, block_len, 1.0 / (math.sqrt(seq_len) * 2 * seq_len), chunk
    )
    tables = (twiddle, untwiddle, forward, inverse)
    held = (key_act, value_act, grad_out, w_key, w_query, w_value)
    results = pl.pallas_call(
        conv_kernel,
        in_specs=[VMEM] * blocks + [HBM] * 10,
        out_shape=arrays(blocks, 3, channels, block_len)
        + [pltpu.VMEM(array.shape, array.dtype) for array in held],
        scratch_shapes=[
            pltpu.VMEM((blocks, 3, channels, block_len), jnp.bfloat16),
            pltpu.VMEM((channels // chunk, blocks + 1, 3, chunk, 2 * block_len), jnp.bfloat16),
            pltpu.VMEM((channels // chunk, blocks + 1, 3, chunk, 2 * block_len), jnp.float32),
            *[pltpu.VMEM(array.shape, array.dtype) for array in tables],
            pltpu.SemaphoreType.DMA((10,)),
        ],
        compiler_params=compiler_params(28),
        name="conv",
    )(*moved, *in_hbm(*tables, *held))
    back, held = swap(results[:blocks]), results[blocks:]
    weights = held[3:]
    lhs, to_mate = pl.pallas_call(
        mate_kernel,
        in_specs=[VMEM] * (blocks + 6),
        out_shape=arrays(1, 3, block_len, width) + arrays(1, block_len, part),
        scratch_shapes=[pltpu.VMEM((blocks, 2, channels, block_len), jnp.bfloat16)],
        compiler_params=compiler_params(16),
        cost_estimate=block_cost,
        name="mate",
    )(*back, *held)
    from_mate = exchange(to_mate, "tp", 1)
    far, near = pl.pallas_call(
        far_kernel,
        in_specs=[VMEM] * 4,
        out_shape=arrays(1, block_len, part, dtype=jnp.float32) + arrays(1, block_len, part),
        compiler_params=compiler_params(16),
        cost_estimate=block_cost,
        name="far",
    )(lhs, *weights)
    far = (far + from_mate.astype(jnp.float32)).astype(jnp.bfloat16)
    far, near, lhs, back = lax.optimization_barrier((far, near, lhs, back))
    from_far = exchange(far, "tp", 2)
    from_near = exchange(near, "tp", 1)
    grad_filter = pl.pallas_call(
        turn_kernel,
        in_specs=[VMEM] * blocks,
        out_shape=jax.ShapeDtypeStruct((block_len, width), jnp.bfloat16),
        scratch_shapes=[pltpu.VMEM((blocks, 1, channels, block_len), jnp.bfloat16)],
        compiler_params=compiler_params(16),
        cost_estimate=block_cost,
        name="turn",
    )(*back)
    own = pl.pallas_call(
        own_kernel,
        in_specs=[VMEM] * 4,
        out_shape=arrays(1, block_len, part, dtype=jnp.float32)[0],
        compiler_params=compiler_params(16),
        cost_estimate=block_cost,
        name="own",
    )(lhs, *weights)
    total = from_far.astype(jnp.float32) + from_near.astype(jnp.float32) + own
    grad_input = total.astype(jnp.bfloat16)
    return (grad_input, grad_filter)


def solution(mesh):
    placed = (P("ctx", "tp"),) * 5 + (P(None, "tp"),) * 3
    return jax.shard_map(
        per_device,
        mesh=mesh,
        in_specs=placed,
        out_specs=(P("ctx", "tp"), P("ctx", "tp")),
        check_vma=False,
    )
```

```python
import math

import jax
import jax.numpy as jnp
import numpy as np
from jax import lax
from jax.experimental import pallas as pl
from jax.experimental.pallas import tpu as pltpu
from jax.sharding import PartitionSpec as P


def compiler_params(mib):
    return pltpu.CompilerParams(vmem_limit_bytes=int(mib * 1024 * 1024))


def dft_tables(blocks, block_len, scale, rows_count):
    index, half = np.arange(block_len), np.arange(block_len // 2)
    bins = 2 * half[None, :] + np.arange(2)[:, None]
    angle = 2.0 * np.pi * (half[None, :, None] * bins[:, None, :] % block_len) / block_len
    cos, sin = np.cos(angle), np.sin(angle)
    forward = np.block([[cos, -sin], [sin, cos]])
    inverse = forward.transpose(0, 2, 1)
    rows = np.arange(blocks + 1)
    phase = 2.0 * np.pi * np.outer(rows, index) / (2 * blocks * block_len)
    weight = np.where((rows == 0) | (rows == blocks), 1.0, 2.0)[:, None] * scale
    twiddle = np.stack([np.cos(phase), np.sin(phase)])
    untwiddle = np.repeat((weight * twiddle)[:, :, None, :], rows_count, axis=2)
    return (
        jnp.asarray(forward, jnp.bfloat16),
        jnp.asarray(inverse, jnp.bfloat16),
        jnp.asarray(twiddle, jnp.float32),
        jnp.asarray(untwiddle, jnp.bfloat16),
    )


def half_spectrum(values):
    size = len(values)
    if size == 1:
        return [(values[0], None), (values[0], None)]
    even, odd = half_spectrum(values[0::2]), half_spectrum(values[1::2])
    half = size // 2
    bins = [None] * (size + 1)
    bins[0] = (even[0][0] + odd[0][0], None)
    bins[size] = (even[0][0] - odd[0][0], None)
    bins[half] = (even[half][0], -odd[half][0])
    for k in range(1, half):
        angle = math.pi * k / size
        cos, sin = math.cos(angle), math.sin(angle)
        even_re, even_im = even[k]
        odd_re, odd_im = odd[k]
        if 2 * k == half:
            turn_re = cos * (odd_re + odd_im)
            turn_im = cos * (odd_im - odd_re)
        else:
            turn_re = cos * odd_re + sin * odd_im
            turn_im = cos * odd_im - sin * odd_re
        bins[k] = (even_re + turn_re, even_im + turn_im)
        bins[size - k] = (even_re - turn_re, turn_im - even_im)
    return bins


def half_spectrum_adjoint(bins):
    size = len(bins) - 1
    if size == 1:
        return [bins[0][0] + bins[1][0]]
    half = size // 2
    even, odd = [None] * (half + 1), [None] * (half + 1)
    even[0] = (bins[0][0] + bins[size][0], None)
    odd[0] = (bins[0][0] - bins[size][0], None)
    even[half] = (bins[half][0], None)
    odd[half] = (-bins[half][1], None)
    for k in range(1, half):
        angle = math.pi * k / size
        cos, sin = math.cos(angle), math.sin(angle)
        low_re, low_im = bins[k]
        high_re, high_im = bins[size - k]
        even[k] = (low_re + high_re, low_im - high_im)
        turn_re, turn_im = low_re - high_re, low_im + high_im
        if 2 * k == half:
            odd[k] = (cos * (turn_re - turn_im), cos * (turn_re + turn_im))
        else:
            odd[k] = (cos * turn_re - sin * turn_im, cos * turn_im + sin * turn_re)
    values = [None] * size
    values[0::2] = half_spectrum_adjoint(even)
    values[1::2] = half_spectrum_adjoint(odd)
    return values


HBM = pl.BlockSpec(memory_space=pltpu.HBM)
VMEM = pl.BlockSpec(memory_space=pltpu.VMEM)


def in_hbm(*arrays):
    return [pltpu.with_memory_space_constraint(array, pltpu.HBM) for array in arrays]


def by_distance(pieces):
    blocks, last = len(pieces), len(pieces) - 1
    middle = [*range(last, 3 * blocks // 4 - 1, -1), *range(blocks // 2, 3 * blocks // 4)]
    order = [middle[i // 2] if i % 2 == 0 else 1 + i // 2 for i in range(last)]
    return zip([*order, 0], pieces)


def fetch(sources, targets, sems):
    copies = [
        pltpu.make_async_copy(source, target, sems.at[i])
        for i, (source, target) in enumerate(zip(sources, targets))
    ]
    for copy in copies:
        copy.start()
    return copies


def gate_kernel(*refs):
    sources, refs = refs[:5], refs[5:]
    out_refs, (turn_ref, held_ref, sems) = refs[:-3], refs[-3:]
    blocks, _, channels, block_len = turn_ref.shape
    filter_copy, *copies = fetch(sources, [held_ref.at[i] for i in range(5)], sems)

    def put(slot, wide):
        turned = wide.T.astype(jnp.bfloat16)
        turn_ref[:, slot] = turned.reshape(blocks, channels, block_len)

    filter_copy.wait()
    put(1, held_ref[0].astype(jnp.float32))
    for copy in copies[:2]:
        copy.wait()
    put(0, held_ref[1].astype(jnp.float32) * held_ref[2].astype(jnp.float32))
    for copy in copies[2:]:
        copy.wait()
    put(2, held_ref[3].astype(jnp.float32) * held_ref[4].astype(jnp.float32))
    me = lax.axis_index("ctx")
    for distance, out_ref in by_distance(out_refs):
        out_ref[...] = turn_ref[me ^ distance]


def conv_kernel(*refs):
    blocks = lax.axis_size("ctx")
    in_refs, sources, refs = refs[:blocks], refs[blocks : blocks + 10], refs[blocks + 10 :]
    out_refs, held_refs = refs[:blocks], refs[blocks : blocks + 6]
    in_ref, rows_ref, spec_ref, twid_ref, back_ref, fwd_ref, inv_ref, sems = refs[blocks + 6 :]
    twid_copy, back_copy, fwd_copy, inv_copy, *held_copies = fetch(
        sources, (twid_ref, back_ref, fwd_ref, inv_ref, *held_refs), sems
    )
    groups, bins_count, signals, chunk, _ = rows_ref.shape
    block_len = in_ref.shape[-1]
    me = lax.axis_index("ctx")
    for distance, ref in by_distance(in_refs):
        in_ref[me ^ distance] = ref[...]
    twid_copy.wait()

    def each(count, body):
        if blocks <= 8:
            for i in range(count):
                body(i)
        else:
            pl.loop(0, count)(body)

    half = block_len // 2

    def put(group, k, slot, part, re, im):
        rows_ref[group, k, slot, :, part * block_len : part * block_len + half] = re.astype(
            jnp.bfloat16
        )
        rows_ref[group, k, slot, :, part * block_len + half : (part + 1) * block_len] = im.astype(
            jnp.bfloat16
        )

    def get(group, k, slot, part):
        re = spec_ref[group, k, slot, :, part * block_len : part * block_len + half]
        im = spec_ref[group, k, slot, :, part * block_len + half : (part + 1) * block_len]
        return re, im

    def put_halves(group, k, slot, re, im):
        put(group, k, slot, 0, re[:, :half] + re[:, half:], im[:, :half] + im[:, half:])
        put(group, k, slot, 1, re[:, :half] - re[:, half:], im[:, :half] - im[:, half:])

    def get_halves(group, k, slot):
        even_re, even_im = get(group, k, slot, 0)
        odd_re, odd_im = get(group, k, slot, 1)
        re = jnp.concatenate([even_re + odd_re, even_re - odd_re], axis=1)
        im = jnp.concatenate([even_im + odd_im, even_im - odd_im], axis=1)
        return re.astype(jnp.bfloat16), im.astype(jnp.bfloat16)

    def analyse(group):
        rows = pl.ds(group * chunk, chunk)

        def one(signal):
            bins = half_spectrum(
                [in_ref[p, signal, rows, :].astype(jnp.float32) for p in range(blocks)]
            )
            for k, (re, im) in enumerate(bins):
                cos, sin = twid_ref[0, k : k + 1, :], twid_ref[1, k : k + 1, :]
                if k == 0:
                    put_halves(group, k, signal, re, jnp.zeros_like(re))
                elif im is None:
                    put_halves(group, k, signal, re * cos, -(re * sin))
                else:
                    put_halves(group, k, signal, re * cos + im * sin, im * cos - re * sin)

        each(signals, one)

    def transform(group, table_ref):
        for part in range(2):
            lanes = slice(part * block_len, (part + 1) * block_len)
            spec_ref[group, :, :, :, lanes] = jnp.dot(
                rows_ref[group, :, :, :, lanes].reshape(bins_count * signals * chunk, block_len),
                table_ref[part],
                preferred_element_type=jnp.float32,
            ).reshape(bins_count, signals, chunk, block_len)

    def forward(group):
        if group == 0:
            fwd_copy.wait()
        transform(group, fwd_ref)

    def combine(group):
        def product(k, part):
            (prod_re, prod_im), (kern_re, kern_im), (grad_re, grad_im) = [
                [value.astype(jnp.bfloat16) for value in get(group, k, slot, part)]
                for slot in range(3)
            ]
            conv_re = prod_re * kern_re - prod_im * kern_im
            conv_im = prod_re * kern_im + prod_im * kern_re
            back_re = grad_re * kern_re + grad_im * kern_im
            back_im = grad_im * kern_re - grad_re * kern_im
            filt_re = grad_re * prod_re + grad_im * prod_im
            filt_im = grad_im * prod_re - grad_re * prod_im
            put(group, k, 0, part, conv_re, conv_im)
            put(group, k, 1, part, back_re, back_im)
            put(group, k, 2, part, filt_re, filt_im)

        def one(k):
            product(k, 0)
            product(k, 1)

        each(bins_count, one)

    def inverse(group):
        if group == 0:
            inv_copy.wait()
            back_copy.wait()
        transform(group, inv_ref)

    def synthesise(group):
        rows = pl.ds(group * chunk, chunk)

        def one(signal):
            bins = []
            for k in range(bins_count):
                re, im = get_halves(group, k, signal)
                cos, sin = back_ref[0, k], back_ref[1, k]
                if k == 0:
                    bins.append((re * cos, None))
                elif k == blocks:
                    bins.append((re * cos - im * sin, None))
                else:
                    bins.append((re * cos - im * sin, im * cos + re * sin))
            for p, value in enumerate(half_spectrum_adjoint(bins)):
                in_ref[p, signal, rows, :] = value

        each(signals, one)

    stages = (analyse, forward, combine, inverse, synthesise)
    for step in range(groups + len(stages) - 1):
        for depth, stage in reversed(list(enumerate(stages))):
            if 0 <= step - depth < groups:
                stage(step - depth)
    for distance, out_ref in by_distance(out_refs):
        out_ref[...] = in_ref[me ^ distance]
    for copy in held_copies:
        copy.wait()


def term(lhs_ref, weight_refs, group):
    part = weight_refs[0].shape[0] // lax.axis_size("tp")
    rows = pl.ds(pl.multiple_of(group * part, part), part)
    dims = (((1,), (1,)), ((), ()))
    total = None
    for slot, weight_ref in enumerate(weight_refs):
        piece = lax.dot_general(
            lhs_ref[slot], weight_ref[rows, :], dims, preferred_element_type=jnp.float32
        )
        total = piece if total is None else total + piece
    return total


def natural(back_refs, turn_ref, slots):
    blocks, _, channels, block_len = turn_ref.shape
    me = lax.axis_index("ctx")
    for distance, ref in by_distance(back_refs):
        for i, slot in enumerate(slots):
            turn_ref[me ^ distance, i] = ref[slot]
    return [
        turn_ref[:, i].reshape(blocks * channels, block_len).astype(jnp.float32).T
        for i in range(len(slots))
    ]


def mate_kernel(*refs):
    blocks = lax.axis_size("ctx")
    back_refs, (key_ref, value_ref, grad_ref) = refs[:blocks], refs[blocks : blocks + 3]
    weight_refs = refs[blocks + 3 : blocks + 6]
    lhs_ref, out_ref, turn_ref = refs[blocks + 6 :]
    conv_out, grad_product = natural(back_refs, turn_ref, (0, 1))
    lhs_ref[0] = (grad_product * value_ref[...].astype(jnp.float32)).astype(jnp.bfloat16)
    lhs_ref[1] = (conv_out * grad_ref[...].astype(jnp.float32)).astype(jnp.bfloat16)
    lhs_ref[2] = (grad_product * key_ref[...].astype(jnp.float32)).astype(jnp.bfloat16)
    out_ref[...] = term(lhs_ref, weight_refs, lax.axis_index("tp") ^ 3).astype(jnp.bfloat16)


def far_kernel(lhs_ref, wk_ref, wq_ref, wv_ref, far_ref, near_ref):
    group = lax.axis_index("tp")
    far_ref[...] = term(lhs_ref, (wk_ref, wq_ref, wv_ref), group ^ 2)
    near_ref[...] = term(lhs_ref, (wk_ref, wq_ref, wv_ref), group ^ 1).astype(jnp.bfloat16)


def own_kernel(lhs_ref, wk_ref, wq_ref, wv_ref, own_ref):
    own_ref[...] = term(lhs_ref, (wk_ref, wq_ref, wv_ref), lax.axis_index("tp"))


def turn_kernel(*refs):
    back_refs, (out_ref, turn_ref) = refs[:-2], refs[-2:]
    out_ref[...] = natural(back_refs, turn_ref, (2,))[0].astype(jnp.bfloat16)


def exchange(block, axis, distance):
    pairs = [(i, i ^ distance) for i in range(lax.axis_size(axis))]
    return lax.ppermute(block, axis, pairs)


def swap(pieces):
    return [
        exchange(piece, "ctx", distance) if distance else piece
        for distance, piece in by_distance(pieces)
    ]


def per_device(key_act, value_act, query_act, grad_out, long_filter, w_key, w_query, w_value):
    blocks = lax.axis_size("ctx")
    groups = lax.axis_size("tp")
    block_len, width = key_act.shape
    channels = width // blocks
    chunk = min(channels, 16)
    seq_len = blocks * block_len
    part = w_key.shape[0] // groups
    block_cost = pl.CostEstimate(
        flops=4 * block_len * 3 * width * part, bytes_accessed=1 << 22, transcendentals=0
    )

    def arrays(count, *shape, dtype=jnp.bfloat16):
        return [pltpu.VMEM(shape, dtype)] * count

    sent = pl.pallas_call(
        gate_kernel,
        in_specs=[HBM] * 5,
        out_shape=arrays(blocks, 3, channels, block_len),
        scratch_shapes=[
            pltpu.VMEM((blocks, 3, channels, block_len), jnp.bfloat16),
            pltpu.VMEM((5, block_len, width), jnp.bfloat16),
            pltpu.SemaphoreType.DMA((5,)),
        ],
        compiler_params=compiler_params(12),
        name="gate",
    )(*in_hbm(long_filter, key_act, value_act, query_act, grad_out))
    moved = swap(sent)

    forward, inverse, twiddle, untwiddle = dft_tables(
        blocks, block_len, 1.0 / (math.sqrt(seq_len) * 2 * seq_len), chunk
    )
    tables = (twiddle, untwiddle, forward, inverse)
    held = (key_act, value_act, grad_out, w_key, w_query, w_value)
    results = pl.pallas_call(
        conv_kernel,
        in_specs=[VMEM] * blocks + [HBM] * 10,
        out_shape=arrays(blocks, 3, channels, block_len)
        + [pltpu.VMEM(array.shape, array.dtype) for array in held],
        scratch_shapes=[
            pltpu.VMEM((blocks, 3, channels, block_len), jnp.bfloat16),
            pltpu.VMEM((channels // chunk, blocks + 1, 3, chunk, 2 * block_len), jnp.bfloat16),
            pltpu.VMEM((channels // chunk, blocks + 1, 3, chunk, 2 * block_len), jnp.float32),
            *[pltpu.VMEM(array.shape, array.dtype) for array in tables],
            pltpu.SemaphoreType.DMA((10,)),
        ],
        compiler_params=compiler_params(28),
        name="conv",
    )(*moved, *in_hbm(*tables, *held))
    back, held = swap(results[:blocks]), results[blocks:]
    weights = held[3:]
    lhs, to_mate = pl.pallas_call(
        mate_kernel,
        in_specs=[VMEM] * (blocks + 6),
        out_shape=arrays(1, 3, block_len, width) + arrays(1, block_len, part),
        scratch_shapes=[pltpu.VMEM((blocks, 2, channels, block_len), jnp.bfloat16)],
        compiler_params=compiler_params(16),
        cost_estimate=block_cost,
        name="mate",
    )(*back, *held)
    from_mate = exchange(to_mate, "tp", 1)
    far, near = pl.pallas_call(
        far_kernel,
        in_specs=[VMEM] * 4,
        out_shape=arrays(1, block_len, part, dtype=jnp.float32) + arrays(1, block_len, part),
        compiler_params=compiler_params(16),
        cost_estimate=block_cost,
        name="far",
    )(lhs, *weights)
    far = (far + from_mate.astype(jnp.float32)).astype(jnp.bfloat16)
    far, near, lhs, back = lax.optimization_barrier((far, near, lhs, back))
    from_far = exchange(far, "tp", 2)
    from_near = exchange(near, "tp", 1)
    grad_filter = pl.pallas_call(
        turn_kernel,
        in_specs=[VMEM] * blocks,
        out_shape=jax.ShapeDtypeStruct((block_len, width), jnp.bfloat16),
        scratch_shapes=[pltpu.VMEM((blocks, 1, channels, block_len), jnp.bfloat16)],
        compiler_params=compiler_params(16),
        cost_estimate=block_cost,
        name="turn",
    )(*back)
    own = pl.pallas_call(
        own_kernel,
        in_specs=[VMEM] * 4,
        out_shape=arrays(1, block_len, part, dtype=jnp.float32)[0],
        compiler_params=compiler_params(16),
        cost_estimate=block_cost,
        name="own",
    )(lhs, *weights)
    total = from_far.astype(jnp.float32) + from_near.astype(jnp.float32) + own
    grad_input = total.astype(jnp.bfloat16)
    return (grad_input, grad_filter)


def solution(mesh):
    placed = (P("ctx", "tp"),) * 5 + (P(None, "tp"),) * 3
    return jax.shard_map(
        per_device,
        mesh=mesh,
        in_specs=placed,
        out_specs=(P("ctx", "tp"), P("ctx", "tp")),
        check_vma=False,
    )
```

```python
import math

import jax
import jax.numpy as jnp
import numpy as np
from jax import lax
from jax.experimental import pallas as pl
from jax.experimental.pallas import tpu as pltpu
from jax.sharding import PartitionSpec as P


def compiler_params(mib):
    return pltpu.CompilerParams(vmem_limit_bytes=int(mib * 1024 * 1024))


def dft_tables(blocks, block_len, scale, rows_count):
    index, half = np.arange(block_len), np.arange(block_len // 2)
    bins = 2 * half[None, :] + np.arange(2)[:, None]
    angle = 2.0 * np.pi * (half[None, :, None] * bins[:, None, :] % block_len) / block_len
    cos, sin = np.cos(angle), np.sin(angle)
    forward = np.block([[cos, -sin], [sin, cos]])
    inverse = forward.transpose(0, 2, 1)
    rows = np.arange(blocks + 1)
    phase = 2.0 * np.pi * np.outer(rows, index) / (2 * blocks * block_len)
    weight = np.where((rows == 0) | (rows == blocks), 1.0, 2.0)[:, None] * scale
    twiddle = np.stack([np.cos(phase), np.sin(phase)])
    untwiddle = np.repeat((weight * twiddle)[:, :, None, :], rows_count, axis=2)
    return (
        jnp.asarray(forward, jnp.bfloat16),
        jnp.asarray(inverse, jnp.bfloat16),
        jnp.asarray(twiddle, jnp.float32),
        jnp.asarray(untwiddle, jnp.bfloat16),
    )


def half_spectrum(values):
    size = len(values)
    if size == 1:
        return [(values[0], None), (values[0], None)]
    even, odd = half_spectrum(values[0::2]), half_spectrum(values[1::2])
    half = size // 2
    bins = [None] * (size + 1)
    bins[0] = (even[0][0] + odd[0][0], None)
    bins[size] = (even[0][0] - odd[0][0], None)
    bins[half] = (even[half][0], -odd[half][0])
    for k in range(1, half):
        angle = math.pi * k / size
        cos, sin = math.cos(angle), math.sin(angle)
        even_re, even_im = even[k]
        odd_re, odd_im = odd[k]
        if 2 * k == half:
            turn_re = cos * (odd_re + odd_im)
            turn_im = cos * (odd_im - odd_re)
        else:
            turn_re = cos * odd_re + sin * odd_im
            turn_im = cos * odd_im - sin * odd_re
        bins[k] = (even_re + turn_re, even_im + turn_im)
        bins[size - k] = (even_re - turn_re, turn_im - even_im)
    return bins


def half_spectrum_adjoint(bins):
    size = len(bins) - 1
    if size == 1:
        return [bins[0][0] + bins[1][0]]
    half = size // 2
    even, odd = [None] * (half + 1), [None] * (half + 1)
    even[0] = (bins[0][0] + bins[size][0], None)
    odd[0] = (bins[0][0] - bins[size][0], None)
    even[half] = (bins[half][0], None)
    odd[half] = (-bins[half][1], None)
    for k in range(1, half):
        angle = math.pi * k / size
        cos, sin = math.cos(angle), math.sin(angle)
        low_re, low_im = bins[k]
        high_re, high_im = bins[size - k]
        even[k] = (low_re + high_re, low_im - high_im)
        turn_re, turn_im = low_re - high_re, low_im + high_im
        if 2 * k == half:
            odd[k] = (cos * (turn_re - turn_im), cos * (turn_re + turn_im))
        else:
            odd[k] = (cos * turn_re - sin * turn_im, cos * turn_im + sin * turn_re)
    values = [None] * size
    values[0::2] = half_spectrum_adjoint(even)
    values[1::2] = half_spectrum_adjoint(odd)
    return values


HBM = pl.BlockSpec(memory_space=pltpu.HBM)
VMEM = pl.BlockSpec(memory_space=pltpu.VMEM)


def in_hbm(*arrays):
    return [pltpu.with_memory_space_constraint(array, pltpu.HBM) for array in arrays]


def by_distance(pieces):
    last = len(pieces) - 1
    order = [last - i // 2 if i % 2 == 0 else 1 + i // 2 for i in range(last)]
    return zip([*order, 0], pieces)


def fetch(sources, targets, sems):
    copies = [
        pltpu.make_async_copy(source, target, sems.at[i])
        for i, (source, target) in enumerate(zip(sources, targets))
    ]
    for copy in copies:
        copy.start()
    return copies


def gate_kernel(*refs):
    sources, refs = refs[:5], refs[5:]
    out_refs, (turn_ref, held_ref, sems) = refs[:-3], refs[-3:]
    blocks, _, channels, block_len = turn_ref.shape
    filter_copy, *copies = fetch(sources, [held_ref.at[i] for i in range(5)], sems)

    def put(slot, wide):
        turned = wide.T.astype(jnp.bfloat16)
        turn_ref[:, slot] = turned.reshape(blocks, channels, block_len)

    filter_copy.wait()
    put(1, held_ref[0].astype(jnp.float32))
    for copy in copies[:2]:
        copy.wait()
    put(0, held_ref[1].astype(jnp.float32) * held_ref[2].astype(jnp.float32))
    for copy in copies[2:]:
        copy.wait()
    put(2, held_ref[3].astype(jnp.float32) * held_ref[4].astype(jnp.float32))
    me = lax.axis_index("ctx")
    for distance, out_ref in by_distance(out_refs):
        out_ref[...] = turn_ref[me ^ distance]


def conv_kernel(*refs):
    blocks = lax.axis_size("ctx")
    in_refs, sources, refs = refs[:blocks], refs[blocks : blocks + 10], refs[blocks + 10 :]
    out_refs, held_refs = refs[:blocks], refs[blocks : blocks + 6]
    in_ref, rows_ref, spec_ref, twid_ref, back_ref, fwd_ref, inv_ref, sems = refs[blocks + 6 :]
    twid_copy, back_copy, fwd_copy, inv_copy, *held_copies = fetch(
        sources, (twid_ref, back_ref, fwd_ref, inv_ref, *held_refs), sems
    )
    groups, bins_count, signals, chunk, _ = rows_ref.shape
    block_len = in_ref.shape[-1]
    me = lax.axis_index("ctx")
    for distance, ref in by_distance(in_refs):
        in_ref[me ^ distance] = ref[...]
    twid_copy.wait()

    def each(count, body):
        if blocks <= 8:
            for i in range(count):
                body(i)
        else:
            pl.loop(0, count)(body)

    half = block_len // 2

    def put(group, k, slot, part, re, im):
        rows_ref[group, k, slot, :, part * block_len : part * block_len + half] = re.astype(
            jnp.bfloat16
        )
        rows_ref[group, k, slot, :, part * block_len + half : (part + 1) * block_len] = im.astype(
            jnp.bfloat16
        )

    def get(group, k, slot, part):
        re = spec_ref[group, k, slot, :, part * block_len : part * block_len + half]
        im = spec_ref[group, k, slot, :, part * block_len + half : (part + 1) * block_len]
        return re, im

    def put_halves(group, k, slot, re, im):
        put(group, k, slot, 0, re[:, :half] + re[:, half:], im[:, :half] + im[:, half:])
        put(group, k, slot, 1, re[:, :half] - re[:, half:], im[:, :half] - im[:, half:])

    def get_halves(group, k, slot):
        even_re, even_im = get(group, k, slot, 0)
        odd_re, odd_im = get(group, k, slot, 1)
        re = jnp.concatenate([even_re + odd_re, even_re - odd_re], axis=1)
        im = jnp.concatenate([even_im + odd_im, even_im - odd_im], axis=1)
        return re.astype(jnp.bfloat16), im.astype(jnp.bfloat16)

    def analyse(group):
        rows = pl.ds(group * chunk, chunk)

        def one(signal):
            bins = half_spectrum(
                [in_ref[p, signal, rows, :].astype(jnp.float32) for p in range(blocks)]
            )
            for k, (re, im) in enumerate(bins):
                cos, sin = twid_ref[0, k : k + 1, :], twid_ref[1, k : k + 1, :]
                if k == 0:
                    put_halves(group, k, signal, re, jnp.zeros_like(re))
                elif im is None:
                    put_halves(group, k, signal, re * cos, -(re * sin))
                else:
                    put_halves(group, k, signal, re * cos + im * sin, im * cos - re * sin)

        each(signals, one)

    def transform(group, table_ref):
        for part in range(2):
            lanes = slice(part * block_len, (part + 1) * block_len)
            spec_ref[group, :, :, :, lanes] = jnp.dot(
                rows_ref[group, :, :, :, lanes].reshape(bins_count * signals * chunk, block_len),
                table_ref[part],
                preferred_element_type=jnp.float32,
            ).reshape(bins_count, signals, chunk, block_len)

    def forward(group):
        if group == 0:
            fwd_copy.wait()
        transform(group, fwd_ref)

    def combine(group):
        def product(k, part):
            (prod_re, prod_im), (kern_re, kern_im), (grad_re, grad_im) = [
                [value.astype(jnp.bfloat16) for value in get(group, k, slot, part)]
                for slot in range(3)
            ]
            conv_re = prod_re * kern_re - prod_im * kern_im
            conv_im = prod_re * kern_im + prod_im * kern_re
            back_re = grad_re * kern_re + grad_im * kern_im
            back_im = grad_im * kern_re - grad_re * kern_im
            filt_re = grad_re * prod_re + grad_im * prod_im
            filt_im = grad_im * prod_re - grad_re * prod_im
            put(group, k, 0, part, conv_re, conv_im)
            put(group, k, 1, part, back_re, back_im)
            put(group, k, 2, part, filt_re, filt_im)

        def one(k):
            product(k, 0)
            product(k, 1)

        each(bins_count, one)

    def inverse(group):
        if group == 0:
            inv_copy.wait()
            back_copy.wait()
        transform(group, inv_ref)

    def synthesise(group):
        rows = pl.ds(group * chunk, chunk)

        def one(signal):
            bins = []
            for k in range(bins_count):
                re, im = get_halves(group, k, signal)
                cos, sin = back_ref[0, k], back_ref[1, k]
                if k == 0:
                    bins.append((re * cos, None))
                elif k == blocks:
                    bins.append((re * cos - im * sin, None))
                else:
                    bins.append((re * cos - im * sin, im * cos + re * sin))
            for p, value in enumerate(half_spectrum_adjoint(bins)):
                in_ref[p, signal, rows, :] = value

        each(signals, one)

    stages = (analyse, forward, combine, inverse, synthesise)
    for step in range(groups + len(stages) - 1):
        for depth in (3, 1, 4, 2, 0):
            if 0 <= step - depth < groups:
                stages[depth](step - depth)
    for distance, out_ref in by_distance(out_refs):
        out_ref[...] = in_ref[me ^ distance]
    for copy in held_copies:
        copy.wait()


def term(lhs_ref, weight_refs, group):
    part = weight_refs[0].shape[0] // lax.axis_size("tp")
    rows = pl.ds(pl.multiple_of(group * part, part), part)
    dims = (((1,), (1,)), ((), ()))
    total = None
    for slot, weight_ref in enumerate(weight_refs):
        piece = lax.dot_general(
            lhs_ref[slot], weight_ref[rows, :], dims, preferred_element_type=jnp.float32
        )
        total = piece if total is None else total + piece
    return total


def natural(back_refs, turn_ref, slots):
    blocks, _, channels, block_len = turn_ref.shape
    me = lax.axis_index("ctx")
    for distance, ref in by_distance(back_refs):
        for i, slot in enumerate(slots):
            turn_ref[me ^ distance, i] = ref[slot]
    return [
        turn_ref[:, i].reshape(blocks * channels, block_len).astype(jnp.float32).T
        for i in range(len(slots))
    ]


def mate_kernel(*refs):
    blocks = lax.axis_size("ctx")
    back_refs, (key_ref, value_ref, grad_ref) = refs[:blocks], refs[blocks : blocks + 3]
    weight_refs = refs[blocks + 3 : blocks + 6]
    lhs_ref, out_ref, turn_ref = refs[blocks + 6 :]
    conv_out, grad_product = natural(back_refs, turn_ref, (0, 1))
    lhs_ref[0] = (grad_product * value_ref[...].astype(jnp.float32)).astype(jnp.bfloat16)
    lhs_ref[1] = (conv_out * grad_ref[...].astype(jnp.float32)).astype(jnp.bfloat16)
    lhs_ref[2] = (grad_product * key_ref[...].astype(jnp.float32)).astype(jnp.bfloat16)
    out_ref[...] = term(lhs_ref, weight_refs, lax.axis_index("tp") ^ 3).astype(jnp.bfloat16)


def far_kernel(lhs_ref, wk_ref, wq_ref, wv_ref, far_ref, near_ref):
    group = lax.axis_index("tp")
    far_ref[...] = term(lhs_ref, (wk_ref, wq_ref, wv_ref), group ^ 2)
    near_ref[...] = term(lhs_ref, (wk_ref, wq_ref, wv_ref), group ^ 1).astype(jnp.bfloat16)


def own_kernel(lhs_ref, wk_ref, wq_ref, wv_ref, own_ref):
    own_ref[...] = term(lhs_ref, (wk_ref, wq_ref, wv_ref), lax.axis_index("tp"))


def turn_kernel(*refs):
    back_refs, (out_ref, turn_ref) = refs[:-2], refs[-2:]
    out_ref[...] = natural(back_refs, turn_ref, (2,))[0].astype(jnp.bfloat16)


def exchange(block, axis, distance):
    pairs = [(i, i ^ distance) for i in range(lax.axis_size(axis))]
    return lax.ppermute(block, axis, pairs)


def swap(pieces):
    return [
        exchange(piece, "ctx", distance) if distance else piece
        for distance, piece in by_distance(pieces)
    ]


def per_device(key_act, value_act, query_act, grad_out, long_filter, w_key, w_query, w_value):
    blocks = lax.axis_size("ctx")
    groups = lax.axis_size("tp")
    block_len, width = key_act.shape
    channels = width // blocks
    chunk = min(channels, 16)
    seq_len = blocks * block_len
    part = w_key.shape[0] // groups
    block_cost = pl.CostEstimate(
        flops=4 * block_len * 3 * width * part, bytes_accessed=1 << 22, transcendentals=0
    )

    def arrays(count, *shape, dtype=jnp.bfloat16):
        return [pltpu.VMEM(shape, dtype)] * count

    sent = pl.pallas_call(
        gate_kernel,
        in_specs=[HBM] * 5,
        out_shape=arrays(blocks, 3, channels, block_len),
        scratch_shapes=[
            pltpu.VMEM((blocks, 3, channels, block_len), jnp.bfloat16),
            pltpu.VMEM((5, block_len, width), jnp.bfloat16),
            pltpu.SemaphoreType.DMA((5,)),
        ],
        compiler_params=compiler_params(12),
        name="gate",
    )(*in_hbm(long_filter, key_act, value_act, query_act, grad_out))
    moved = swap(sent)

    forward, inverse, twiddle, untwiddle = dft_tables(
        blocks, block_len, 1.0 / (math.sqrt(seq_len) * 2 * seq_len), chunk
    )
    tables = (twiddle, untwiddle, forward, inverse)
    held = (key_act, value_act, grad_out, w_key, w_query, w_value)
    results = pl.pallas_call(
        conv_kernel,
        in_specs=[VMEM] * blocks + [HBM] * 10,
        out_shape=arrays(blocks, 3, channels, block_len)
        + [pltpu.VMEM(array.shape, array.dtype) for array in held],
        scratch_shapes=[
            pltpu.VMEM((blocks, 3, channels, block_len), jnp.bfloat16),
            pltpu.VMEM((channels // chunk, blocks + 1, 3, chunk, 2 * block_len), jnp.bfloat16),
            pltpu.VMEM((channels // chunk, blocks + 1, 3, chunk, 2 * block_len), jnp.float32),
            *[pltpu.VMEM(array.shape, array.dtype) for array in tables],
            pltpu.SemaphoreType.DMA((10,)),
        ],
        compiler_params=compiler_params(28),
        name="conv",
    )(*moved, *in_hbm(*tables, *held))
    back, held = swap(results[:blocks]), results[blocks:]
    weights = held[3:]
    lhs, to_mate = pl.pallas_call(
        mate_kernel,
        in_specs=[VMEM] * (blocks + 6),
        out_shape=arrays(1, 3, block_len, width) + arrays(1, block_len, part),
        scratch_shapes=[pltpu.VMEM((blocks, 2, channels, block_len), jnp.bfloat16)],
        compiler_params=compiler_params(16),
        cost_estimate=block_cost,
        name="mate",
    )(*back, *held)
    from_mate = exchange(to_mate, "tp", 1)
    far, near = pl.pallas_call(
        far_kernel,
        in_specs=[VMEM] * 4,
        out_shape=arrays(1, block_len, part, dtype=jnp.float32) + arrays(1, block_len, part),
        compiler_params=compiler_params(16),
        cost_estimate=block_cost,
        name="far",
    )(lhs, *weights)
    far = (far + from_mate.astype(jnp.float32)).astype(jnp.bfloat16)
    far, near, lhs, back = lax.optimization_barrier((far, near, lhs, back))
    from_far = exchange(far, "tp", 2)
    from_near = exchange(near, "tp", 1)
    grad_filter = pl.pallas_call(
        turn_kernel,
        in_specs=[VMEM] * blocks,
        out_shape=jax.ShapeDtypeStruct((block_len, width), jnp.bfloat16),
        scratch_shapes=[pltpu.VMEM((blocks, 1, channels, block_len), jnp.bfloat16)],
        compiler_params=compiler_params(16),
        cost_estimate=block_cost,
        name="turn",
    )(*back)
    own = pl.pallas_call(
        own_kernel,
        in_specs=[VMEM] * 4,
        out_shape=arrays(1, block_len, part, dtype=jnp.float32)[0],
        compiler_params=compiler_params(16),
        cost_estimate=block_cost,
        name="own",
    )(lhs, *weights)
    total = from_far.astype(jnp.float32) + from_near.astype(jnp.float32) + own
    grad_input = total.astype(jnp.bfloat16)
    return (grad_input, grad_filter)


def solution(mesh):
    placed = (P("ctx", "tp"),) * 5 + (P(None, "tp"),) * 3
    return jax.shard_map(
        per_device,
        mesh=mesh,
        in_specs=placed,
        out_specs=(P("ctx", "tp"), P("ctx", "tp")),
        check_vma=False,
    )
```
